128 devices in a mesh: seq: 64 (over z, x_hi, y, core), head: 2 (over x_lo).
Axes of the slice: x: 4 (x_hi: 2, x_lo: 2; x = x_hi * 2 + x_lo), y: 4, z: 4, core: 2. Of those that a mesh axis runs over, the one named last changes fastest.
Arguments:
- tokens: bfloat16 [24576, 1536], P(('seq', 'head')), may hold values from -6 to 6
- cotangent: bfloat16 [24576, 1536], P(('seq', 'head')), may hold values from -24 to 24
- w_query: bfloat16 [1536, 1536], P(('seq', 'head')), may hold values from -0.3125 to 0.3125
- w_key: bfloat16 [1536, 128], P(('seq', 'head')), may hold values from -0.15625 to 0.15625
- w_value: bfloat16 [1536, 128], P(('seq', 'head')), may hold values from -0.15625 to 0.15625
- w_out: bfloat16 [1536, 1536], P('head', 'seq'), may hold values from -0.625 to 0.625
- w_gate: bfloat16 [1536, 4608], P('seq', 'head'), may hold values from -0.15625 to 0.15625
- w_up: bfloat16 [1536, 4608], P('seq', 'head'), may hold values from -0.15625 to 0.15625
- w_down: bfloat16 [4608, 1536], P('head', 'seq'), may hold values from -0.09375 to 0.09375
- gain_attn: bfloat16 [1536], P(('seq', 'head')), may hold values from 0.5 to 1.5
- gain_mlp: bfloat16 [1536], P(('seq', 'head')), may hold values from 0.5 to 1.5
Outputs:
- block_out: bfloat16 [24576, 1536], P(('seq', 'head'))
- input_grad: bfloat16 [24576, 1536], P(('seq', 'head'))
- grad_w_query: float32 [1536, 1536], P(('seq', 'head'))
- grad_w_key: float32 [1536, 128], P(('seq', 'head'))
- grad_w_value: float32 [1536, 128], P(('seq', 'head'))
- grad_w_out: float32 [1536, 1536], P('head', 'seq')
- grad_w_gate: float32 [1536, 4608], P('seq', 'head')
- grad_w_up: float32 [1536, 4608], P('seq', 'head')
- grad_w_down: float32 [4608, 1536], P('head', 'seq')
- grad_gain_attn: float32 [1536], P(('seq', 'head'))
- grad_gain_mlp: float32 [1536], P(('seq', 'head'))
The draws below stay inside these ranges and needn't reach their ends.
All inputs are finite; a program needn't handle non-finite values.
Results may differ from the reference program's by a relative error of at most 0.02.
Values may be sent and summed in bfloat16 or wider, within the bound.
No kernel may reach another device: no remote copies, remote signals or barrier semaphores. Data moves between devices by JAX's collectives and lax.ppermute only.
A program may use at most 256 MiB of HBM per device.

```python
import math
import jax
import jax.numpy as jnp
from jax import lax

D = 1536
NH = 12
HD = 128
FF = 4608
WINDOW = 1024
TOKENS = 24576


def raised(drawn, stream_key, source, target, blocks, factor):
    owner, partner = [(jnp.arange(drawn.shape[position]) // (drawn.shape[position] // blocks)).reshape([-1 if axis == position else 1 for axis in range(drawn.ndim)]) for position in (source, target)]
    chosen = jax.random.permutation(stream_key, blocks)[partner]
    strong = (owner == chosen) | (owner == (partner + blocks // 2) % blocks)
    return jnp.where(strong, factor * drawn, drawn)


def steps_of(stream_key, extent, pieces, smallest, largest):
    def one(axis_at, shards_of):
        steps = jax.random.uniform(jax.random.fold_in(jax.random.fold_in(stream_key, 6), axis_at), (shards_of,), jnp.float32, smallest / len(pieces), largest / len(pieces))
        return jnp.repeat(jnp.exp(steps), extent[axis_at] // shards_of).reshape((-1,) + (1,) * (len(extent) - axis_at - 1))

    level = one(*pieces[0])
    for cut in pieces[1:]:
        level = level * one(*cut)
    return level


def noise(key, dims, spread, reach, pieces=(), kind=jnp.bfloat16):
    array = spread * jax.random.normal(key, dims, jnp.float32)
    if pieces:
        array = array * steps_of(key, dims, pieces, -0.22, 0.18)
    return jnp.clip(array, -reach, reach).astype(kind)


def heavy_noise(key, dims, scale, reach, pieces, heavy, kind=jnp.bfloat16):
    array = scale * jax.random.normal(key, dims, jnp.float32)
    if pieces:
        array = array * steps_of(key, dims, pieces, -0.22, 0.18)
    return jnp.clip(raised(array, jax.random.fold_in(key, 3), *heavy), -reach, reach).astype(kind)


def setup_inputs(seed: int = 0) -> dict:
    seeds = jax.random.split(jax.random.key(seed), 12)
    tokens = noise(seeds[0], (TOKENS, D), 1.0, 6.0, ((0, 128),))
    cotangent = heavy_noise(seeds[1], (TOKENS, D), 1.0, 24.0, ((0, 128),), (0, 1, 128, 5.5))
    w_query = noise(seeds[2], (D, NH * HD), (D // 4) ** -0.5, 0.3125, ((0, 128),))
    w_key = noise(seeds[3], (D, HD), D ** -0.5, 0.15625, ((0, 128),))
    w_value = noise(seeds[4], (D, HD), D ** -0.5, 0.15625, ((0, 128),))
    w_out = noise(seeds[5], (NH * HD, D), (NH * HD // 16) ** -0.5, 0.625, ((0, 2), (1, 64)))
    w_gate = noise(seeds[6], (D, FF), D ** -0.5, 0.15625, ((0, 64), (1, 2)))
    w_up = noise(seeds[7], (D, FF), D ** -0.5, 0.15625, ((0, 64), (1, 2)))
    w_down = noise(seeds[8], (FF, D), FF ** -0.5, 0.09375, ((0, 2), (1, 64)))
    gain_attn = jnp.clip(1.0 + 0.1 * jax.random.normal(seeds[9], (D,), jnp.float32), 0.5, 1.5).astype(jnp.bfloat16)
    gain_mlp = jnp.clip(1.0 + 0.1 * jax.random.normal(seeds[10], (D,), jnp.float32), 0.5, 1.5).astype(jnp.bfloat16)
    return {"tokens": tokens, "cotangent": cotangent, "w_query": w_query, "w_key": w_key, "w_value": w_value, "w_out": w_out, "w_gate": w_gate, "w_up": w_up, "w_down": w_down, "gain_attn": gain_attn, "gain_mlp": gain_mlp}


@jax.custom_vjp
def low(v):
    return lax.optimization_barrier(v.astype(jnp.bfloat16)).astype(jnp.float32)

@jax.custom_vjp
def low_back(v):
    return v

def low_keep(v):
    return (low(v), None)

def low_pass(kept, grad):
    return (grad,)

def back_keep(v):
    return (v, None)

def back_low(kept, grad):
    return (low(grad),)
low.defvjp(low_keep, low_pass)
low_back.defvjp(back_keep, back_low)
EPSILON = 1e-06

def matmul(first_op, second_op):
    return jnp.dot(first_op, second_op, precision=lax.Precision.HIGHEST)

def rms_scale(values_in, gain_vec):
    inverse = lax.rsqrt(lax.optimization_barrier(jnp.mean(values_in * values_in, axis=-1, keepdims=True)) + EPSILON)
    return values_in * inverse * gain_vec

def attend(queries, keys, values):
    block_rows = math.gcd(TOKENS, 512)
    blocks = TOKENS // block_rows
    score_scale = HD ** (-0.5)
    key_pad = jnp.pad(keys, ((WINDOW, 0), (0, 0)))
    value_pad = jnp.pad(values, ((WINDOW, 0), (0, 0)))
    query_blocks = queries.reshape(blocks, block_rows, NH, HD)

    def one_block(block_pair):
        block_index, query_block = block_pair
        block_start = block_index * block_rows
        key_block = lax.dynamic_slice_in_dim(key_pad, block_start, block_rows + WINDOW, 0)
        value_block = lax.dynamic_slice_in_dim(value_pad, block_start, block_rows + WINDOW, 0)
        scores = low_back(jnp.einsum('qhd,kd->hqk', query_block, key_block, precision=lax.Precision.HIGHEST) * score_scale)
        query_pos = block_start + jnp.arange(block_rows, dtype=jnp.int32)
        key_pos = block_start - WINDOW + jnp.arange(block_rows + WINDOW, dtype=jnp.int32)
        offset = query_pos[:, None] - key_pos[None, :]
        in_window = (offset >= 0) & (offset < WINDOW) & (key_pos[None, :] >= 0)
        masked = jnp.where(in_window[None], scores, -1e+30)
        weights = low(jax.nn.softmax(masked, axis=-1))
        mixed = jnp.einsum('hqk,kd->qhd', weights, value_block, precision=lax.Precision.HIGHEST)
        return mixed.reshape(block_rows, NH * HD)
    block_outputs = lax.map(jax.checkpoint(one_block), (jnp.arange(blocks, dtype=jnp.int32), query_blocks))
    return block_outputs.reshape(TOKENS, NH * HD)

def forward(tokens, w_query, w_key, w_value, w_out, w_gate, w_up, w_down, gain_attn, gain_mlp):
    normed_in = low(rms_scale(tokens, gain_attn))
    queries = low_back(low(matmul(normed_in, w_query))).reshape(TOKENS, NH, HD)
    keys = low_back(low(matmul(normed_in, w_key)))
    values = low_back(low(matmul(normed_in, w_value)))
    attended = low_back(low(attend(queries, keys, values)))
    branch = low_back(matmul(attended, w_out))
    middle = tokens + branch
    second_in = low(rms_scale(middle, gain_mlp))
    mlp_rows = math.gcd(TOKENS, 2048)

    def mlp_block(rows_in):
        gate = low_back(matmul(rows_in, w_gate))
        upward = low_back(matmul(rows_in, w_up))
        hidden = low(jax.nn.gelu(gate, approximate=True) * upward)
        return matmul(hidden, w_down)
    mlp_out = lax.map(jax.checkpoint(mlp_block), second_in.reshape(TOKENS // mlp_rows, mlp_rows, D))
    return middle + mlp_out.reshape(TOKENS, D)

def reference(tokens, cotangent, w_query, w_key, w_value, w_out, w_gate, w_up, w_down, gain_attn, gain_mlp):
    float_args = tuple((item.astype(jnp.float32) for item in (tokens, w_query, w_key, w_value, w_out, w_gate, w_up, w_down, gain_attn, gain_mlp)))
    output_value, pull_back = jax.vjp(forward, *float_args)
    gradients = pull_back(cotangent.astype(jnp.float32))
    return (output_value.astype(jnp.bfloat16), gradients[0].astype(jnp.bfloat16), gradients[1], gradients[2], gradients[3], gradients[4], gradients[5], gradients[6], gradients[7], gradients[8], gradients[9])
```

```python
import functools
import jax
import jax.numpy as jnp
from jax import lax
from jax.experimental import pallas as pl
from jax.experimental.pallas import tpu as pltpu
from jax.sharding import Mesh
from jax.sharding import PartitionSpec as P

WINDOW = 1024
EPSILON = 1e-06
AXES = ("z", "xh", "y", "core", "head")
SIZES = (4, 2, 4, 2, 2)
CHIPS_X = ("xh", "head")
PLANE = ("z", "y")
ROW = 192
KEYS = 1216
HEADS = 12
HD = 128
BF = jnp.bfloat16
F32 = jnp.float32
NEG = -1e30
SCALE = HD ** (-0.5)
LOG2E = 1.4426950408889634
VMEM_BYTES = 56 * 1024 * 1024

NN = (((1,), (0,)), ((), ()))
NT = (((1,), (1,)), ((), ()))
TN = (((0,), (0,)), ((), ()))


def dot(a, b, dims=NN):
    return lax.dot_general(a, b, dims, preferred_element_type=F32)


def two_heads(pair):
    return jnp.concatenate([pair[:, :HD], pair[:, HD:]], axis=0)


def attend_kernel(block_ref, q_ref, kv_ref, out_ref, probs_ref, bias):
    @pl.when(pl.program_id(0) == 0)
    def _():
        key = lax.broadcasted_iota(jnp.int32, (KEYS, ROW), 0)
        query = lax.broadcasted_iota(jnp.int32, (KEYS, ROW), 1)
        first = WINDOW - ROW * block_ref[0]
        inside = (key > query) & (key <= query + WINDOW) & (key >= first)
        one = jnp.where(inside, 0.0, NEG)
        bias[:, :] = jnp.concatenate([one, one], axis=1)

    queries = two_heads(q_ref[...])
    scores = dot(kv_ref[:, :HD], queries, NT) + bias[...]
    highest = jnp.max(scores, axis=0, keepdims=True)
    powers = jnp.exp2((scores - highest) * (SCALE * LOG2E))
    total = jnp.sum(powers, axis=0, keepdims=True)
    probs = (powers * (1.0 / total)).astype(BF)
    probs_ref[0] = probs
    mixed = dot(kv_ref[:, HD:], probs, TN).T.astype(BF)
    out_ref[...] = jnp.concatenate([mixed[:ROW], mixed[ROW:]], axis=1)


def attend(block, queries, keyval):
    return pl.pallas_call(
        attend_kernel,
        grid_spec=pltpu.PrefetchScalarGridSpec(
            num_scalar_prefetch=1,
            grid=(HEADS // 2,),
            in_specs=[
                pl.BlockSpec((ROW, 2 * HD), lambda h, b: (0, h)),
                pl.BlockSpec((KEYS, 2 * HD), lambda h, b: (0, 0)),
            ],
            out_specs=[
                pl.BlockSpec((ROW, 2 * HD), lambda h, b: (0, h)),
                pl.BlockSpec((1, KEYS, 2 * ROW), lambda h, b: (h, 0, 0)),
            ],
            scratch_shapes=[pltpu.VMEM((KEYS, 2 * ROW), F32)],
        ),
        out_shape=[
            jax.ShapeDtypeStruct((ROW, HEADS * HD), BF),
            jax.ShapeDtypeStruct((HEADS // 2, KEYS, 2 * ROW), BF),
        ],
        compiler_params=pltpu.CompilerParams(vmem_limit_bytes=VMEM_BYTES),
        cost_estimate=pl.CostEstimate(
            flops=4 * HEADS * ROW * KEYS * HD,
            bytes_accessed=8 * 1024 * 1024,
            transcendentals=HEADS * ROW * KEYS,
        ),
        name="attend",
    )(block, queries, keyval)


def attend_back_kernel(q_ref, kv_ref, out_ref, grad_ref, probs_ref, dq_ref, dkv_ref, dk, dv):
    step = pl.program_id(0)

    @pl.when(step == 0)
    def _():
        dk[...] = jnp.zeros_like(dk)
        dv[...] = jnp.zeros_like(dv)

    queries = two_heads(q_ref[...])
    grads = two_heads(grad_ref[...])
    outs = two_heads(out_ref[...])
    probs = probs_ref[0]
    delta = jnp.sum((grads.astype(F32) * outs.astype(F32)).T, axis=0, keepdims=True)
    dprobs = dot(kv_ref[:, HD:], grads, NT)
    dscores = (probs.astype(F32) * (dprobs - delta)).astype(BF)
    dqueries = (dot(kv_ref[:, :HD], dscores, TN).T * SCALE).astype(BF)
    dq_ref[...] = jnp.concatenate([dqueries[:ROW], dqueries[ROW:]], axis=1)
    dk[...] += dot(dscores, queries)
    dv[...] += dot(probs, grads)

    @pl.when(step == HEADS // 2 - 1)
    def _():
        dkv_ref[:, :HD] = (dk[...] * SCALE).astype(BF)
        dkv_ref[:, HD:] = dv[...].astype(BF)


def attend_back(queries, keyval, attended, grads, probs):
    pair = pl.BlockSpec((ROW, 2 * HD), lambda h: (0, h))
    table = pl.BlockSpec((KEYS, 2 * HD), lambda h: (0, 0))
    return pl.pallas_call(
        attend_back_kernel,
        grid=(HEADS // 2,),
        in_specs=[pair, table, pair, pair, pl.BlockSpec((1, KEYS, 2 * ROW), lambda h: (h, 0, 0))],
        out_specs=[pair, table],
        scratch_shapes=[pltpu.VMEM((KEYS, HD), F32), pltpu.VMEM((KEYS, HD), F32)],
        out_shape=[
            jax.ShapeDtypeStruct((ROW, HEADS * HD), BF),
            jax.ShapeDtypeStruct((KEYS, 2 * HD), BF),
        ],
        compiler_params=pltpu.CompilerParams(vmem_limit_bytes=VMEM_BYTES),
        cost_estimate=pl.CostEstimate(
            flops=8 * HEADS * ROW * KEYS * HD,
            bytes_accessed=9 * 1024 * 1024,
            transcendentals=0,
        ),
        name="attend_back",
    )(queries, keyval, attended, grads, probs)


def shift_all(block, distance):
    count = 128
    route = [(i, i + distance) for i in range(count) if 0 <= i + distance < count]
    return lax.ppermute(block, AXES, route)


def shift_x(block, distance):
    return lax.ppermute(block, CHIPS_X, [(i, (i + distance) % 4) for i in range(4)])


def swap_core(block):
    return lax.ppermute(block, "core", [(0, 1), (1, 0)])


def mixed_order(rows):
    count = rows.shape[0]
    return rows.reshape(count, 4, 2, 192).transpose(0, 2, 1, 3).reshape(count, 1536)


def true_order(rows):
    count = rows.shape[0]
    return rows.reshape(count, 2, 4, 192).transpose(0, 2, 1, 3).reshape(count, 1536)


def shards(tokens, cotangent, w_query, w_key, w_value, w_out, w_gate, w_up, w_down, gain_attn, gain_mlp):
    core = lax.axis_index("core")
    xh = lax.axis_index("xh")
    block = lax.axis_index(AXES)

    def halves(full, axis):
        size = full.shape[axis] // 2
        return (
            lax.dynamic_slice_in_dim(full, core * size, size, axis),
            lax.dynamic_slice_in_dim(full, (1 - core) * size, size, axis),
        )

    def joined(mine, other, axis):
        return jnp.concatenate(
            [jnp.where(core == 0, mine, other), jnp.where(core == 0, other, mine)], axis=axis
        )

    def spread(piece):
        mine = lax.all_gather(piece, PLANE, axis=0, tiled=True)
        return mine, swap_core(mine)

    gains = jnp.pad(jnp.stack([gain_attn, gain_mlp], axis=1), ((0, 0), (0, 126)))
    own_qkv = jnp.concatenate([w_query, w_key, w_value, gains], axis=1)
    eight = ("xh", "core", "head")
    got = lax.all_to_all(jnp.broadcast_to(own_qkv[None], (8, 12, 1920)), eight, 0, 0, tiled=True)
    piece = lax.dynamic_slice_in_dim(got, core * 4, 4, 0).reshape(48, 1920)
    qkv_mine, qkv_other = spread(piece)

    got = lax.all_to_all(jnp.broadcast_to(w_out.T[None], (8, 24, 768)), eight, 0, 0, tiled=True)
    piece = lax.dynamic_slice_in_dim(got, core * 4, 4, 0).reshape(2, 2, 24, 768)
    out_mine, out_other = spread(piece.transpose(0, 2, 1, 3).reshape(48, 1536))

    own_mlp = jnp.stack([w_gate, w_up, w_down.T], axis=1).reshape(24, 3, 2, 1152)
    own_mlp = own_mlp.transpose(2, 0, 1, 3).reshape(2, 1, 24, 3456)
    own_mlp = jnp.broadcast_to(own_mlp, (2, 2, 24, 3456)).reshape(4, 24, 3456)
    got = lax.all_to_all(own_mlp, ("xh", "core"), 0, 0, tiled=True)
    piece = lax.dynamic_slice_in_dim(got, core * 2, 2, 0).reshape(48, 3456)
    mlp_mine, mlp_other = spread(piece)

    cots_own = mixed_order(cotangent)
    cots = jnp.concatenate([cots_own] + [shift_x(cots_own, k) for k in (1, 2, 3)], axis=0)

    gain_table = joined(qkv_mine[:, 1792:1794], qkv_other[:, 1792:1794], 0).astype(F32).T
    first_gain, second_gain = gain_table[0:1], gain_table[1:2]

    inputs = mixed_order(tokens).astype(F32)
    rs1 = lax.rsqrt(jnp.mean(inputs * inputs, axis=-1, keepdims=True) + EPSILON)
    n1 = inputs * rs1
    first_low = (n1 * first_gain).astype(BF)
    first_mine, first_other = halves(first_low, 1)
    projected = (dot(first_mine, qkv_mine[:, :1792]) + dot(first_other, qkv_other[:, :1792])).astype(BF)
    queries = projected[:, :1536]
    keyval_own = projected[:, 1536:]
    earlier = [shift_all(keyval_own[128:], 6)] + [shift_all(keyval_own, k) for k in (5, 4, 3, 2, 1)]
    keyval = jnp.concatenate(earlier + [keyval_own], axis=0)
    attended, probs = attend(block.astype(jnp.int32).reshape(1), queries, keyval)
    branch = joined(dot(attended, out_mine, NT), dot(attended, out_other, NT), 1)
    middle = inputs + branch
    rs2 = lax.rsqrt(jnp.mean(middle * middle, axis=-1, keepdims=True) + EPSILON)
    n2 = middle * rs2
    second_own = (n2 * second_gain).astype(BF)
    seconds = jnp.concatenate([second_own] + [shift_x(second_own, k) for k in (1, 2, 3)], axis=0)

    second_mine, second_other = halves(seconds, 1)
    cots_mine, cots_other = halves(cots, 1)
    gate_up = dot(second_mine, mlp_mine[:, :2304]) + dot(second_other, mlp_other[:, :2304])
    gate, up = gate_up[:, :1152], gate_up[:, 1152:]
    grad_hidden = dot(cots_mine, mlp_mine[:, 2304:]) + dot(cots_other, mlp_other[:, 2304:])

    def geglu(gate_val, up_val):
        return jax.nn.gelu(gate_val, approximate=True) * up_val

    hidden, geglu_back = jax.vjp(geglu, gate, up)
    hidden = hidden.astype(BF)
    grad_gate, grad_up = geglu_back(grad_hidden)
    grad_gate_up = jnp.concatenate([grad_gate, grad_up], axis=1).astype(BF)

    def to_owners(partial):
        pieces = partial.reshape(4, ROW, 1536)
        total = pieces[0].astype(F32)
        for k in (1, 2, 3):
            total = total + shift_x(pieces[k], -k).astype(F32)
        return total

    second_part = joined(dot(grad_gate_up, mlp_mine[:, :2304], NT), dot(grad_gate_up, mlp_other[:, :2304], NT), 1)
    grad_second = to_owners(second_part.astype(BF))
    mlp_part = joined(dot(hidden, mlp_mine[:, 2304:], NT), dot(hidden, mlp_other[:, 2304:], NT), 1)
    block_out = true_order((middle + to_owners(mlp_part.astype(BF))).astype(BF))

    def planes(mine, other):
        total = mine.astype(F32) + swap_core(other.astype(BF)).astype(F32)
        total = total.astype(BF).reshape(16, 48, -1)
        got = lax.all_to_all(total, PLANE, 0, 0, tiled=True)
        return jnp.sum(got.astype(F32), axis=0)

    mlp_grads = []
    for lhs, rhs in (
        ((cots_mine, cots_other), hidden),
        ((second_mine, second_other), grad_gate_up[:, :1152]),
        ((second_mine, second_other), grad_gate_up[:, 1152:]),
    ):
        mlp_grads.append(planes(dot(lhs[0], rhs, TN), dot(lhs[1], rhs, TN)))
    mlp_grads = jnp.concatenate(mlp_grads, axis=1).astype(BF).reshape(1, 2, 24, 3456)
    sent = jnp.broadcast_to(mlp_grads, (2, 2, 24, 3456)).reshape(4, 24, 3456)
    got = lax.all_to_all(sent, ("xh", "core"), 0, 0, tiled=True).reshape(2, 2, 24, 3, 1152)
    got = lax.dynamic_index_in_dim(got, xh, 1, keepdims=False).transpose(2, 1, 0, 3).reshape(3, 24, 2304)
    grad_w_down, grad_w_gate, grad_w_up = got[0].astype(F32).T, got[1].astype(F32), got[2].astype(F32)

    scaled = grad_second * second_gain
    grad_middle = cots_own.astype(F32) + rs2 * (scaled - n2 * jnp.mean(scaled * n2, axis=-1, keepdims=True))
    gain_second_grad = jnp.sum(grad_second * n2, axis=0)
    grad_branch = grad_middle.astype(BF)
    branch_mine, branch_other = halves(grad_branch, 1)
    grad_attended = (dot(branch_mine, out_mine) + dot(branch_other, out_other)).astype(BF)
    out_grads = planes(dot(branch_mine, attended, TN), dot(branch_other, attended, TN))

    def to_eight(grads):
        sent = jnp.where(jnp.arange(2).reshape(2, 1, 1, 1, 1) == core, grads[None], 0.0).astype(BF)
        sent = sent.reshape((8,) + grads.shape[2:])
        return jnp.sum(lax.all_to_all(sent, eight, 0, 0, tiled=True).astype(F32), axis=0)

    grad_w_out = to_eight(out_grads.reshape(2, 24, 2, 768).transpose(0, 2, 1, 3)).T

    dqueries, dkeyval = attend_back(queries, keyval, attended, grad_attended, probs)
    keyval_home = dkeyval[1024:].astype(F32)
    for k in (1, 2, 3, 4, 5):
        start = 1024 - ROW * k
        keyval_home = keyval_home + shift_all(dkeyval[start : start + ROW], -k).astype(F32)
    keyval_home = keyval_home + jnp.pad(shift_all(dkeyval[:64], -6).astype(F32), ((128, 0), (0, 0)))
    dqkv = jnp.concatenate([dqueries, keyval_home.astype(BF)], axis=1)
    grad_first = joined(dot(dqkv, qkv_mine[:, :1792], NT), dot(dqkv, qkv_other[:, :1792], NT), 1)
    scaled = grad_first * first_gain
    input_grad = grad_middle + rs1 * (scaled - n1 * jnp.mean(scaled * n1, axis=-1, keepdims=True))
    input_grad = true_order(input_grad.astype(BF))
    gain_first_grad = jnp.sum(grad_first * n1, axis=0)
    gain_grads = jnp.pad(jnp.stack([gain_first_grad, gain_second_grad], axis=1), ((0, 0), (0, 126)))
    gains_mine, gains_other = halves(gain_grads, 0)
    qkv_grads = planes(
        jnp.concatenate([dot(first_mine, dqkv, TN), gains_mine], axis=1),
        jnp.concatenate([dot(first_other, dqkv, TN), gains_other], axis=1),
    )
    qkv_own = to_eight(qkv_grads.reshape(2, 2, 12, 1920))
    return (
        block_out,
        input_grad,
        qkv_own[:, :1536],
        qkv_own[:, 1536:1664],
        qkv_own[:, 1664:1792],
        grad_w_out,
        grad_w_gate,
        grad_w_up,
        grad_w_down,
        qkv_own[:, 1792],
        qkv_own[:, 1793],
    )


def solution(mesh):
    grid = Mesh(mesh.devices.reshape(SIZES), AXES)
    seq = ("z", "xh", "y", "core")
    rows, both, cols = P(AXES, None), P(seq, "head"), P("head", seq)
    in_specs = (rows, rows, rows, rows, rows, cols, both, both, cols, P(AXES), P(AXES))
    out_specs = (rows, rows, rows, rows, rows, cols, both, both, cols, P(AXES), P(AXES))
    return jax.shard_map(shards, mesh=grid, in_specs=in_specs, out_specs=out_specs, check_vma=False)
```

```python
import functools
import jax
import jax.numpy as jnp
from jax import lax
from jax.experimental import pallas as pl
from jax.experimental.pallas import tpu as pltpu
from jax.sharding import Mesh
from jax.sharding import PartitionSpec as P

WINDOW = 1024
EPSILON = 1e-06
AXES = ("z", "xh", "y", "core", "head")
SIZES = (4, 2, 4, 2, 2)
CHIPS_X = ("xh", "head")
PLANE = ("z", "y")
ROW = 192
KEYS = 1216
HEADS = 12
HD = 128
BF = jnp.bfloat16
F32 = jnp.float32
NEG = -1e30
SCALE = HD ** (-0.5)
LOG2E = 1.4426950408889634
VMEM_BYTES = 56 * 1024 * 1024
FF = 1152
FF_TILES = 3
FF_TILE = 384
RING = 768
GELU_A = 0.7978845608028654
GELU_B = GELU_A * 0.044715

NN = (((1,), (0,)), ((), ()))
NT = (((1,), (1,)), ((), ()))
TN = (((0,), (0,)), ((), ()))


def dot(a, b, dims=NN):
    return lax.dot_general(a, b, dims, preferred_element_type=F32)


ANY = pl.BlockSpec(memory_space=pl.ANY)


def cost(micros):
    return pl.CostEstimate(flops=int(micros * 1.0e9), bytes_accessed=1000000, transcendentals=0)


def call(kernel, name, outs, args, needs=(), micros=0.01, grid=None, in_specs=None, out_specs=None, scratch=(), scalars=0):
    count = len(args)

    def body(*refs):
        kernel(*refs[:count], *refs[count + len(needs) :])

    if in_specs is None:
        whole = pl.BlockSpec(memory_space=pltpu.VMEM)
        in_specs = [pl.BlockSpec(memory_space=pltpu.SMEM)] * scalars + [whole] * (count - scalars)
        out_specs = [whole] * len(outs)
        spec = dict(in_specs=in_specs + [ANY] * len(needs), out_specs=out_specs, scratch_shapes=list(scratch))
    else:
        spec = dict(
            grid_spec=pltpu.PrefetchScalarGridSpec(
                num_scalar_prefetch=scalars,
                grid=grid,
                in_specs=in_specs + [ANY] * len(needs),
                out_specs=out_specs,
                scratch_shapes=list(scratch),
            )
        )
    return pl.pallas_call(
        body,
        out_shape=[jax.ShapeDtypeStruct(shape, kind) for shape, kind in outs],
        compiler_params=pltpu.CompilerParams(vmem_limit_bytes=VMEM_BYTES),
        cost_estimate=cost(micros),
        name=name,
        **spec,
    )(*args, *needs)


def after(values, *needs):
    count = len(values)
    return pl.pallas_call(
        lambda *refs: None,
        in_specs=[ANY] * (count + len(needs)),
        out_specs=[ANY] * count,
        out_shape=[jax.ShapeDtypeStruct(value.shape, value.dtype) for value in values],
        input_output_aliases={i: i for i in range(count)},
        cost_estimate=cost(0.01),
        name="after",
    )(*values, *needs)


def two_heads(pair):
    return jnp.concatenate([pair[:, :HD], pair[:, HD:]], axis=0)


def attend_kernel(place_ref, q_ref, far_ref, near_ref, here_ref, out_ref, probs_ref, kv_ref, bias, table):
    @pl.when(pl.program_id(0) == 0)
    def _():
        key = lax.broadcasted_iota(jnp.int32, (KEYS, ROW), 0)
        query = lax.broadcasted_iota(jnp.int32, (KEYS, ROW), 1)
        first = WINDOW - ROW * place_ref[0]
        inside = (key > query) & (key <= query + WINDOW) & (key >= first)
        one = jnp.where(inside, 0.0, NEG)
        bias[:, :] = jnp.concatenate([one, one], axis=1)
        table[:256, :] = far_ref[...]
        table[256:1024, :] = near_ref[...]
        table[1024:, :] = here_ref[...]
        kv_ref[...] = table[pl.ds(pl.multiple_of(place_ref[1] * ROW, ROW), KEYS), :]

    queries = two_heads(q_ref[...])
    scores = dot(kv_ref[:, :HD], queries, NT) + bias[...]
    highest = jnp.max(scores, axis=0, keepdims=True)
    powers = jnp.exp2((scores - highest) * (SCALE * LOG2E))
    total = jnp.sum(powers, axis=0, keepdims=True)
    probs = (powers * (1.0 / total)).astype(BF)
    probs_ref[0] = probs
    mixed = dot(kv_ref[:, HD:], probs, TN).T.astype(BF)
    out_ref[...] = jnp.concatenate([mixed[:ROW], mixed[ROW:]], axis=1)


def attend(place, queries, far, near, here, needs):
    pair = pl.BlockSpec((ROW, 2 * HD), lambda h, b: (0, h))

    def fixed(rows):
        return pl.BlockSpec((rows, 2 * HD), lambda h, b: (0, 0))

    return call(
        attend_kernel,
        "attend",
        [((ROW, HEADS * HD), BF), ((HEADS // 2, KEYS, 2 * ROW), BF), ((KEYS, 2 * HD), BF)],
        [place, queries, far, near, here],
        needs=needs,
        grid=(HEADS // 2,),
        in_specs=[pair, fixed(256), fixed(768), fixed(768)],
        out_specs=[pair, pl.BlockSpec((1, KEYS, 2 * ROW), lambda h, b: (h, 0, 0)), fixed(KEYS)],
        scratch=[pltpu.VMEM((KEYS, 2 * ROW), F32), pltpu.VMEM((1792, 2 * HD), BF)],
        scalars=1,
    )


HOME_ROWS = [slice(0, 64)] + [slice(64 + ROW * i, 64 + ROW * (i + 1)) for i in range(6)]


def attend_back_kernel(q_ref, kv_ref, out_ref, grad_ref, probs_ref, dq_ref, *rest):
    homes, (dk, dv) = rest[:7], rest[7:]
    step = pl.program_id(0)

    @pl.when(step == 0)
    def _():
        dk[...] = jnp.zeros_like(dk)
        dv[...] = jnp.zeros_like(dv)

    queries = two_heads(q_ref[...])
    grads = two_heads(grad_ref[...])
    outs = two_heads(out_ref[...])
    probs = probs_ref[0]
    delta = jnp.sum((grads.astype(F32) * outs.astype(F32)).T, axis=0, keepdims=True)
    dprobs = dot(kv_ref[:, HD:], grads, NT)
    dscores = (probs.astype(F32) * (dprobs - delta)).astype(BF)
    dqueries = (dot(kv_ref[:, :HD], dscores, TN).T * SCALE).astype(BF)
    dq_ref[...] = jnp.concatenate([dqueries[:ROW], dqueries[ROW:]], axis=1)
    dk[...] += dot(dscores, queries)
    dv[...] += dot(probs, grads)

    @pl.when(step == HEADS // 2 - 1)
    def _():
        for home, rows in zip(homes, HOME_ROWS):
            home[:, :HD] = (dk[rows, :] * SCALE).astype(BF)
            home[:, HD:] = dv[rows, :].astype(BF)


def attend_back(queries, keyval, attended, grads, probs, needs):
    pair = pl.BlockSpec((ROW, 2 * HD), lambda h: (0, h))
    table = pl.BlockSpec((KEYS, 2 * HD), lambda h: (0, 0))

    def home(rows):
        return pl.BlockSpec((rows, 2 * HD), lambda h: (0, 0))

    return call(
        attend_back_kernel,
        "attend_back",
        [((ROW, HEADS * HD), BF), ((64, 2 * HD), BF)] + [((ROW, 2 * HD), BF)] * 6,
        [queries, keyval, attended, grads, probs],
        needs=needs,
        micros=6.0,
        grid=(HEADS // 2,),
        in_specs=[pair, table, pair, pair, pl.BlockSpec((1, KEYS, 2 * ROW), lambda h: (h, 0, 0))],
        out_specs=[pair, home(64)] + [home(ROW)] * 6,
        scratch=[pltpu.VMEM((KEYS, HD), F32), pltpu.VMEM((KEYS, HD), F32)],
    )


def ring_rows(ring, back):
    return pl.ds(pl.multiple_of(lax.rem(ring + 4 - back, 4) * ROW, ROW), ROW)


BACKS = (0, 1, 3, 2)


def mlp_kernel(
    ring_ref, zero, one, three, two, cots, pair_a, pair_b, down_a, down_b, hidden_ref, dpair_ref, rows, rows_b, second_ref,
    second_sum
):
    @pl.when(pl.program_id(0) == 0)
    def _():
        for block, back in zip((zero, one, three, two), BACKS):
            rows[ring_rows(ring_ref[0], back), :] = block[...]
            rows_b[ring_rows(ring_ref[0], back), :] = block[:, 768:]

    step = pl.program_id(0)
    low, high = slice(0, 768), slice(768, 1536)
    both = dot(rows[:, low], pair_a[...]) + dot(rows[:, high], pair_b[...])
    gate, up = both[:, :FF_TILE], both[:, FF_TILE:]
    dhidden = dot(cots[:, low], down_a[...]) + dot(cots[:, high], down_b[...])
    square = gate * gate
    wave = jnp.tanh(gate * (GELU_A + GELU_B * square))
    half = 0.5 + 0.5 * wave
    gelu = gate * half
    slope = half + gate * (0.5 - 0.5 * wave * wave) * (GELU_A + 3.0 * GELU_B * square)
    hidden_ref[...] = (gelu * up).astype(BF)
    dpair = jnp.concatenate([(dhidden * up * slope).astype(BF), (dhidden * gelu).astype(BF)], axis=1)
    dpair_ref[...] = dpair
    part_a = dot(dpair, pair_a[...], NT)
    part_b = dot(dpair, pair_b[...], NT)

    @pl.when(step == 0)
    def _():
        second_sum[:, low] = part_a
        second_sum[:, high] = part_b

    @pl.when((step > 0) & (step < FF_TILES - 1))
    def _():
        second_sum[:, low] += part_a
        second_sum[:, high] += part_b

    @pl.when(step == FF_TILES - 1)
    def _():
        second_ref[:, low] = (second_sum[:, low] + part_a).astype(BF)
        second_ref[:, high] = (second_sum[:, high] + part_b).astype(BF)


def mlp(ring, blocks, cots, rest_mine, rest_other):
    whole = pl.BlockSpec((ROW, 1536), lambda f, r: (0, 0))
    table = pl.BlockSpec((RING, 1536), lambda f, r: (0, 0))
    half = pl.BlockSpec((RING, 768), lambda f, r: (0, 0))
    unit = pl.BlockSpec((RING, FF_TILE), lambda f, r: (0, f))
    pair_unit = pl.BlockSpec((RING, 2 * FF_TILE), lambda f, r: (0, f))
    pair = pl.BlockSpec((768, 2 * FF_TILE), lambda f, r: (0, 2 + f))
    down = pl.BlockSpec((768, FF_TILE), lambda f, r: (0, 10 + f))
    return call(
        mlp_kernel,
        "mlp",
        [((RING, FF), BF), ((RING, 2 * FF), BF), ((RING, 1536), BF), ((RING, 768), BF), ((RING, 1536), BF)],
        [ring, *blocks, cots, rest_mine, rest_other, rest_mine, rest_other],
        grid=(FF_TILES,),
        in_specs=[whole] * 4 + [table, pair, pair, down, down],
        out_specs=[unit, pair_unit, table, half, table],
        scratch=[pltpu.VMEM((RING, 1536), F32)],
        scalars=1,
    )


def down_project_kernel(ring_ref, hidden_ref, down_a, down_b, out_0, out_1, out_3, out_2, total):
    low, high = slice(0, 768), slice(768, 1536)
    total[:, low] = dot(hidden_ref[...], down_a[...], NT)
    total[:, high] = dot(hidden_ref[...], down_b[...], NT)
    for block, back in zip((out_0, out_1, out_3, out_2), BACKS):
        block[...] = total[ring_rows(ring_ref[0], back), :].astype(BF)


def down_project(ring, hidden, rest_mine, rest_other, needs):
    down = pl.BlockSpec((pl.Element(768), pl.Element(FF)), lambda f, r: (0, 1536 + 2 * FF))
    return call(
        down_project_kernel,
        "down_project",
        [((ROW, 1536), BF)] * 4,
        [ring, hidden, rest_mine, rest_other],
        needs=needs,
        grid=(1,),
        in_specs=[pl.BlockSpec((RING, FF), lambda f, r: (0, 0)), down, down],
        out_specs=[pl.BlockSpec((ROW, 1536), lambda f, r: (0, 0))] * 4,
        scratch=[pltpu.VMEM((RING, 1536), F32)],
        scalars=1,
    )


def out_grad_kernel(ring_ref, left_a, left_b, zero, one, three, two, mine_ref, other_ref, rights):
    for block, back in zip((zero, one, three, two), BACKS):
        rights[ring_rows(ring_ref[0], back), :] = block[...]
    mine_ref[...] = dot(left_a[...], rights[...], TN).astype(BF)
    other_ref[...] = dot(left_b[...], rights[...], TN).astype(BF)


def out_grad(ring, left, rights, needs=()):
    tile = 256
    steps = 768 // tile
    out = pl.BlockSpec((tile, 384), lambda i, r: (i, 0))
    return call(
        out_grad_kernel,
        "out_grad",
        [((768, 384), BF)] * 2,
        [ring, left, left, *rights],
        needs=needs,
        grid=(steps,),
        in_specs=[
            pl.BlockSpec((RING, tile), lambda i, r: (0, i)),
            pl.BlockSpec((RING, tile), lambda i, r: (0, i + steps)),
        ]
        + [pl.BlockSpec((ROW, 384), lambda i, r: (0, 0))] * 4,
        out_specs=[out, out],
        scratch=[pltpu.VMEM((RING, 384), BF)],
        scalars=1,
    )


def unit_grad_kernel(left, left_b, cot, cot_b, dpair, dpair_b, hidden, hidden_b, out_ref):
    pair = dot(left[...], dpair[...], TN) + dot(left_b[...], dpair_b[...], TN)
    down = dot(cot[...], hidden[...], TN) + dot(cot_b[...], hidden_b[...], TN)
    out_ref[:, : 2 * FF] = pair.astype(BF)
    out_ref[:, 2 * FF :] = down.astype(BF)


def unit_grad(args):
    tile = 256
    left = pl.BlockSpec((RING, tile), lambda i: (0, i))
    return call(
        unit_grad_kernel,
        "unit_grad",
        [((768, 3 * FF), BF)],
        args,
        micros=6.0,
        grid=(768 // tile,),
        in_specs=[left] * 4 + [pl.BlockSpec(a.shape, lambda i: (0, 0)) for a in args[4:]],
        out_specs=[pl.BlockSpec((tile, 3 * FF), lambda i: (i, 0))],
    )


def merge_kernel(mine_ref, other_ref, out_ref):
    out_ref[...] = (mine_ref[...].astype(F32) + other_ref[...].astype(F32)).astype(BF)


def merge(mine, other, needs=()):
    return call(merge_kernel, "merge", [(mine.shape, BF)], [mine, other], needs=needs)[0]


def normed(rows):
    values = rows.astype(F32)
    inverse = lax.rsqrt(jnp.mean(values * values, axis=-1, keepdims=True) + EPSILON)
    return values, values * inverse, inverse


def norm_back(grad, gain, n, inverse):
    scaled = grad * gain
    return inverse * (scaled - n * jnp.mean(scaled * n, axis=-1, keepdims=True))


def keyval_kernel(head_ref, own, one, three, mine_ref, other_ref, gain_ref, first_ref, keyval_ref):
    gain_ref[:, :768] = mine_ref[:, 640:].astype(F32).T[:8]
    gain_ref[:, 768:] = other_ref[:, 640:].astype(F32).T[:8]

    def project(block):
        first = (normed(block[...])[1] * gain_ref[0:1, :]).astype(BF)
        total = dot(first[:, :768], mine_ref[:, 384:640]) + dot(first[:, 768:], other_ref[:, 384:640])
        return first, total.astype(BF)

    first, total = project(own)
    first_ref[...] = first

    @pl.when(head_ref[0] == 0)
    def _():
        keyval_ref[:ROW, :] = total
        keyval_ref[ROW:, :] = project(three)[1]

    @pl.when(head_ref[0] == 1)
    def _():
        keyval_ref[:ROW, :] = project(one)[1]
        keyval_ref[ROW:, :] = total


def table_kernel(core_ref, mine_ref, other_ref, table_ref, last_ref):
    @pl.when(core_ref[0] == 0)
    def _():
        table_ref[: 2 * ROW, :] = mine_ref[...]
        table_ref[2 * ROW :, :] = other_ref[...]

    @pl.when(core_ref[0] == 1)
    def _():
        table_ref[: 2 * ROW, :] = other_ref[...]
        table_ref[2 * ROW :, :] = mine_ref[...]

    last_ref[...] = table_ref[512:, :]


def ring_cols(ring, ahead):
    return pl.ds(pl.multiple_of(lax.rem(ring + ahead, 4) * 384, 384), 384)


def turn_kernel(ring_ref, zero, one, two, three, out_ref):
    for ahead, block in enumerate((zero, one, two, three)):
        out_ref[:, ring_cols(ring_ref[0], ahead)] = block[...]


def split_kernel(ring_ref, rows_ref, zero, one, two, three):
    for ahead, block in enumerate((zero, one, two, three)):
        block[...] = rows_ref[:, ring_cols(ring_ref[0], ahead)]


def split(ring, rows):
    return call(split_kernel, "split", [((ROW, 384), BF)] * 4, [ring, rows], scalars=1)


def query_kernel(first_ref, one, three, two, gain_ref, mine_ref, other_ref, all_ref, *outs):
    all_ref[:ROW, :] = first_ref[...]
    for i, block in ((1, one), (2, three), (3, two)):
        all_ref[ROW * i : ROW * (i + 1), :] = (normed(block[...])[1] * gain_ref[0:1, :]).astype(BF)
    rows = all_ref[...]
    total = (dot(rows[:, :768], mine_ref[:, :384]) + dot(rows[:, 768:], other_ref[:, :384])).astype(BF)
    for i in range(4):
        outs[i][...] = total[ROW * i : ROW * (i + 1)]


def middle_kernel(attended_ref, mine_ref, other_ref, token_ref, gain_ref, middle_ref, second_ref):
    attended = attended_ref[...]
    branch = jnp.concatenate([dot(attended, mine_ref[...], NT), dot(attended, other_ref[...], NT)], axis=1)
    middle = token_ref[...].astype(F32) + branch
    middle_ref[...] = middle
    second_ref[...] = (normed(middle)[1] * gain_ref[1:2, :]).astype(BF)


def middle_back_kernel(
    parts, middle_ref, cot_ref, gain_ref, mine_ref, other_ref, grad_ref, low_ref, terms_ref, attended_ref
):
    grad_second = sum(parts[i].astype(F32) for i in range(4))
    _, n2, rs2 = normed(middle_ref[...])
    grad_middle = cot_ref[...].astype(F32) + norm_back(grad_second, gain_ref[1:2, :], n2, rs2)
    grad_ref[...] = grad_middle
    low = grad_middle.astype(BF)
    for i in range(4):
        low_ref[i] = low
    terms_ref[...] = (grad_second * n2).astype(BF)
    attended_ref[...] = (dot(low[:, :768], mine_ref[...]) + dot(low[:, 768:], other_ref[...])).astype(BF)


def first_back_kernel(
    dquery_0, dquery_1, dquery_3, dquery_2, home_6, home_5, home_4, home_3, home_2, home_1, home_0, rest_a, rest_b,
    first_ref, second_terms, own_ref, one, three, two, tail_a, tail_b, sums,
):
    dquery = jnp.concatenate([dquery_0[...], dquery_1[...], dquery_3[...], dquery_2[...]], axis=0)
    sums[...] = sum(home[...].astype(F32) for home in (home_5, home_4, home_3, home_2, home_1, home_0))
    sums[128:, :] += home_6[...].astype(F32)
    dkeyval = sums[...].astype(BF)
    column = lax.broadcasted_iota(jnp.int32, (RING + ROW, 128), 1)
    row = lax.broadcasted_iota(jnp.int32, (RING + ROW, 128), 0)
    picks = jnp.where(column == (row >= RING).astype(jnp.int32), 1.0, 0.0).astype(BF)
    for cols, rest, tail in ((slice(0, 768), rest_a, tail_a), (slice(768, 1536), rest_b, tail_b)):
        first = first_ref[:, cols]
        grads = dot(dquery, rest[:, :384], NT)
        own = grads[:ROW] + dot(dkeyval, rest[:, 384:640], NT)
        own_ref[:, cols] = own
        for i, ref in ((1, one), (2, three), (3, two)):
            ref[:, cols] = grads[ROW * i : ROW * (i + 1)].astype(BF)
        grads = jnp.concatenate([own, grads[ROW:]], axis=0)
        terms = jnp.concatenate([(grads * first.astype(F32)).astype(BF), second_terms[:, cols]], axis=0)
        tail[:, :384] = dot(first, dquery, TN).astype(BF)
        tail[:, 384:640] = dot(first[:ROW], dkeyval, TN).astype(BF)
        tail[:, 640:] = dot(terms, picks, TN).astype(BF)


def input_kernel(own_ref, one, three, two, token_ref, gain_ref, middle_ref, input_ref):
    grad_first = own_ref[...] + sum(part[...].astype(F32) for part in (one, three, two))
    _, n1, rs1 = normed(token_ref[...])
    input_ref[...] = (middle_ref[...] + norm_back(grad_first, gain_ref[0:1, :], n1, rs1)).astype(BF)


def shift_all(block, distance):
    count = 128
    route = [(i, i + distance) for i in range(count) if 0 <= i + distance < count]
    return lax.ppermute(block, AXES, route)


def shift_groups(block, distance):
    return lax.ppermute(block, ("z", "xh", "y"), [(i, i + distance) for i in range(32 - distance)])


def shift_x(block, distance):
    return lax.ppermute(block, CHIPS_X, [(i, (i + distance) % 4) for i in range(4)])


def swap(block, axis):
    return lax.ppermute(block, axis, [(0, 1), (1, 0)])


def shards(tokens, cotangent, w_query, w_key, w_value, w_out, w_gate, w_up, w_down, gain_attn, gain_mlp):
    core = lax.axis_index("core")
    xh = lax.axis_index("xh")
    head = lax.axis_index("head")
    ring = 2 * xh + head
    place = jnp.stack([lax.axis_index(AXES), 2 * core + head]).astype(jnp.int32)
    ring_scalar, core_scalar, head_scalar = (i.astype(jnp.int32).reshape(1) for i in (ring, core, head))
    eight = ("xh", "core", "head")
    four = ("xh", "core")

    def ordered(index, first, second, axis):
        return jnp.concatenate(
            [jnp.where(index == 0, first, second), jnp.where(index == 0, second, first)], axis=axis
        )

    def local_order(rows):
        cut = rows.reshape(ROW, 4, 2, 192)
        low = cut[:, :, 0].reshape(ROW, 768)
        high = cut[:, :, 1].reshape(ROW, 768)
        return ordered(core, low, high, 1)

    def true_order(rows):
        low = jnp.where(core == 0, rows[:, :768], rows[:, 768:]).reshape(ROW, 4, 192)
        high = jnp.where(core == 0, rows[:, 768:], rows[:, :768]).reshape(ROW, 4, 192)
        return jnp.stack([low, high], axis=2).reshape(ROW, 1536)

    def spread(piece):
        sent = jnp.broadcast_to(piece[None], (16,) + piece.shape)
        return lax.all_to_all(sent, PLANE, 0, 0, tiled=True).reshape(768, -1)

    def gather(piece):
        return lax.all_gather(piece, PLANE, axis=0, tiled=True)

    gains = jnp.pad(jnp.stack([gain_attn, gain_mlp], axis=1), ((0, 0), (0, 126)))
    query_cut = w_query.reshape(12, 2, 2, 384).transpose(2, 1, 0, 3)
    common = jnp.broadcast_to(jnp.concatenate([w_key, w_value, gains], axis=1), (2, 2, 12, 384))
    own_qkv = jnp.concatenate([query_cut, common], axis=3)
    own_attn = jnp.concatenate([jnp.broadcast_to(w_out.T, (2, 2, 24, 768)), own_qkv], axis=2)
    own_attn = jnp.broadcast_to(own_attn[:, None], (2, 2, 2, 36, 768)).reshape(8, 36, 768)
    got = lax.all_to_all(own_attn, eight, 0, 0, tiled=True)
    got = lax.dynamic_slice_in_dim(got, core * 4, 4, 0)
    qkv_piece = got[:, 24:].reshape(48, 768)
    out_piece = got[:, :24].reshape(2, 2, 24, 2, 384).transpose(0, 2, 3, 1, 4).reshape(48, 1536)
    token_own = local_order(tokens)
    token_1, token_3, token_2 = (local_order(shift_x(tokens, k)) for k in (1, 3, 2))
    qkv_mine = spread(qkv_piece)
    (qkv_mine,) = after([qkv_mine], token_1, token_3)

    pair_cut = jnp.stack([w_gate, w_up], axis=1).reshape(24, 2, 2, FF_TILES, FF_TILE)
    pair_cut = pair_cut.transpose(2, 0, 3, 1, 4).reshape(2, 24, 2 * FF)
    down_cut = w_down.T.reshape(24, 2, FF).transpose(1, 0, 2)
    own_mlp = jnp.concatenate([pair_cut, down_cut], axis=2)
    sent_a = jnp.where(core == 0, own_mlp[0], own_mlp[1])
    sent_b = jnp.where(core == 0, own_mlp[1], own_mlp[0])
    got_a = lax.ppermute(sent_a, four, [(0, 0), (1, 2), (2, 1), (3, 3)])
    got_b = lax.ppermute(sent_b, four, [(0, 2), (1, 0), (2, 3), (3, 1)])
    rest_mine = gather(jnp.concatenate([out_piece, ordered(xh, got_a, got_b, 0)], axis=1))

    qkv_other = swap(qkv_mine, "core")
    gain_rows, first_own, keyval_pair = call(
        keyval_kernel,
        "keyval",
        [((8, 1536), F32), ((ROW, 1536), BF), ((2 * ROW, 256), BF)],
        [head_scalar, token_own, token_1, token_3, qkv_mine, qkv_other],
        scalars=1,
    )
    here, last = call(
        table_kernel,
        "table",
        [((768, 256), BF), ((256, 256), BF)],
        [core_scalar, keyval_pair, swap(keyval_pair, "core")],
        scalars=1,
    )
    near, far = shift_groups(here, 1), shift_groups(last, 2)
    first_all, query_0, ring_1, ring_3, ring_2 = call(
        query_kernel,
        "query",
        [((RING, 1536), BF)] + [((ROW, 384), BF)] * 4,
        [first_own, token_1, token_3, token_2, gain_rows, qkv_mine, qkv_other],
        needs=[here],
    )
    query_1, query_3, query_2 = shift_x(ring_1, -1), shift_x(ring_3, -3), shift_x(ring_2, -2)
    (queries,) = call(
        turn_kernel, "turn", [((ROW, 1536), BF)], [ring_scalar, query_0, query_1, query_2, query_3], scalars=1
    )
    cot_own = local_order(cotangent)
    (cot_sent,) = after([cot_own], qkv_mine)
    cots = lax.all_to_all(jnp.broadcast_to(cot_sent[None], (4, ROW, 1536)), CHIPS_X, 0, 0, tiled=True)
    cots = cots.reshape(RING, 1536)
    attended, probs, keyval = attend(place, queries, far, near, here, [cots])

    attended_0, attended_1, attended_2, attended_3 = split(ring_scalar, attended)
    attended_1, attended_3, attended_2 = (
        shift_x(block, k) for block, k in ((attended_1, 1), (attended_3, 3), (attended_2, 2))
    )
    (rest_mine,) = after([rest_mine], attended)
    out_mine = rest_mine[:, :1536]
    out_other = swap(out_mine, "core")
    middle, second_own = call(
        middle_kernel,
        "middle",
        [((ROW, 1536), F32), ((ROW, 1536), BF)],
        [attended, out_mine, out_other, token_own, gain_rows],
    )
    blocks = [second_own] + [shift_x(second_own, k) for k in (1, 3, 2)]
    (rest_mine,) = after([rest_mine], out_other)
    rest_other = swap(rest_mine, "core")

    hidden, dpair, seconds, seconds_b, second_part = mlp(ring_scalar, blocks, cots, rest_mine, rest_other)
    second_home = lax.all_to_all(second_part.reshape(4, ROW, 1536), CHIPS_X, 0, 0, tiled=True)

    def planes(total):
        got = lax.all_to_all(total.reshape(16, 48, -1), PLANE, 0, 0, tiled=True)
        return jnp.sum(got.astype(F32), axis=0).astype(BF)

    (unit_total,) = unit_grad(
        [seconds, swap(seconds_b, "core"), cots, swap(cots[:, 768:], "core")]
        + [dpair, swap(dpair, "core"), hidden, swap(hidden, "core")]
    )
    (unit_total,) = after([unit_total], second_home)
    unit_grads = lax.psum_scatter(unit_total, PLANE, scatter_dimension=0, tiled=True)
    grad_middle, grad_branch, second_terms, grad_attended = call(
        middle_back_kernel,
        "middle_back",
        [((ROW, 1536), F32), ((4, ROW, 1536), BF), ((ROW, 1536), BF), ((ROW, 1536), BF)],
        [second_home, middle, cot_own, gain_rows, out_mine, out_other],
    )
    branches = lax.all_to_all(grad_branch, CHIPS_X, 0, 0, tiled=True).reshape(RING, 1536)
    dqueries, *homes = attend_back(queries, keyval, attended, grad_attended, probs, [])

    outs = down_project(ring_scalar, hidden, rest_mine, rest_other, [dqueries])
    dquery_0, dquery_1, dquery_2, dquery_3 = split(ring_scalar, dqueries)
    dquery_1, dquery_3, dquery_2 = (
        shift_x(block, k) for block, k in ((dquery_1, 1), (dquery_3, 3), (dquery_2, 2))
    )
    homes = [shift_all(home, -k) for home, k in zip(homes, (6, 5, 4, 3, 2, 1))] + [homes[6]]
    own_first, first_1, first_3, first_2, tail_mine, tail_other = call(
        first_back_kernel,
        "first_back",
        [((ROW, 1536), F32)] + [((ROW, 1536), BF)] * 3 + [((768, 768), BF)] * 2,
        [
            dquery_0, dquery_1, dquery_3, dquery_2, *homes, qkv_mine, qkv_other, first_all, second_terms,
        ],
        scratch=[pltpu.VMEM((ROW, 256), F32)],
    )
    tail_total = merge(tail_mine, swap(tail_other, "core"))
    tail_grads = planes(tail_total)
    mlp_own = outs[0].astype(F32)
    for out, k in zip(after(outs[1:], tail_mine), (1, 3, 2)):
        mlp_own = mlp_own + shift_x(out, -k).astype(F32)
    block_out = true_order((middle + mlp_own).astype(BF))
    tail_grads = tail_grads.reshape(4, 12, 768)
    tail_sent = jnp.where(jnp.arange(2).reshape(2, 1, 1, 1) == core, tail_grads[None], 0).reshape(8, 12, 768)
    tail_got = lax.all_to_all(tail_sent, eight, 0, 0, tiled=True).reshape(2, 2, 2, 12, 768)
    tail_got = jnp.where(xh == 0, tail_got[:, 0], tail_got[:, 1])
    grad_w_query = tail_got[..., :384].astype(F32).transpose(2, 1, 0, 3).reshape(12, 1536)
    tail_sum = jnp.sum(tail_got[..., 384:].astype(F32), axis=(0, 1))
    (input_grad,) = call(
        input_kernel,
        "input",
        [((ROW, 1536), BF)],
        [own_first, shift_x(first_1, -1), shift_x(first_3, -3), shift_x(first_2, -2), token_own, gain_rows, grad_middle],
        needs=[tail_got],
    )
    input_grad = true_order(input_grad)

    out_a, out_b = out_grad(
        ring_scalar, branches, [attended_0, attended_1, attended_3, attended_2], [tail_total]
    )
    out_grads = planes(merge(out_a, swap(out_b, "core"), needs=[tail_grads]))

    owned = jnp.concatenate([unit_grads, out_grads], axis=1)
    give_a = jnp.where(xh == 0, owned[:24], owned[24:])
    give_b = jnp.where(xh == 0, owned[24:], owned[:24])
    got_a = lax.ppermute(give_a, four, [(0, 0), (2, 1), (1, 2), (3, 3)])
    got_b = lax.ppermute(give_b, four, [(2, 0), (0, 1), (3, 2), (1, 3)])
    low = jnp.where(core == 0, got_a, got_b).astype(F32)
    high = jnp.where(core == 0, got_b, got_a).astype(F32)

    def both(start, width):
        return jnp.concatenate([low[:, start : start + width], high[:, start : start + width]], axis=1)

    def pair_out(which):
        cut = jnp.stack([low[:, : 2 * FF], high[:, : 2 * FF]], axis=1).reshape(24, 2, FF_TILES, 2, FF_TILE)
        return cut[:, :, :, which].reshape(24, 2 * FF)

    return (
        block_out,
        input_grad,
        grad_w_query,
        tail_sum[:, :128],
        tail_sum[:, 128:256],
        both(3 * FF, 384).T,
        pair_out(0),
        pair_out(1),
        both(2 * FF, FF).T,
        tail_sum[:, 256] / gain_attn.astype(F32),
        tail_sum[:, 257],
    )


def solution(mesh):
    grid = Mesh(mesh.devices.reshape(SIZES), AXES)
    seq = ("z", "xh", "y", "core")
    rows, both, cols = P(AXES, None), P(seq, "head"), P("head", seq)
    in_specs = (rows, rows, rows, rows, rows, cols, both, both, cols, P(AXES), P(AXES))
    out_specs = (rows, rows, rows, rows, rows, cols, both, both, cols, P(AXES), P(AXES))
    return jax.shard_map(shards, mesh=grid, in_specs=in_specs, out_specs=out_specs, check_vma=False)
```

```python
import functools
import jax
import jax.numpy as jnp
from jax import lax
from jax.experimental import pallas as pl
from jax.experimental.pallas import tpu as pltpu
from jax.sharding import Mesh
from jax.sharding import PartitionSpec as P

WINDOW = 1024
EPSILON = 1e-06
AXES = ("z", "xh", "y", "core", "head")
SIZES = (4, 2, 4, 2, 2)
CHIPS_X = ("xh", "head")
PLANE = ("z", "y")
ROW = 192
KEYS = 1216
HEADS = 12
HD = 128
BF = jnp.bfloat16
F32 = jnp.float32
NEG = -1e30
SCALE = HD ** (-0.5)
LOG2E = 1.4426950408889634
VMEM_BYTES = 56 * 1024 * 1024
FF = 1152
FF_TILES = 3
FF_TILE = 384
RING = 768
GELU_A = 0.7978845608028654
GELU_B = GELU_A * 0.044715

NN = (((1,), (0,)), ((), ()))
NT = (((1,), (1,)), ((), ()))
TN = (((0,), (0,)), ((), ()))


def dot(a, b, dims=NN):
    return lax.dot_general(a, b, dims, preferred_element_type=F32)


ANY = pl.BlockSpec(memory_space=pl.ANY)


def cost(micros):
    return pl.CostEstimate(flops=int(micros * 1.0e9), bytes_accessed=1000000, transcendentals=0)


def call(kernel, name, outs, args, needs=(), micros=0.01, grid=None, in_specs=None, out_specs=None, scratch=(), scalars=0):
    count = len(args)

    def body(*refs):
        kernel(*refs[:count], *refs[count + len(needs) :])

    if in_specs is None:
        whole = pl.BlockSpec(memory_space=pltpu.VMEM)
        in_specs = [pl.BlockSpec(memory_space=pltpu.SMEM)] * scalars + [whole] * (count - scalars)
        out_specs = [whole] * len(outs)
        spec = dict(in_specs=in_specs + [ANY] * len(needs), out_specs=out_specs, scratch_shapes=list(scratch))
    else:
        spec = dict(
            grid_spec=pltpu.PrefetchScalarGridSpec(
                num_scalar_prefetch=scalars,
                grid=grid,
                in_specs=in_specs + [ANY] * len(needs),
                out_specs=out_specs,
                scratch_shapes=list(scratch),
            )
        )
    return pl.pallas_call(
        body,
        out_shape=[jax.ShapeDtypeStruct(shape, kind) for shape, kind in outs],
        compiler_params=pltpu.CompilerParams(vmem_limit_bytes=VMEM_BYTES),
        cost_estimate=cost(micros),
        name=name,
        **spec,
    )(*args, *needs)


def after(values, *needs):
    count = len(values)
    return pl.pallas_call(
        lambda *refs: None,
        in_specs=[ANY] * (count + len(needs)),
        out_specs=[ANY] * count,
        out_shape=[jax.ShapeDtypeStruct(value.shape, value.dtype) for value in values],
        input_output_aliases={i: i for i in range(count)},
        cost_estimate=cost(0.01),
        name="after",
    )(*values, *needs)


def two_heads(pair):
    return jnp.concatenate([pair[:, :HD], pair[:, HD:]], axis=0)


def attend_kernel(place_ref, q_ref, far_ref, near_ref, here_ref, out_ref, probs_ref, kv_ref, bias, table):
    @pl.when(pl.program_id(0) == 0)
    def _():
        key = lax.broadcasted_iota(jnp.int32, (KEYS, ROW), 0)
        query = lax.broadcasted_iota(jnp.int32, (KEYS, ROW), 1)
        first = WINDOW - ROW * place_ref[0]
        inside = (key > query) & (key <= query + WINDOW) & (key >= first)
        one = jnp.where(inside, 0.0, NEG)
        bias[:, :] = jnp.concatenate([one, one], axis=1)
        table[:256, :] = far_ref[...]
        table[256:1024, :] = near_ref[...]
        table[1024:, :] = here_ref[...]
        kv_ref[...] = table[pl.ds(pl.multiple_of(place_ref[1] * ROW, ROW), KEYS), :]

    queries = two_heads(q_ref[...])
    scores = dot(kv_ref[:, :HD], queries, NT) + bias[...]
    highest = jnp.max(scores, axis=0, keepdims=True)
    powers = jnp.exp2((scores - highest) * (SCALE * LOG2E))
    total = jnp.sum(powers, axis=0, keepdims=True)
    probs = (powers * (1.0 / total)).astype(BF)
    probs_ref[0] = probs
    mixed = dot(kv_ref[:, HD:], probs, TN).T.astype(BF)
    out_ref[...] = jnp.concatenate([mixed[:ROW], mixed[ROW:]], axis=1)


def attend(place, queries, far, near, here, needs):
    pair = pl.BlockSpec((ROW, 2 * HD), lambda h, b: (0, h))

    def fixed(rows):
        return pl.BlockSpec((rows, 2 * HD), lambda h, b: (0, 0))

    return call(
        attend_kernel,
        "attend",
        [((ROW, HEADS * HD), BF), ((HEADS // 2, KEYS, 2 * ROW), BF), ((KEYS, 2 * HD), BF)],
        [place, queries, far, near, here],
        needs=needs,
        micros=10.0,
        grid=(HEADS // 2,),
        in_specs=[pair, fixed(256), fixed(768), fixed(768)],
        out_specs=[pair, pl.BlockSpec((1, KEYS, 2 * ROW), lambda h, b: (h, 0, 0)), fixed(KEYS)],
        scratch=[pltpu.VMEM((KEYS, 2 * ROW), F32), pltpu.VMEM((1792, 2 * HD), BF)],
        scalars=1,
    )


HOME_ROWS = [slice(0, 64)] + [slice(64 + ROW * i, 64 + ROW * (i + 1)) for i in range(6)]


def attend_back_kernel(q_ref, kv_ref, out_ref, grad_ref, probs_ref, dq_ref, *rest):
    homes, (dk, dv) = rest[:7], rest[7:]
    step = pl.program_id(0)

    @pl.when(step == 0)
    def _():
        dk[...] = jnp.zeros_like(dk)
        dv[...] = jnp.zeros_like(dv)

    queries = two_heads(q_ref[...])
    grads = two_heads(grad_ref[...])
    outs = two_heads(out_ref[...])
    probs = probs_ref[0]
    delta = jnp.sum((grads.astype(F32) * outs.astype(F32)).T, axis=0, keepdims=True)
    dprobs = dot(kv_ref[:, HD:], grads, NT)
    dscores = (probs.astype(F32) * (dprobs - delta)).astype(BF)
    dqueries = (dot(kv_ref[:, :HD], dscores, TN).T * SCALE).astype(BF)
    dq_ref[...] = jnp.concatenate([dqueries[:ROW], dqueries[ROW:]], axis=1)
    dk[...] += dot(dscores, queries)
    dv[...] += dot(probs, grads)

    @pl.when(step == HEADS // 2 - 1)
    def _():
        for home, rows in zip(homes, HOME_ROWS):
            home[:, :HD] = (dk[rows, :] * SCALE).astype(BF)
            home[:, HD:] = dv[rows, :].astype(BF)


def attend_back(queries, keyval, attended, grads, probs, needs):
    pair = pl.BlockSpec((ROW, 2 * HD), lambda h: (0, h))
    table = pl.BlockSpec((KEYS, 2 * HD), lambda h: (0, 0))

    def home(rows):
        return pl.BlockSpec((rows, 2 * HD), lambda h: (0, 0))

    return call(
        attend_back_kernel,
        "attend_back",
        [((ROW, HEADS * HD), BF), ((64, 2 * HD), BF)] + [((ROW, 2 * HD), BF)] * 6,
        [queries, keyval, attended, grads, probs],
        needs=needs,
        micros=6.0,
        grid=(HEADS // 2,),
        in_specs=[pair, table, pair, pair, pl.BlockSpec((1, KEYS, 2 * ROW), lambda h: (h, 0, 0))],
        out_specs=[pair, home(64)] + [home(ROW)] * 6,
        scratch=[pltpu.VMEM((KEYS, HD), F32), pltpu.VMEM((KEYS, HD), F32)],
    )


def ring_rows(ring, back):
    return pl.ds(pl.multiple_of(lax.rem(ring + 4 - back, 4) * ROW, ROW), ROW)


BACKS = (0, 1, 3, 2)


def mlp_kernel(
    ring_ref, zero, one, three, two, cots, pair_a, pair_b, down_a, down_b, hidden_ref, dpair_ref, rows, rows_b, second_ref,
    second_sum
):
    @pl.when(pl.program_id(0) == 0)
    def _():
        for block, back in zip((zero, one, three, two), BACKS):
            rows[ring_rows(ring_ref[0], back), :] = block[...]
            rows_b[ring_rows(ring_ref[0], back), :] = block[:, 768:]

    step = pl.program_id(0)
    low, high = slice(0, 768), slice(768, 1536)
    both = dot(rows[:, low], pair_a[...]) + dot(rows[:, high], pair_b[...])
    gate, up = both[:, :FF_TILE], both[:, FF_TILE:]
    dhidden = dot(cots[:, low], down_a[...]) + dot(cots[:, high], down_b[...])
    square = gate * gate
    wave = jnp.tanh(gate * (GELU_A + GELU_B * square))
    half = 0.5 + 0.5 * wave
    gelu = gate * half
    slope = half + gate * (0.5 - 0.5 * wave * wave) * (GELU_A + 3.0 * GELU_B * square)
    hidden_ref[...] = (gelu * up).astype(BF)
    dpair = jnp.concatenate([(dhidden * up * slope).astype(BF), (dhidden * gelu).astype(BF)], axis=1)
    dpair_ref[...] = dpair
    part_a = dot(dpair, pair_a[...], NT)
    part_b = dot(dpair, pair_b[...], NT)

    @pl.when(step == 0)
    def _():
        second_sum[:, low] = part_a
        second_sum[:, high] = part_b

    @pl.when((step > 0) & (step < FF_TILES - 1))
    def _():
        second_sum[:, low] += part_a
        second_sum[:, high] += part_b

    @pl.when(step == FF_TILES - 1)
    def _():
        second_ref[:, low] = (second_sum[:, low] + part_a).astype(BF)
        second_ref[:, high] = (second_sum[:, high] + part_b).astype(BF)


def mlp(ring, blocks, cots, rest_mine, rest_other, needs):
    whole = pl.BlockSpec((ROW, 1536), lambda f, r: (0, 0))
    table = pl.BlockSpec((RING, 1536), lambda f, r: (0, 0))
    half = pl.BlockSpec((RING, 768), lambda f, r: (0, 0))
    unit = pl.BlockSpec((RING, FF_TILE), lambda f, r: (0, f))
    pair_unit = pl.BlockSpec((RING, 2 * FF_TILE), lambda f, r: (0, f))
    pair = pl.BlockSpec((768, 2 * FF_TILE), lambda f, r: (0, 2 + f))
    down = pl.BlockSpec((768, FF_TILE), lambda f, r: (0, 10 + f))
    return call(
        mlp_kernel,
        "mlp",
        [((RING, FF), BF), ((RING, 2 * FF), BF), ((RING, 1536), BF), ((RING, 768), BF), ((RING, 1536), BF)],
        [ring, *blocks, cots, rest_mine, rest_other, rest_mine, rest_other],
        needs=needs,
        micros=20.0,
        grid=(FF_TILES,),
        in_specs=[whole] * 4 + [table, pair, pair, down, down],
        out_specs=[unit, pair_unit, table, half, table],
        scratch=[pltpu.VMEM((RING, 1536), F32)],
        scalars=1,
    )


def down_project_kernel(hidden_ref, down_a, down_b, out_ref):
    out_ref[:, :768] = dot(hidden_ref[...], down_a[...], NT).astype(BF)
    out_ref[:, 768:] = dot(hidden_ref[...], down_b[...], NT).astype(BF)


def down_project(hidden, rest_mine, rest_other):
    down = pl.BlockSpec((pl.Element(768), pl.Element(FF)), lambda f: (0, 1536 + 2 * FF))
    table = pl.BlockSpec((RING, 1536), lambda f: (0, 0))
    return call(
        down_project_kernel,
        "down_project",
        [((RING, 1536), BF)],
        [hidden, rest_mine, rest_other],
        grid=(1,),
        in_specs=[pl.BlockSpec((RING, FF), lambda f: (0, 0)), down, down],
        out_specs=[table],
    )[0]


def out_grad_kernel(left, left_b, right, right_b, out_ref):
    lefts = jnp.concatenate([left[...], left_b[...]], axis=0)
    rights = jnp.concatenate([right[...], right_b[...]], axis=0)
    out_ref[...] = dot(lefts, rights, TN).astype(BF)


def out_grad(left, left_b, right, right_b, total):
    lefts = pl.BlockSpec((ROW, 768), lambda i: (0, 0))
    rights = pl.BlockSpec((ROW, 384), lambda i: (0, i))
    return pl.pallas_call(
        lambda *refs: out_grad_kernel(*refs[:4], refs[5]),
        grid=(4,),
        in_specs=[lefts, lefts, rights, rights, ANY],
        out_specs=pl.BlockSpec((768, 384), lambda i: (0, 3 * FF // 384 + i)),
        out_shape=jax.ShapeDtypeStruct(total.shape, BF),
        input_output_aliases={4: 0},
        compiler_params=pltpu.CompilerParams(vmem_limit_bytes=VMEM_BYTES),
        cost_estimate=cost(0.01),
        name="out_grad",
    )(left, left_b, right, right_b, total)


def unit_grad_kernel(left, left_b, cot, cot_b, dpair, dpair_b, hidden, hidden_b, out_ref):
    pair = dot(left[...], dpair[...], TN) + dot(left_b[...], dpair_b[...], TN)
    down = dot(cot[...], hidden[...], TN) + dot(cot_b[...], hidden_b[...], TN)
    out_ref[:, : 2 * FF] = pair.astype(BF)
    out_ref[:, 2 * FF :] = down.astype(BF)


def unit_grad(args, needs):
    tile = 256
    left = pl.BlockSpec((RING, tile), lambda i: (0, i))
    return call(
        unit_grad_kernel,
        "unit_grad",
        [((768, 3 * FF + 1536), BF)],
        args,
        needs=needs,
        micros=6.0,
        grid=(768 // tile,),
        in_specs=[left] * 4 + [pl.BlockSpec(a.shape, lambda i: (0, 0)) for a in args[4:]],
        out_specs=[pl.BlockSpec((tile, 3 * FF), lambda i: (i, 0))],
    )


def merge_kernel(*refs):
    out_ref = refs[-1]
    start = 0
    for mine, other in zip(refs[:-1:2], refs[1:-1:2]):
        width = mine.shape[1]
        out_ref[:, start : start + width] = (mine[...].astype(F32) + other[...].astype(F32)).astype(BF)
        start += width


def merge(*pairs, needs=()):
    width = sum(mine.shape[1] for mine, _ in pairs)
    return call(merge_kernel, "merge", [((768, width), BF)], [array for pair in pairs for array in pair], needs)[0]


def normed(rows):
    values = rows.astype(F32)
    inverse = lax.rsqrt(jnp.mean(values * values, axis=-1, keepdims=True) + EPSILON)
    return values, values * inverse, inverse


def norm_back(grad, gain, n, inverse):
    scaled = grad * gain
    return inverse * (scaled - n * jnp.mean(scaled * n, axis=-1, keepdims=True))


def keyval_kernel(ids, own, one, three, mine_ref, other_ref, gain_ref, token_ref, first_ref, keyval_ref):
    head, core = ids[0], ids[1]
    gain_ref[:, :768] = mine_ref[:, 640:].astype(F32).T[:8]
    gain_ref[:, 768:] = other_ref[:, 640:].astype(F32).T[:8]

    def local(block):
        return local_order(block[...].astype(F32), core)

    def project(block):
        first = (normed(block)[1] * gain_ref[0:1, :]).astype(BF)
        total = dot(first[:, :768], mine_ref[:, 384:640]) + dot(first[:, 768:], other_ref[:, 384:640])
        return first, total.astype(BF)

    token = local(own)
    token_ref[...] = token.astype(BF)
    first, total = project(token)
    first_ref[...] = first

    @pl.when(head == 0)
    def _():
        keyval_ref[:ROW, :] = total
        keyval_ref[ROW:, :] = project(local(three))[1]

    @pl.when(head == 1)
    def _():
        keyval_ref[:ROW, :] = project(local(one))[1]
        keyval_ref[ROW:, :] = total


def local_order(rows, core):
    low = jnp.concatenate([rows[:, 384 * z : 384 * z + 192] for z in range(4)], axis=1)
    high = jnp.concatenate([rows[:, 384 * z + 192 : 384 * z + 384] for z in range(4)], axis=1)
    return jnp.concatenate([jnp.where(core == 0, low, high), jnp.where(core == 0, high, low)], axis=1)


def true_order(rows, core):
    low = jnp.where(core == 0, rows[:, :768], rows[:, 768:])
    high = jnp.where(core == 0, rows[:, 768:], rows[:, :768])
    cuts = [half[:, 192 * z : 192 * (z + 1)] for z in range(4) for half in (low, high)]
    return jnp.concatenate(cuts, axis=1)


def order_kernel(core_ref, rows_ref, out_ref, copies):
    rows = local_order(rows_ref[...].astype(F32), core_ref[0]).astype(BF)
    out_ref[...] = rows
    for i in range(4):
        copies[i] = rows


def table_kernel(core_ref, mine_ref, other_ref, table_ref, last_ref):
    @pl.when(core_ref[0] == 0)
    def _():
        table_ref[: 2 * ROW, :] = mine_ref[...]
        table_ref[2 * ROW :, :] = other_ref[...]

    @pl.when(core_ref[0] == 1)
    def _():
        table_ref[: 2 * ROW, :] = other_ref[...]
        table_ref[2 * ROW :, :] = mine_ref[...]

    last_ref[...] = table_ref[512:, :]


def ring_cols(ring, ahead):
    return pl.ds(pl.multiple_of(lax.rem(ring + ahead, 4) * 384, 384), 384)


def turn_kernel(ring_ref, zero, one, two, three, out_ref):
    for ahead, block in enumerate((zero, one, two, three)):
        out_ref[:, ring_cols(ring_ref[0], ahead)] = block[...]


def split_kernel(ring_ref, rows_ref, zero, one, two, three):
    for ahead, block in enumerate((zero, one, two, three)):
        block[...] = rows_ref[:, ring_cols(ring_ref[0], ahead)]


def split(ring, rows):
    return call(split_kernel, "split", [((ROW, 384), BF)] * 4, [ring, rows], scalars=1)


def query_kernel(core_ref, first_ref, one, three, two, gain_ref, mine_ref, other_ref, all_ref, *outs):
    all_ref[:ROW, :] = first_ref[...]
    for i, block in ((1, one), (2, three), (3, two)):
        all_ref[ROW * i : ROW * (i + 1), :] = (
            normed(local_order(block[...].astype(F32), core_ref[0]))[1] * gain_ref[0:1, :]
        ).astype(BF)
    rows = all_ref[...]
    total = (dot(rows[:, :768], mine_ref[:, :384]) + dot(rows[:, 768:], other_ref[:, :384])).astype(BF)
    for i in range(4):
        outs[i][...] = total[ROW * i : ROW * (i + 1)]


def middle_kernel(attended_ref, mine_ref, other_ref, token_ref, gain_ref, middle_ref, second_ref):
    attended = attended_ref[...]
    branch = jnp.concatenate([dot(attended, mine_ref[...], NT), dot(attended, other_ref[...], NT)], axis=1)
    middle = token_ref[...].astype(F32) + branch
    middle_ref[...] = middle
    second_ref[...] = (normed(middle)[1] * gain_ref[1:2, :]).astype(BF)


def middle_back_kernel(
    parts, middle_ref, cot_ref, gain_ref, mine_ref, other_ref, grad_ref, low_ref, high_ref, terms_ref, attended_ref
):
    grad_second = sum(parts[i].astype(F32) for i in range(4))
    _, n2, rs2 = normed(middle_ref[...])
    grad_middle = cot_ref[...].astype(F32) + norm_back(grad_second, gain_ref[1:2, :], n2, rs2)
    grad_ref[...] = grad_middle
    low = grad_middle.astype(BF)
    low_ref[...] = low[:, :768]
    high_ref[...] = low[:, 768:]
    terms_ref[...] = (grad_second * n2).astype(BF)
    attended_ref[...] = (dot(low[:, :768], mine_ref[...]) + dot(low[:, 768:], other_ref[...])).astype(BF)


def first_back_kernel(
    dquery_0, dquery_1, dquery_3, dquery_2, home_6, home_5, home_4, home_3, home_2, home_1, home_0, rest_a, rest_b,
    first_ref, second_terms, own_ref, one, three, two, tail_a, tail_b, sums,
):
    dquery = jnp.concatenate([dquery_0[...], dquery_1[...], dquery_3[...], dquery_2[...]], axis=0)
    sums[...] = sum(home[...].astype(F32) for home in (home_5, home_4, home_3, home_2, home_1, home_0))
    sums[128:, :] += home_6[...].astype(F32)
    dkeyval = sums[...].astype(BF)
    column = lax.broadcasted_iota(jnp.int32, (RING + ROW, 128), 1)
    row = lax.broadcasted_iota(jnp.int32, (RING + ROW, 128), 0)
    picks = jnp.where(column == (row >= RING).astype(jnp.int32), 1.0, 0.0).astype(BF)
    for cols, rest, tail in ((slice(0, 768), rest_a, tail_a), (slice(768, 1536), rest_b, tail_b)):
        first = first_ref[:, cols]
        grads = dot(dquery, rest[:, :384], NT)
        own = grads[:ROW] + dot(dkeyval, rest[:, 384:640], NT)
        own_ref[:, cols] = own
        for i, ref in ((1, one), (2, three), (3, two)):
            ref[:, cols] = grads[ROW * i : ROW * (i + 1)].astype(BF)
        grads = jnp.concatenate([own, grads[ROW:]], axis=0)
        terms = jnp.concatenate([(grads * first.astype(F32)).astype(BF), second_terms[:, cols]], axis=0)
        tail[:, :384] = dot(first, dquery, TN).astype(BF)
        tail[:, 384:640] = dot(first[:ROW], dkeyval, TN).astype(BF)
        tail[:, 640:] = dot(terms, picks, TN).astype(BF)


def input_kernel(core_ref, own_ref, one, three, two, token_ref, gain_ref, middle_ref, input_ref):
    grad_first = own_ref[...] + sum(part[...].astype(F32) for part in (one, three, two))
    _, n1, rs1 = normed(token_ref[...])
    total = middle_ref[...] + norm_back(grad_first, gain_ref[0:1, :], n1, rs1)
    input_ref[...] = true_order(total, core_ref[0]).astype(BF)


def block_kernel(core_ref, middle_ref, parts, out_ref):
    total = middle_ref[...] + sum(parts[i].astype(F32) for i in range(4))
    out_ref[...] = true_order(total, core_ref[0]).astype(BF)


def turn_xc(block, flip, cross, back=False):
    route = []
    for xh in range(2):
        for core in range(2):
            for head in range(2):
                target = (core ^ flip) * 4 + xh * 2 + (head ^ cross)
                source = xh * 4 + core * 2 + head
                route.append((target, source) if back else (source, target))
    return lax.ppermute(block, ("xh", "core", "head"), route)


def shift_all(block, distance):
    count = 128
    route = [(i, i + distance) for i in range(count) if 0 <= i + distance < count]
    return lax.ppermute(block, AXES, route)


def shift_groups(block, distance):
    return lax.ppermute(block, ("z", "xh", "y"), [(i, i + distance) for i in range(32 - distance)])


def shift_x(block, distance):
    return lax.ppermute(block, CHIPS_X, [(i, (i + distance) % 4) for i in range(4)])


def swap(block, axis):
    return lax.ppermute(block, axis, [(0, 1), (1, 0)])


def shards(tokens, cotangent, w_query, w_key, w_value, w_out, w_gate, w_up, w_down, gain_attn, gain_mlp):
    core = lax.axis_index("core")
    xh = lax.axis_index("xh")
    head = lax.axis_index("head")
    ring = 2 * xh + head
    place = jnp.stack([lax.axis_index(AXES), 2 * core + head]).astype(jnp.int32)
    ring_scalar, core_scalar, head_scalar = (i.astype(jnp.int32).reshape(1) for i in (ring, core, head))
    eight = ("xh", "core", "head")

    def ordered(index, first, second, axis):
        return jnp.concatenate(
            [jnp.where(index == 0, first, second), jnp.where(index == 0, second, first)], axis=axis
        )

    def spread(piece):
        sent = jnp.broadcast_to(piece[None], (16,) + piece.shape)
        return lax.all_to_all(sent, PLANE, 0, 0, tiled=True).reshape(768, -1)

    def gather(piece):
        return lax.all_gather(piece, PLANE, axis=0, tiled=True)

    gains = jnp.pad(jnp.stack([gain_attn, gain_mlp], axis=1), ((0, 0), (0, 126)))
    query_cut = w_query.reshape(12, 2, 2, 384).transpose(2, 1, 0, 3)
    common = jnp.broadcast_to(jnp.concatenate([w_key, w_value, gains], axis=1), (2, 2, 12, 384))
    own_qkv = jnp.concatenate([query_cut, common], axis=3)
    own_qkv = jnp.broadcast_to(own_qkv[:, None], (2, 2, 2, 12, 768)).reshape(8, 12, 768)
    got = lax.all_to_all(own_qkv, eight, 0, 0, tiled=True)
    qkv_piece = lax.dynamic_slice_in_dim(got, core * 4, 4, 0).reshape(48, 768)
    token_1, token_3, token_2 = (shift_x(tokens, k) for k in (1, 3, 2))
    qkv_mine = spread(qkv_piece)
    cot_own, cot_sent = call(
        order_kernel,
        "order",
        [((ROW, 1536), BF), ((4, ROW, 1536), BF)],
        [core_scalar, cotangent],
        scalars=1,
    )
    (cot_sent,) = after([cot_sent], qkv_mine)
    cots = lax.all_to_all(cot_sent, CHIPS_X, 0, 0, tiled=True).reshape(RING, 1536)
    (qkv_mine,) = after([qkv_mine], token_1, token_3, token_2)

    pair_cut = jnp.stack([w_gate, w_up], axis=1).reshape(24, 2, 2, FF_TILES, FF_TILE)
    pair_cut = pair_cut.transpose(2, 0, 3, 1, 4).reshape(2, 24, 2 * FF)
    down_cut = w_down.T.reshape(24, 2, FF).transpose(1, 0, 2)
    own_mlp = jnp.concatenate([pair_cut, down_cut], axis=2)
    sent_a = jnp.where(core == 0, own_mlp[0], own_mlp[1])
    sent_b = jnp.where(core == 0, own_mlp[1], own_mlp[0])
    out_low = w_out.T
    got_a = turn_xc(jnp.concatenate([out_low, sent_a], axis=1), False, False)
    got_b = turn_xc(jnp.concatenate([out_low, sent_b], axis=1), True, False)
    cross_a, cross_b = turn_xc(out_low, False, True), turn_xc(out_low, True, True)
    out_same = ordered(xh, got_a[:, :768], got_b[:, :768], 0).reshape(48, 2, 1, 384)
    out_cross = ordered(xh, cross_a, cross_b, 0).reshape(48, 2, 1, 384)
    out_piece = ordered(head, out_same, out_cross, 2).reshape(48, 1536)
    mlp_piece = ordered(xh, got_a[:, 768:], got_b[:, 768:], 0)
    (rest_piece,) = after([jnp.concatenate([out_piece, mlp_piece], axis=1)], qkv_piece)
    rest_mine = gather(rest_piece)

    qkv_other = swap(qkv_mine, "core")
    gain_rows, token_own, first_own, keyval_pair = call(
        keyval_kernel,
        "keyval",
        [((8, 1536), F32), ((ROW, 1536), BF), ((ROW, 1536), BF), ((2 * ROW, 256), BF)],
        [jnp.concatenate([head_scalar, core_scalar]), tokens, token_1, token_3, qkv_mine, qkv_other],
        scalars=1,
    )
    here, last = call(
        table_kernel,
        "table",
        [((768, 256), BF), ((256, 256), BF)],
        [core_scalar, keyval_pair, swap(keyval_pair, "core")],
        scalars=1,
    )
    near, far = shift_groups(here, 1), shift_groups(last, 2)
    first_all, query_0, ring_1, ring_3, ring_2 = call(
        query_kernel,
        "query",
        [((RING, 1536), BF)] + [((ROW, 384), BF)] * 4,
        [core_scalar, first_own, token_1, token_3, token_2, gain_rows, qkv_mine, qkv_other],
        scalars=1,
        needs=[here],
    )
    query_1, query_3, query_2 = shift_x(ring_1, -1), shift_x(ring_3, -3), shift_x(ring_2, -2)
    (queries,) = call(
        turn_kernel, "turn", [((ROW, 1536), BF)], [ring_scalar, query_0, query_1, query_2, query_3], scalars=1
    )
    (rest_mine,) = after([rest_mine], queries, near, far, cots)
    out_mine = rest_mine[:, :1536]
    attended, probs, keyval = attend(place, queries, far, near, here, [out_mine])

    out_other = swap(out_mine, "core")
    middle, second_own = call(
        middle_kernel,
        "middle",
        [((ROW, 1536), F32), ((ROW, 1536), BF)],
        [attended, out_mine, out_other, token_own, gain_rows],
    )
    blocks = [second_own] + [shift_x(second_own, k) for k in (1, 3, 2)]
    (rest_mine,) = after([rest_mine], attended, out_other)
    rest_other = swap(rest_mine, "core")

    hidden, dpair, seconds, seconds_b, second_part = mlp(
        ring_scalar, blocks, cots, rest_mine, rest_other, []
    )
    second_home = lax.all_to_all(second_part.reshape(4, ROW, 1536), CHIPS_X, 0, 0, tiled=True)

    def planes(total):
        got = lax.all_to_all(total.reshape(16, 48, -1), PLANE, 0, 0, tiled=True)
        return jnp.sum(got.astype(F32), axis=0).astype(BF)

    mlp_out = down_project(hidden, rest_mine, rest_other)
    (unit_total,) = unit_grad(
        [seconds, swap(seconds_b, "core"), cots, swap(cots[:, 768:], "core")]
        + [dpair, swap(dpair, "core"), hidden, swap(hidden, "core")],
        [mlp_out],
    )
    grad_middle, branch_a, branch_b, second_terms, grad_attended = call(
        middle_back_kernel,
        "middle_back",
        [((ROW, 1536), F32), ((ROW, 768), BF), ((ROW, 768), BF), ((ROW, 1536), BF), ((ROW, 1536), BF)],
        [second_home, middle, cot_own, gain_rows, out_mine, out_other],
        needs=[unit_total],
    )
    dqueries, *homes = attend_back(queries, keyval, attended, grad_attended, probs, [])

    dquery_0, dquery_1, dquery_2, dquery_3 = split(ring_scalar, dqueries)
    dquery_1, dquery_3, dquery_2 = (
        shift_x(block, k) for block, k in ((dquery_1, 1), (dquery_3, 3), (dquery_2, 2))
    )
    homes = [shift_all(home, -k) for home, k in zip(homes, (6, 5, 4, 3, 2, 1))] + [homes[6]]
    (mlp_out,) = after([mlp_out], second_home)
    mlp_home = lax.all_to_all(mlp_out.reshape(4, ROW, 1536), CHIPS_X, 0, 0, tiled=True)
    total = out_grad(branch_a, swap(branch_b, "core"), attended, swap(attended, "core"), unit_total)
    owned = lax.psum_scatter(total, PLANE, scatter_dimension=0, tiled=True)
    own_first, first_1, first_3, first_2, tail_mine, tail_other = call(
        first_back_kernel,
        "first_back",
        [((ROW, 1536), F32)] + [((ROW, 1536), BF)] * 3 + [((768, 768), BF)] * 2,
        [
            dquery_0, dquery_1, dquery_3, dquery_2, *homes, qkv_mine, qkv_other, first_all, second_terms,
        ],
        scratch=[pltpu.VMEM((ROW, 256), F32)],
    )
    tail_total = merge((tail_mine, swap(tail_other, "core")), needs=[mlp_home])
    tail_grads = planes(tail_total)
    first_1, first_3, first_2 = shift_x(first_1, -1), shift_x(first_3, -3), shift_x(first_2, -2)
    (input_grad,) = call(
        input_kernel,
        "input",
        [((ROW, 1536), BF)],
        [core_scalar, own_first, first_1, first_3, first_2, token_own, gain_rows, grad_middle],
        scalars=1,
    )
    (block_out,) = call(
        block_kernel, "block", [((ROW, 1536), BF)], [core_scalar, middle, mlp_home], scalars=1
    )
    tail_grads = tail_grads.reshape(4, 12, 768)
    tail_sent = jnp.where(jnp.arange(2).reshape(2, 1, 1, 1) == core, tail_grads[None], 0).reshape(8, 12, 768)
    tail_got = lax.all_to_all(tail_sent, eight, 0, 0, tiled=True)
    (owned,) = after([owned], first_1, first_3, first_2, tail_grads)
    out_grads = owned[:, 3 * FF :].reshape(48, 2, 2, 384)
    out_same = jnp.where(head == 0, out_grads[:, :, 0], out_grads[:, :, 1]).reshape(48, 768)
    out_cross = jnp.where(head == 0, out_grads[:, :, 1], out_grads[:, :, 0]).reshape(48, 768)
    same = jnp.concatenate([owned[:, : 3 * FF], out_same], axis=1)

    def chosen(rows, other):
        return jnp.where((xh == 0) != other, rows[:24], rows[24:])

    got_a, got_b = (turn_xc(chosen(same, flip), flip, False, True) for flip in (False, True))
    cross_a, cross_b = (turn_xc(chosen(out_cross, flip), flip, True, True) for flip in (False, True))
    low = jnp.where(core == 0, got_a, got_b).astype(F32)
    high = jnp.where(core == 0, got_b, got_a).astype(F32)

    (tail_got,) = after([tail_got], input_grad, block_out, got_a, got_b, cross_a, cross_b)
    tail_got = tail_got.reshape(2, 2, 2, 12, 768)
    tail_got = jnp.where(xh == 0, tail_got[:, 0], tail_got[:, 1])
    grad_w_query = tail_got[..., :384].astype(F32).transpose(2, 1, 0, 3).reshape(12, 1536)
    tail_sum = jnp.sum(tail_got[..., 384:].astype(F32), axis=(0, 1))

    def both(start, width):
        return jnp.concatenate([low[:, start : start + width], high[:, start : start + width]], axis=1)

    def pair_out(which):
        cut = jnp.stack([low[:, : 2 * FF], high[:, : 2 * FF]], axis=1).reshape(24, 2, FF_TILES, 2, FF_TILE)
        return cut[:, :, :, which].reshape(24, 2 * FF)

    return (
        block_out,
        input_grad,
        grad_w_query,
        tail_sum[:, :128],
        tail_sum[:, 128:256],
        (low[:, 3 * FF :] + high[:, 3 * FF :] + cross_a.astype(F32) + cross_b.astype(F32)).T,
        pair_out(0),
        pair_out(1),
        both(2 * FF, FF).T,
        tail_sum[:, 256] / gain_attn.astype(F32),
        tail_sum[:, 257],
    )


def solution(mesh):
    grid = Mesh(mesh.devices.reshape(SIZES), AXES)
    seq = ("z", "xh", "y", "core")
    rows, both, cols = P(AXES, None), P(seq, "head"), P("head", seq)
    in_specs = (rows, rows, rows, rows, rows, cols, both, both, cols, P(AXES), P(AXES))
    out_specs = (rows, rows, rows, rows, rows, cols, both, both, cols, P(AXES), P(AXES))
    return jax.shard_map(shards, mesh=grid, in_specs=in_specs, out_specs=out_specs, check_vma=False)
```

```python
import functools
import jax
import jax.numpy as jnp
from jax import lax
from jax.experimental import pallas as pl
from jax.experimental.pallas import tpu as pltpu
from jax.sharding import Mesh
from jax.sharding import PartitionSpec as P

WINDOW = 1024
EPSILON = 1e-06
AXES = ("z", "xh", "y", "core", "head")
SIZES = (4, 2, 4, 2, 2)
CHIPS_X = ("xh", "head")
PLANE = ("z", "y")
ROW = 192
KEYS = 1216
HEADS = 12
PAIRS = 2
HD = 128
BF = jnp.bfloat16
F32 = jnp.float32
NEG = -1e30
SCALE = HD ** (-0.5)
LOG2E = 1.4426950408889634
VMEM_BYTES = 56 * 1024 * 1024
FF = 1152
FF_TILES = 3
FF_TILE = 384
RING = 768
GELU_A = 0.7978845608028654
GELU_B = GELU_A * 0.044715

NN = (((1,), (0,)), ((), ()))
NT = (((1,), (1,)), ((), ()))
TN = (((0,), (0,)), ((), ()))


def dot(a, b, dims=NN):
    return lax.dot_general(a, b, dims, preferred_element_type=F32)


ANY = pl.BlockSpec(memory_space=pl.ANY)


def cost(micros):
    return pl.CostEstimate(flops=int(micros * 1.0e9), bytes_accessed=1000000, transcendentals=0)


def call(kernel, name, outs, args, needs=(), micros=0.01, grid=None, in_specs=None, out_specs=None, scratch=(), scalars=0):
    count = len(args)

    def body(*refs):
        kernel(*refs[:count], *refs[count + len(needs) :])

    if in_specs is None:
        whole = pl.BlockSpec(memory_space=pltpu.VMEM)
        in_specs = [pl.BlockSpec(memory_space=pltpu.SMEM)] * scalars + [whole] * (count - scalars)
        out_specs = [whole] * len(outs)
        spec = dict(in_specs=in_specs + [ANY] * len(needs), out_specs=out_specs, scratch_shapes=list(scratch))
    else:
        spec = dict(
            grid_spec=pltpu.PrefetchScalarGridSpec(
                num_scalar_prefetch=scalars,
                grid=grid,
                in_specs=in_specs + [ANY] * len(needs),
                out_specs=out_specs,
                scratch_shapes=list(scratch),
            )
        )
    return pl.pallas_call(
        body,
        out_shape=[jax.ShapeDtypeStruct(shape, kind) for shape, kind in outs],
        compiler_params=pltpu.CompilerParams(vmem_limit_bytes=VMEM_BYTES),
        cost_estimate=cost(micros),
        name=name,
        **spec,
    )(*args, *needs)


def after(values, *needs):
    count = len(values)
    return pl.pallas_call(
        lambda *refs: None,
        in_specs=[ANY] * (count + len(needs)),
        out_specs=[ANY] * count,
        out_shape=[jax.ShapeDtypeStruct(value.shape, value.dtype) for value in values],
        input_output_aliases={i: i for i in range(count)},
        cost_estimate=cost(0.01),
        name="after",
    )(*values, *needs)


def two_heads(pair):
    return jnp.concatenate([pair[:, :HD], pair[:, HD:]], axis=0)


def attend_kernel(place_ref, q_ref, far_ref, near_ref, here_ref, out_ref, probs_ref, kv_ref, bias, table):
    @pl.when(pl.program_id(0) == 0)
    def _():
        key = lax.broadcasted_iota(jnp.int32, (KEYS, ROW), 0)
        query = lax.broadcasted_iota(jnp.int32, (KEYS, ROW), 1)
        first = WINDOW - ROW * place_ref[0]
        inside = (key > query) & (key <= query + WINDOW) & (key >= first)
        one = jnp.where(inside, 0.0, NEG)
        bias[:, :] = jnp.concatenate([one, one], axis=1)
        table[:256, :] = far_ref[...]
        table[256:1024, :] = near_ref[...]
        table[1024:, :] = here_ref[...]
        kv_ref[...] = table[pl.ds(pl.multiple_of(place_ref[1] * ROW, ROW), KEYS), :]

    tables = [
        dot(kv_ref[:, :HD], two_heads(q_ref[:, 2 * HD * i : 2 * HD * (i + 1)]), NT) for i in range(PAIRS)
    ]
    for i, table in enumerate(tables):
        scores = table + bias[...]
        highest = jnp.max(scores, axis=0, keepdims=True)
        powers = jnp.exp2((scores - highest) * (SCALE * LOG2E))
        total = jnp.sum(powers, axis=0, keepdims=True)
        probs = (powers * (1.0 / total)).astype(BF)
        probs_ref[i] = probs
        mixed = dot(kv_ref[:, HD:], probs, TN).T.astype(BF)
        out_ref[:, 2 * HD * i : 2 * HD * (i + 1)] = jnp.concatenate([mixed[:ROW], mixed[ROW:]], axis=1)


def attend(place, queries, far, near, here, needs):
    pair = pl.BlockSpec((ROW, 2 * HD * PAIRS), lambda h, b: (0, h))

    def fixed(rows):
        return pl.BlockSpec((rows, 2 * HD), lambda h, b: (0, 0))

    return call(
        attend_kernel,
        "attend",
        [((ROW, HEADS * HD), BF), ((HEADS // 2, KEYS, 2 * ROW), BF), ((KEYS, 2 * HD), BF)],
        [place, queries, far, near, here],
        needs=needs,
        micros=10.0,
        grid=(HEADS // 2 // PAIRS,),
        in_specs=[pair, fixed(256), fixed(768), fixed(768)],
        out_specs=[pair, pl.BlockSpec((PAIRS, KEYS, 2 * ROW), lambda h, b: (h, 0, 0)), fixed(KEYS)],
        scratch=[pltpu.VMEM((KEYS, 2 * ROW), F32), pltpu.VMEM((1792, 2 * HD), BF)],
        scalars=1,
    )


HOME_ROWS = [slice(0, 64)] + [slice(64 + ROW * i, 64 + ROW * (i + 1)) for i in range(6)]


def attend_back_kernel(q_ref, kv_ref, out_ref, grad_ref, probs_ref, dq_ref, *rest):
    homes, (dk, dv) = rest[:7], rest[7:]
    step = pl.program_id(0)

    @pl.when(step == 0)
    def _():
        dk[...] = jnp.zeros_like(dk)
        dv[...] = jnp.zeros_like(dv)

    pairs = [slice(2 * HD * i, 2 * HD * (i + 1)) for i in range(PAIRS)]
    tables = [dot(kv_ref[:, HD:], two_heads(grad_ref[:, pair]), NT) for pair in pairs]
    for i, (pair, dprobs) in enumerate(zip(pairs, tables)):
        queries = two_heads(q_ref[:, pair])
        grads = two_heads(grad_ref[:, pair])
        outs = two_heads(out_ref[:, pair])
        probs = probs_ref[i]
        delta = jnp.sum((grads.astype(F32) * outs.astype(F32)).T, axis=0, keepdims=True)
        dscores = (probs.astype(F32) * (dprobs - delta)).astype(BF)
        dqueries = (dot(kv_ref[:, :HD], dscores, TN).T * SCALE).astype(BF)
        dq_ref[:, pair] = jnp.concatenate([dqueries[:ROW], dqueries[ROW:]], axis=1)
        dk[...] += dot(dscores, queries)
        dv[...] += dot(probs, grads)

    @pl.when(step == HEADS // 2 // PAIRS - 1)
    def _():
        for home, rows in zip(homes, HOME_ROWS):
            home[:, :HD] = (dk[rows, :] * SCALE).astype(BF)
            home[:, HD:] = dv[rows, :].astype(BF)


def attend_back(queries, keyval, attended, grads, probs, needs):
    pair = pl.BlockSpec((ROW, 2 * HD * PAIRS), lambda h: (0, h))
    table = pl.BlockSpec((KEYS, 2 * HD), lambda h: (0, 0))

    def home(rows):
        return pl.BlockSpec((rows, 2 * HD), lambda h: (0, 0))

    return call(
        attend_back_kernel,
        "attend_back",
        [((ROW, HEADS * HD), BF), ((64, 2 * HD), BF)] + [((ROW, 2 * HD), BF)] * 6,
        [queries, keyval, attended, grads, probs],
        needs=needs,
        micros=0.01,
        grid=(HEADS // 2 // PAIRS,),
        in_specs=[pair, table, pair, pair, pl.BlockSpec((PAIRS, KEYS, 2 * ROW), lambda h: (h, 0, 0))],
        out_specs=[pair, home(64)] + [home(ROW)] * 6,
        scratch=[pltpu.VMEM((KEYS, HD), F32), pltpu.VMEM((KEYS, HD), F32)],
    )


def down_back_kernel(cots, down_a, down_b, out_ref):
    out_ref[...] = dot(cots[:, :768], down_a[...]) + dot(cots[:, 768:], down_b[...])


def down_back(cots, rest_mine, rest_other):
    down = pl.BlockSpec((768, FF_TILE), lambda f: (0, 10 + f))
    return call(
        down_back_kernel,
        "down_back",
        [((RING, FF), F32)],
        [cots, rest_mine, rest_other],
        micros=6.0,
        grid=(FF_TILES,),
        in_specs=[pl.BlockSpec((RING, 1536), lambda f: (0, 0)), down, down],
        out_specs=[pl.BlockSpec((RING, FF_TILE), lambda f: (0, f))],
    )[0]


def ring_rows(ring, back):
    return pl.ds(pl.multiple_of(lax.rem(ring + 4 - back, 4) * ROW, ROW), ROW)


BACKS = (0, 1, 3, 2)


def mlp_kernel(
    ring_ref, zero, one, three, two, dhidden_ref, pair_a, pair_b, hidden_ref, dpair_ref, rows, rows_b, second_ref,
    second_sum
):
    @pl.when(pl.program_id(0) == 0)
    def _():
        for block, back in zip((zero, one, three, two), BACKS):
            rows[ring_rows(ring_ref[0], back), :] = block[...]
            rows_b[ring_rows(ring_ref[0], back), :] = block[:, 768:]

    step = pl.program_id(0)
    low, high = slice(0, 768), slice(768, 1536)
    both = dot(rows[:, low], pair_a[...]) + dot(rows[:, high], pair_b[...])
    gate, up = both[:, :FF_TILE], both[:, FF_TILE:]
    dhidden = dhidden_ref[...]
    square = gate * gate
    wave = jnp.tanh(gate * (GELU_A + GELU_B * square))
    half = 0.5 + 0.5 * wave
    gelu = gate * half
    slope = half + gate * (0.5 - 0.5 * wave * wave) * (GELU_A + 3.0 * GELU_B * square)
    hidden_ref[...] = (gelu * up).astype(BF)
    dpair = jnp.concatenate([(dhidden * up * slope).astype(BF), (dhidden * gelu).astype(BF)], axis=1)
    dpair_ref[...] = dpair
    part_a = dot(dpair, pair_a[...], NT)
    part_b = dot(dpair, pair_b[...], NT)

    @pl.when(step == 0)
    def _():
        second_sum[:, low] = part_a
        second_sum[:, high] = part_b

    @pl.when((step > 0) & (step < FF_TILES - 1))
    def _():
        second_sum[:, low] += part_a
        second_sum[:, high] += part_b

    @pl.when(step == FF_TILES - 1)
    def _():
        second_ref[:, low] = (second_sum[:, low] + part_a).astype(BF)
        second_ref[:, high] = (second_sum[:, high] + part_b).astype(BF)


def mlp(ring, blocks, dhidden, rest_mine, rest_other):
    whole = pl.BlockSpec((ROW, 1536), lambda f, r: (0, 0))
    table = pl.BlockSpec((RING, 1536), lambda f, r: (0, 0))
    half = pl.BlockSpec((RING, 768), lambda f, r: (0, 0))
    unit = pl.BlockSpec((RING, FF_TILE), lambda f, r: (0, f))
    pair_unit = pl.BlockSpec((RING, 2 * FF_TILE), lambda f, r: (0, f))
    pair = pl.BlockSpec((768, 2 * FF_TILE), lambda f, r: (0, 2 + f))
    return call(
        mlp_kernel,
        "mlp",
        [((RING, FF), BF), ((RING, 2 * FF), BF), ((RING, 1536), BF), ((RING, 768), BF), ((RING, 1536), BF)],
        [ring, *blocks, dhidden, rest_mine, rest_other],
        micros=20.0,
        grid=(FF_TILES,),
        in_specs=[whole] * 4 + [unit, pair, pair],
        out_specs=[unit, pair_unit, table, half, table],
        scratch=[pltpu.VMEM((RING, 1536), F32)],
        scalars=1,
    )


def down_project_kernel(hidden_ref, down_a, down_b, out_ref):
    out_ref[:, :768] = dot(hidden_ref[...], down_a[...], NT).astype(BF)
    out_ref[:, 768:] = dot(hidden_ref[...], down_b[...], NT).astype(BF)


def down_project(hidden, rest_mine, rest_other):
    down = pl.BlockSpec((pl.Element(768), pl.Element(FF)), lambda f: (0, 1536 + 2 * FF))
    table = pl.BlockSpec((RING, 1536), lambda f: (0, 0))
    return call(
        down_project_kernel,
        "down_project",
        [((RING, 1536), BF)],
        [hidden, rest_mine, rest_other],
        grid=(1,),
        in_specs=[pl.BlockSpec((RING, FF), lambda f: (0, 0)), down, down],
        out_specs=[table],
    )[0]


def out_grad_kernel(left, left_b, right, right_b, out_ref):
    lefts = jnp.concatenate([left[...], left_b[...]], axis=0)
    rights = jnp.concatenate([right[...], right_b[...]], axis=0)
    out_ref[...] = dot(lefts, rights, TN).astype(BF)


def out_grad(left, left_b, right, right_b, total):
    lefts = pl.BlockSpec((ROW, 768), lambda i: (0, 0))
    rights = pl.BlockSpec((ROW, 384), lambda i: (0, i))
    return pl.pallas_call(
        lambda *refs: out_grad_kernel(*refs[:4], refs[5]),
        grid=(4,),
        in_specs=[lefts, lefts, rights, rights, ANY],
        out_specs=pl.BlockSpec((768, 384), lambda i: (0, 3 * FF // 384 + i)),
        out_shape=jax.ShapeDtypeStruct(total.shape, BF),
        input_output_aliases={4: 0},
        compiler_params=pltpu.CompilerParams(vmem_limit_bytes=VMEM_BYTES),
        cost_estimate=cost(0.01),
        name="out_grad",
    )(left, left_b, right, right_b, total)


def unit_grad_kernel(left, left_b, cot, cot_b, dpair, dpair_b, hidden, hidden_b, out_ref):
    pair = dot(left[...], dpair[...], TN) + dot(left_b[...], dpair_b[...], TN)
    down = dot(cot[...], hidden[...], TN) + dot(cot_b[...], hidden_b[...], TN)
    out_ref[:, : 2 * FF] = pair.astype(BF)
    out_ref[:, 2 * FF :] = down.astype(BF)


def unit_grad(args, needs):
    tile = 256
    left = pl.BlockSpec((RING, tile), lambda i: (0, i))
    return call(
        unit_grad_kernel,
        "unit_grad",
        [((768, 3 * FF + 1536), BF)],
        args,
        needs=needs,
        micros=6.0,
        grid=(768 // tile,),
        in_specs=[left] * 4 + [pl.BlockSpec(a.shape, lambda i: (0, 0)) for a in args[4:]],
        out_specs=[pl.BlockSpec((tile, 3 * FF), lambda i: (i, 0))],
    )


def merge_kernel(*refs):
    out_ref = refs[-1]
    start = 0
    for mine, other in zip(refs[:-1:2], refs[1:-1:2]):
        width = mine.shape[1]
        out_ref[:, start : start + width] = (mine[...].astype(F32) + other[...].astype(F32)).astype(BF)
        start += width


def merge(*pairs, needs=()):
    width = sum(mine.shape[1] for mine, _ in pairs)
    return call(merge_kernel, "merge", [((768, width), BF)], [array for pair in pairs for array in pair], needs)[0]


def normed(rows):
    values = rows.astype(F32)
    inverse = lax.rsqrt(jnp.mean(values * values, axis=-1, keepdims=True) + EPSILON)
    return values, values * inverse, inverse


def norm_back(grad, gain, n, inverse):
    scaled = grad * gain
    return inverse * (scaled - n * jnp.mean(scaled * n, axis=-1, keepdims=True))


def keyval_kernel(ids, own, one, three, mine_ref, other_ref, gain_ref, token_ref, first_ref, keyval_ref):
    head, core = ids[0], ids[1]
    gain_ref[:, :768] = mine_ref[:, 640:].astype(F32).T[:8]
    gain_ref[:, 768:] = other_ref[:, 640:].astype(F32).T[:8]

    def local(block):
        return local_order(block[...].astype(F32), core)

    def project(block):
        first = (normed(block)[1] * gain_ref[0:1, :]).astype(BF)
        total = dot(first[:, :768], mine_ref[:, 384:640]) + dot(first[:, 768:], other_ref[:, 384:640])
        return first, total.astype(BF)

    token = local(own)
    token_ref[...] = token.astype(BF)
    first, total = project(token)
    first_ref[...] = first

    @pl.when(head == 0)
    def _():
        keyval_ref[:ROW, :] = total
        keyval_ref[ROW:, :] = project(local(three))[1]

    @pl.when(head == 1)
    def _():
        keyval_ref[:ROW, :] = project(local(one))[1]
        keyval_ref[ROW:, :] = total


def local_order(rows, core):
    low = jnp.concatenate([rows[:, 384 * z : 384 * z + 192] for z in range(4)], axis=1)
    high = jnp.concatenate([rows[:, 384 * z + 192 : 384 * z + 384] for z in range(4)], axis=1)
    return jnp.concatenate([jnp.where(core == 0, low, high), jnp.where(core == 0, high, low)], axis=1)


def true_order(rows, core):
    low = jnp.where(core == 0, rows[:, :768], rows[:, 768:])
    high = jnp.where(core == 0, rows[:, 768:], rows[:, :768])
    cuts = [half[:, 192 * z : 192 * (z + 1)] for z in range(4) for half in (low, high)]
    return jnp.concatenate(cuts, axis=1)


def order_kernel(core_ref, rows_ref, out_ref, copies):
    rows = local_order(rows_ref[...].astype(F32), core_ref[0]).astype(BF)
    out_ref[...] = rows
    for i in range(4):
        copies[i] = rows


def table_kernel(core_ref, mine_ref, other_ref, table_ref, last_ref):
    @pl.when(core_ref[0] == 0)
    def _():
        table_ref[: 2 * ROW, :] = mine_ref[...]
        table_ref[2 * ROW :, :] = other_ref[...]

    @pl.when(core_ref[0] == 1)
    def _():
        table_ref[: 2 * ROW, :] = other_ref[...]
        table_ref[2 * ROW :, :] = mine_ref[...]

    last_ref[...] = table_ref[512:, :]


def ring_cols(ring, ahead):
    return pl.ds(pl.multiple_of(lax.rem(ring + ahead, 4) * 384, 384), 384)


def turn_kernel(ring_ref, zero, one, two, three, out_ref):
    for ahead, block in enumerate((zero, one, two, three)):
        out_ref[:, ring_cols(ring_ref[0], ahead)] = block[...]


def cut_kernel(rows_ref, out_ref):
    for i in range(4):
        out_ref[i] = rows_ref[:, 384 * i : 384 * (i + 1)]


def query_kernel(ids, first_ref, one, three, two, gain_ref, mine_ref, other_ref, all_ref, *outs_total):
    outs, total = outs_total[:4], outs_total[4]
    core, ring = ids[0], ids[1]
    all_ref[ring_rows(ring, 0), :] = first_ref[...]
    for back, block in ((1, one), (3, three), (2, two)):
        first = normed(local_order(block[...].astype(F32), core))[1] * gain_ref[0:1, :]
        all_ref[ring_rows(ring, back), :] = first.astype(BF)
    rows = all_ref[...]
    total[...] = (dot(rows[:, :768], mine_ref[:, :384]) + dot(rows[:, 768:], other_ref[:, :384])).astype(BF)
    for out, back in zip(outs, BACKS):
        out[...] = total[ring_rows(ring, back), :]


def middle_kernel(attended_ref, mine_ref, other_ref, token_ref, gain_ref, middle_ref, second_ref):
    attended = attended_ref[...]
    branch = jnp.concatenate([dot(attended, mine_ref[...], NT), dot(attended, other_ref[...], NT)], axis=1)
    middle = token_ref[...].astype(F32) + branch
    middle_ref[...] = middle
    second_ref[...] = (normed(middle)[1] * gain_ref[1:2, :]).astype(BF)


def middle_back_kernel(
    parts, middle_ref, cot_ref, gain_ref, mine_ref, other_ref, grad_ref, low_ref, high_ref, terms_ref, attended_ref
):
    grad_second = sum(parts[i].astype(F32) for i in range(4))
    _, n2, rs2 = normed(middle_ref[...])
    grad_middle = cot_ref[...].astype(F32) + norm_back(grad_second, gain_ref[1:2, :], n2, rs2)
    grad_ref[...] = grad_middle
    low = grad_middle.astype(BF)
    low_ref[...] = low[:, :768]
    high_ref[...] = low[:, 768:]
    terms_ref[...] = (grad_second * n2).astype(BF)
    attended_ref[...] = (dot(low[:, :768], mine_ref[...]) + dot(low[:, 768:], other_ref[...])).astype(BF)


def first_back_kernel(
    ring_ref, dqueries, home_6, home_5, home_4, home_3, home_2, home_1, home_0, rest_a, rest_b, first_ref,
    second_terms, own_ref, one, three, two, tail_a, tail_b, sums, partial,
):
    ring = ring_ref[0]
    dquery = jnp.concatenate([dqueries[i] for i in range(4)], axis=0)
    sums[...] = sum(home[...].astype(F32) for home in (home_5, home_4, home_3, home_2, home_1, home_0))
    sums[128:, :] += home_6[...].astype(F32)
    dkeyval = sums[...].astype(BF)
    column = lax.broadcasted_iota(jnp.int32, (RING + ROW, 128), 1)
    row = lax.broadcasted_iota(jnp.int32, (RING + ROW, 128), 0)
    picks = jnp.where(column == (row >= RING).astype(jnp.int32), 1.0, 0.0).astype(BF)
    own_rows = ring_rows(ring, 0)
    for cols, rest, tail in ((slice(0, 768), rest_a, tail_a), (slice(768, 1536), rest_b, tail_b)):
        partial[...] = dot(dquery, rest[:, :384], NT)
        partial[own_rows, :] += dot(dkeyval, rest[:, 384:640], NT)
        own_ref[:, cols] = partial[own_rows, :]
        for back, ref in ((1, one), (3, three), (2, two)):
            ref[:, cols] = partial[ring_rows(ring, back), :].astype(BF)
        first = first_ref[:, cols]
        terms = jnp.concatenate([(partial[...] * first.astype(F32)).astype(BF), second_terms[:, cols]], axis=0)
        tail[:, :384] = dot(first, dquery, TN).astype(BF)
        tail[:, 384:640] = dot(first_ref[own_rows, cols], dkeyval, TN).astype(BF)
        tail[:, 640:] = dot(terms, picks, TN).astype(BF)


def input_kernel(core_ref, own_ref, one, three, two, token_ref, gain_ref, middle_ref, input_ref):
    grad_first = own_ref[...] + sum(part[...].astype(F32) for part in (one, three, two))
    _, n1, rs1 = normed(token_ref[...])
    total = middle_ref[...] + norm_back(grad_first, gain_ref[0:1, :], n1, rs1)
    input_ref[...] = true_order(total, core_ref[0]).astype(BF)


def block_kernel(core_ref, middle_ref, parts, out_ref):
    total = middle_ref[...] + sum(parts[i].astype(F32) for i in range(4))
    out_ref[...] = true_order(total, core_ref[0]).astype(BF)


def tail_kernel(core_ref, parts, out_ref):
    total = sum(parts[i].astype(F32) for i in range(16))
    out_ref[...] = jnp.zeros_like(out_ref)
    for xh in range(2):
        keep = jnp.where(core_ref[0] == xh, 1.0, 0.0)
        for i in range(4):
            out_ref[4 * xh + i, :12, :768] = (total[12 * i : 12 * (i + 1)] * keep).astype(BF)


def deal_kernel(ids, owned_ref, give_a, give_b, cross_a, cross_b):
    head, xh = ids[0], ids[1]
    start = 3 * FF

    def rows(cols, flip):
        block = owned_ref[:, cols].astype(F32)
        return jnp.where((xh == 0) != flip, block[:24], block[24:]).astype(BF)

    def part(chip):
        return pl.ds(pl.multiple_of(start + 384 * chip, 384), 384)

    for flip, give, cross in ((False, give_a, cross_a), (True, give_b, cross_b)):
        give[:, :start] = rows(slice(0, start), flip)
        for i in range(2):
            give[:, start + 384 * i : start + 384 * (i + 1)] = rows(part(2 * i + head), flip)
            cross[:, 384 * i : 384 * (i + 1)] = rows(part(2 * i + 1 - head), flip)


def final_kernel(ids, tail, got_a, got_b, cross_a, cross_b, query_ref, key_ref, value_ref, gain_ref, out_ref, gate_ref,
                 up_ref, down_ref):
    core, xh = ids[0], ids[1]
    total = jnp.zeros((12, 384), F32)
    for xh_from in range(2):
        for head in range(2):
            block = tail[4 * xh_from + 2 * xh + head].astype(F32)[:12]
            quarter = 2 * head + xh_from
            query_ref[:, 384 * quarter : 384 * (quarter + 1)] = block[:, :384]
            total = total + block[:, 384:768]
    key_ref[...] = total[:, :HD]
    value_ref[...] = total[:, HD : 2 * HD]
    gain_ref[...] = total[:, 2 * HD :]
    first, second = got_a[...].astype(F32), got_b[...].astype(F32)
    halves = (jnp.where(core == 0, first, second), jnp.where(core == 0, second, first))
    for i, half in enumerate(halves):
        for f in range(FF_TILES):
            place = slice(FF * i + FF_TILE * f, FF * i + FF_TILE * (f + 1))
            gate_ref[:, place] = half[:, 2 * FF_TILE * f : 2 * FF_TILE * f + FF_TILE]
            up_ref[:, place] = half[:, 2 * FF_TILE * f + FF_TILE : 2 * FF_TILE * (f + 1)]
        down_ref[:, FF * i : FF * (i + 1)] = half[:, 2 * FF : 3 * FF]
    out_ref[...] = (
        halves[0][:, 3 * FF :] + halves[1][:, 3 * FF :] + cross_a[...].astype(F32) + cross_b[...].astype(F32)
    )


def turn_xc(block, flip, cross, back=False):
    route = []
    for xh in range(2):
        for core in range(2):
            for head in range(2):
                target = (core ^ flip) * 4 + xh * 2 + (head ^ cross)
                source = xh * 4 + core * 2 + head
                route.append((target, source) if back else (source, target))
    return lax.ppermute(block, ("xh", "core", "head"), route)


def shift_all(block, distance):
    count = 128
    route = [(i, i + distance) for i in range(count) if 0 <= i + distance < count]
    return lax.ppermute(block, AXES, route)


def shift_groups(block, distance):
    return lax.ppermute(block, ("z", "xh", "y"), [(i, i + distance) for i in range(32 - distance)])


def shift_x(block, distance):
    return lax.ppermute(block, CHIPS_X, [(i, (i + distance) % 4) for i in range(4)])


def swap(block, axis):
    return lax.ppermute(block, axis, [(0, 1), (1, 0)])


def shards(tokens, cotangent, w_query, w_key, w_value, w_out, w_gate, w_up, w_down, gain_attn, gain_mlp):
    core = lax.axis_index("core")
    xh = lax.axis_index("xh")
    head = lax.axis_index("head")
    ring = 2 * xh + head
    place = jnp.stack([lax.axis_index(AXES), 2 * core + head]).astype(jnp.int32)
    ring_scalar, core_scalar, head_scalar = (i.astype(jnp.int32).reshape(1) for i in (ring, core, head))
    eight = ("xh", "core", "head")

    def ordered(index, first, second, axis):
        return jnp.concatenate(
            [jnp.where(index == 0, first, second), jnp.where(index == 0, second, first)], axis=axis
        )

    def spread(piece):
        sent = jnp.broadcast_to(piece[None], (16,) + piece.shape)
        return lax.all_to_all(sent, PLANE, 0, 0, tiled=True).reshape(768, -1)

    def gather(piece):
        return lax.all_gather(piece, PLANE, axis=0, tiled=True)

    gains = jnp.pad(jnp.stack([gain_attn, gain_mlp], axis=1), ((0, 0), (0, 126)))
    query_cut = w_query.reshape(12, 2, 2, 384).transpose(2, 1, 0, 3)
    common = jnp.broadcast_to(jnp.concatenate([w_key, w_value, gains], axis=1), (2, 2, 12, 384))
    own_qkv = jnp.concatenate([query_cut, common], axis=3)
    own_qkv = jnp.broadcast_to(own_qkv[:, None], (2, 2, 2, 12, 768)).reshape(8, 12, 768)
    got = lax.all_to_all(own_qkv, eight, 0, 0, tiled=True)
    qkv_piece = lax.dynamic_slice_in_dim(got, core * 4, 4, 0).reshape(48, 768)
    token_1, token_3, token_2 = (shift_x(tokens, k) for k in (1, 3, 2))
    qkv_mine = spread(qkv_piece)
    cot_own, cot_sent = call(
        order_kernel,
        "order",
        [((ROW, 1536), BF), ((4, ROW, 1536), BF)],
        [core_scalar, cotangent],
        scalars=1,
    )
    (cot_sent,) = after([cot_sent], qkv_mine)
    cots = lax.all_to_all(cot_sent, CHIPS_X, 0, 0, tiled=True).reshape(RING, 1536)
    (qkv_mine,) = after([qkv_mine], token_1, token_3, token_2)

    pair_cut = jnp.stack([w_gate, w_up], axis=1).reshape(24, 2, 2, FF_TILES, FF_TILE)
    pair_cut = pair_cut.transpose(2, 0, 3, 1, 4).reshape(2, 24, 2 * FF)
    down_cut = w_down.T.reshape(24, 2, FF).transpose(1, 0, 2)
    own_mlp = jnp.concatenate([pair_cut, down_cut], axis=2)
    sent_a = jnp.where(core == 0, own_mlp[0], own_mlp[1])
    sent_b = jnp.where(core == 0, own_mlp[1], own_mlp[0])
    out_low = w_out.T
    got_a = turn_xc(jnp.concatenate([out_low, sent_a], axis=1), False, False)
    got_b = turn_xc(jnp.concatenate([out_low, sent_b], axis=1), True, False)
    cross_a, cross_b = turn_xc(out_low, False, True), turn_xc(out_low, True, True)
    out_same = ordered(xh, got_a[:, :768], got_b[:, :768], 0).reshape(48, 2, 1, 384)
    out_cross = ordered(xh, cross_a, cross_b, 0).reshape(48, 2, 1, 384)
    out_piece = ordered(head, out_same, out_cross, 2).reshape(48, 1536)
    mlp_piece = ordered(xh, got_a[:, 768:], got_b[:, 768:], 0)
    (rest_piece,) = after([jnp.concatenate([out_piece, mlp_piece], axis=1)], qkv_piece)
    rest_mine = gather(rest_piece)

    qkv_other = swap(qkv_mine, "core")
    gain_rows, token_own, first_own, keyval_pair = call(
        keyval_kernel,
        "keyval",
        [((8, 1536), F32), ((ROW, 1536), BF), ((ROW, 1536), BF), ((2 * ROW, 256), BF)],
        [jnp.concatenate([head_scalar, core_scalar]), tokens, token_1, token_3, qkv_mine, qkv_other],
        scalars=1,
    )
    here, last = call(
        table_kernel,
        "table",
        [((768, 256), BF), ((256, 256), BF)],
        [core_scalar, keyval_pair, swap(keyval_pair, "core")],
        scalars=1,
    )
    near, far = shift_groups(here, 1), shift_groups(last, 2)
    first_all, query_0, ring_1, ring_3, ring_2 = call(
        query_kernel,
        "query",
        [((RING, 1536), BF)] + [((ROW, 384), BF)] * 4,
        [jnp.concatenate([core_scalar, ring_scalar]), first_own, token_1, token_3, token_2, gain_rows, qkv_mine, qkv_other],
        scratch=[pltpu.VMEM((RING, 384), BF)],
        scalars=1,
        needs=[here],
    )
    query_1, query_3, query_2 = shift_x(ring_1, -1), shift_x(ring_3, -3), shift_x(ring_2, -2)
    (queries,) = call(
        turn_kernel, "turn", [((ROW, 1536), BF)], [ring_scalar, query_0, query_1, query_2, query_3], scalars=1
    )
    (rest_mine,) = after([rest_mine], queries, near, far, cots)
    out_mine = rest_mine[:, :1536]
    attended, probs, keyval = attend(place, queries, far, near, here, [out_mine])

    out_other = swap(out_mine, "core")
    middle, second_own = call(
        middle_kernel,
        "middle",
        [((ROW, 1536), F32), ((ROW, 1536), BF)],
        [attended, out_mine, out_other, token_own, gain_rows],
    )
    blocks = [second_own] + [shift_x(second_own, k) for k in (1, 3, 2)]
    (rest_mine,) = after([rest_mine], attended, out_other)
    rest_other = swap(rest_mine, "core")
    dhidden = down_back(cots, rest_mine, rest_other)

    hidden, dpair, seconds, seconds_b, second_part = mlp(ring_scalar, blocks, dhidden, rest_mine, rest_other)
    second_home = lax.all_to_all(second_part.reshape(4, ROW, 1536), CHIPS_X, 0, 0, tiled=True)

    def planes(total):
        got = lax.all_to_all(total.reshape(16, 48, -1), PLANE, 0, 0, tiled=True)
        return jnp.sum(got.astype(F32), axis=0).astype(BF)

    mlp_out = down_project(hidden, rest_mine, rest_other)
    (unit_total,) = unit_grad(
        [seconds, swap(seconds_b, "core"), cots, swap(cots[:, 768:], "core")]
        + [dpair, swap(dpair, "core"), hidden, swap(hidden, "core")],
        [mlp_out],
    )
    grad_middle, branch_a, branch_b, second_terms, grad_attended = call(
        middle_back_kernel,
        "middle_back",
        [((ROW, 1536), F32), ((ROW, 768), BF), ((ROW, 768), BF), ((ROW, 1536), BF), ((ROW, 1536), BF)],
        [second_home, middle, cot_own, gain_rows, out_mine, out_other],
        needs=[unit_total],
    )
    dqueries, *homes = attend_back(queries, keyval, attended, grad_attended, probs, [])

    (mlp_out,) = after([mlp_out], second_home)
    mlp_home = lax.all_to_all(mlp_out.reshape(4, ROW, 1536), CHIPS_X, 0, 0, tiled=True)
    homes = [shift_all(home, -k) for home, k in zip(homes, (6, 5, 4, 3, 2, 1))] + [homes[6]]
    (dquery_cut,) = call(cut_kernel, "cut", [((4, ROW, 384), BF)], [dqueries], needs=[mlp_home, *homes[:4]])
    dquery_ring = lax.all_to_all(dquery_cut, CHIPS_X, 0, 0, tiled=True)
    total = out_grad(branch_a, swap(branch_b, "core"), attended, swap(attended, "core"), unit_total)
    owned = lax.psum_scatter(total, PLANE, scatter_dimension=0, tiled=True)
    own_first, first_1, first_3, first_2, tail_mine, tail_other = call(
        first_back_kernel,
        "first_back",
        [((ROW, 1536), F32)] + [((ROW, 1536), BF)] * 3 + [((768, 768), BF)] * 2,
        [
            ring_scalar, dquery_ring, *homes, qkv_mine, qkv_other, first_all, second_terms,
        ],
        scratch=[pltpu.VMEM((ROW, 256), F32), pltpu.VMEM((RING, 768), F32)],
        scalars=1,
    )
    tail_total = merge((tail_mine, swap(tail_other, "core")))
    tail_parts = lax.all_to_all(tail_total.reshape(16, 48, 768), PLANE, 0, 0, tiled=True)
    (block_out,) = call(
        block_kernel, "block", [((ROW, 1536), BF)], [core_scalar, middle, mlp_home], scalars=1
    )
    (tail_sent,) = call(
        tail_kernel, "tail", [((8, 16, 1024), BF)], [core_scalar, tail_parts], needs=[block_out], scalars=1
    )
    first_1, first_3, first_2 = shift_x(first_1, -1), shift_x(first_3, -3), shift_x(first_2, -2)
    (input_grad,) = call(
        input_kernel,
        "input",
        [((ROW, 1536), BF)],
        [core_scalar, own_first, first_1, first_3, first_2, token_own, gain_rows, grad_middle],
        scalars=1,
    )
    tail_got = lax.all_to_all(tail_sent, eight, 0, 0, tiled=True)
    give_a, give_b, cross_a, cross_b = call(
        deal_kernel,
        "deal",
        [((24, 3 * FF + 768), BF)] * 2 + [((24, 768), BF)] * 2,
        [jnp.concatenate([head_scalar, xh.astype(jnp.int32).reshape(1)]), owned],
        needs=[first_1, first_3, first_2, tail_sent],
        scalars=1,
    )
    got_a, got_b = turn_xc(give_a, False, False, True), turn_xc(give_b, True, False, True)
    cross_a, cross_b = turn_xc(cross_a, False, True, True), turn_xc(cross_b, True, True, True)
    query_grad, key_grad, value_grad, gain_grads, out_grad_own, gate_grad, up_grad, down_grad = call(
        final_kernel,
        "final",
        [((12, 1536), F32)] + [((12, 128), F32)] * 3 + [((24, 768), F32)] + [((24, 2 * FF), F32)] * 3,
        [jnp.concatenate([core_scalar, xh.astype(jnp.int32).reshape(1)]), tail_got, got_a, got_b, cross_a, cross_b],
        needs=[input_grad, block_out],
        scalars=1,
    )
    return (
        block_out,
        input_grad,
        query_grad,
        key_grad,
        value_grad,
        out_grad_own.T,
        gate_grad,
        up_grad,
        down_grad.T,
        gain_grads[:, 0] / gain_attn.astype(F32),
        gain_grads[:, 1],
    )


def solution(mesh):
    grid = Mesh(mesh.devices.reshape(SIZES), AXES)
    seq = ("z", "xh", "y", "core")
    rows, both, cols = P(AXES, None), P(seq, "head"), P("head", seq)
    in_specs = (rows, rows, rows, rows, rows, cols, both, both, cols, P(AXES), P(AXES))
    out_specs = (rows, rows, rows, rows, rows, cols, both, both, cols, P(AXES), P(AXES))
    return jax.shard_map(shards, mesh=grid, in_specs=in_specs, out_specs=out_specs, check_vma=False)
```

```python
import functools
import jax
import jax.numpy as jnp
from jax import lax
from jax.experimental import pallas as pl
from jax.experimental.pallas import tpu as pltpu
from jax.sharding import Mesh
from jax.sharding import PartitionSpec as P

WINDOW = 1024
EPSILON = 1e-06
AXES = ("z", "xh", "y", "core", "head")
SIZES = (4, 2, 4, 2, 2)
CHIPS_X = ("xh", "head")
PLANE = ("z", "y")
ROW = 192
KEYS = 1216
HEADS = 12
PAIRS = 2
HD = 128
BF = jnp.bfloat16
F32 = jnp.float32
NEG = -1e30
SCALE = HD ** (-0.5)
LOG2E = 1.4426950408889634
VMEM_BYTES = 56 * 1024 * 1024
FF = 1152
FF_TILES = 3
FF_TILE = 384
RING = 768
GELU_A = 0.7978845608028654
GELU_B = GELU_A * 0.044715

NN = (((1,), (0,)), ((), ()))
NT = (((1,), (1,)), ((), ()))
TN = (((0,), (0,)), ((), ()))


def dot(a, b, dims=NN):
    return lax.dot_general(a, b, dims, preferred_element_type=F32)


ANY = pl.BlockSpec(memory_space=pl.ANY)


def cost(micros):
    return pl.CostEstimate(flops=int(micros * 1.0e9), bytes_accessed=1000000, transcendentals=0)


def call(kernel, name, outs, args, needs=(), micros=0.01, grid=None, in_specs=None, out_specs=None, scratch=(), scalars=0):
    count = len(args)

    def body(*refs):
        kernel(*refs[:count], *refs[count + len(needs) :])

    if in_specs is None:
        whole = pl.BlockSpec(memory_space=pltpu.VMEM)
        in_specs = [pl.BlockSpec(memory_space=pltpu.SMEM)] * scalars + [whole] * (count - scalars)
        out_specs = [whole] * len(outs)
        spec = dict(in_specs=in_specs + [ANY] * len(needs), out_specs=out_specs, scratch_shapes=list(scratch))
    else:
        spec = dict(
            grid_spec=pltpu.PrefetchScalarGridSpec(
                num_scalar_prefetch=scalars,
                grid=grid,
                in_specs=in_specs + [ANY] * len(needs),
                out_specs=out_specs,
                scratch_shapes=list(scratch),
            )
        )
    return pl.pallas_call(
        body,
        out_shape=[jax.ShapeDtypeStruct(shape, kind) for shape, kind in outs],
        compiler_params=pltpu.CompilerParams(vmem_limit_bytes=VMEM_BYTES),
        cost_estimate=cost(micros),
        name=name,
        **spec,
    )(*args, *needs)


def after(values, *needs):
    count = len(values)
    return pl.pallas_call(
        lambda *refs: None,
        in_specs=[ANY] * (count + len(needs)),
        out_specs=[ANY] * count,
        out_shape=[jax.ShapeDtypeStruct(value.shape, value.dtype) for value in values],
        input_output_aliases={i: i for i in range(count)},
        cost_estimate=cost(0.01),
        name="after",
    )(*values, *needs)


def two_heads(pair):
    return jnp.concatenate([pair[:, :HD], pair[:, HD:]], axis=0)


def attend_kernel(place_ref, q_ref, far_ref, near_ref, here_ref, out_ref, probs_ref, kv_ref, bias, table):
    @pl.when(pl.program_id(0) == 0)
    def _():
        key = lax.broadcasted_iota(jnp.int32, (KEYS, ROW), 0)
        query = lax.broadcasted_iota(jnp.int32, (KEYS, ROW), 1)
        first = WINDOW - ROW * place_ref[0]
        inside = (key > query) & (key <= query + WINDOW) & (key >= first)
        one = jnp.where(inside, 0.0, NEG)
        bias[:, :] = jnp.concatenate([one, one], axis=1)
        table[:256, :] = far_ref[...]
        table[256:1024, :] = near_ref[...]
        table[1024:, :] = here_ref[...]
        kv_ref[...] = table[pl.ds(pl.multiple_of(place_ref[1] * ROW, ROW), KEYS), :]

    tables = [
        dot(kv_ref[:, :HD], two_heads(q_ref[:, 2 * HD * i : 2 * HD * (i + 1)]), NT) for i in range(PAIRS)
    ]
    for i, table in enumerate(tables):
        scores = table + bias[...]
        highest = jnp.max(scores, axis=0, keepdims=True)
        powers = jnp.exp2((scores - highest) * (SCALE * LOG2E))
        total = jnp.sum(powers, axis=0, keepdims=True)
        probs = (powers * (1.0 / total)).astype(BF)
        probs_ref[i] = probs
        mixed = dot(kv_ref[:, HD:], probs, TN).T.astype(BF)
        out_ref[:, 2 * HD * i : 2 * HD * (i + 1)] = jnp.concatenate([mixed[:ROW], mixed[ROW:]], axis=1)


def attend(place, queries, far, near, here, needs):
    pair = pl.BlockSpec((ROW, 2 * HD * PAIRS), lambda h, b: (0, h))

    def fixed(rows):
        return pl.BlockSpec((rows, 2 * HD), lambda h, b: (0, 0))

    return call(
        attend_kernel,
        "attend",
        [((ROW, HEADS * HD), BF), ((HEADS // 2, KEYS, 2 * ROW), BF), ((KEYS, 2 * HD), BF)],
        [place, queries, far, near, here],
        needs=needs,
        micros=10.0,
        grid=(HEADS // 2 // PAIRS,),
        in_specs=[pair, fixed(256), fixed(768), fixed(768)],
        out_specs=[pair, pl.BlockSpec((PAIRS, KEYS, 2 * ROW), lambda h, b: (h, 0, 0)), fixed(KEYS)],
        scratch=[pltpu.VMEM((KEYS, 2 * ROW), F32), pltpu.VMEM((1792, 2 * HD), BF)],
        scalars=1,
    )


HOME_ROWS = [slice(0, 64)] + [slice(64 + ROW * i, 64 + ROW * (i + 1)) for i in range(6)]


def attend_back_kernel(q_ref, kv_ref, out_ref, grad_ref, probs_ref, dq_ref, *rest):
    homes, (dk, dv) = rest[:7], rest[7:]
    step = pl.program_id(0)

    @pl.when(step == 0)
    def _():
        dk[...] = jnp.zeros_like(dk)
        dv[...] = jnp.zeros_like(dv)

    pairs = [slice(2 * HD * i, 2 * HD * (i + 1)) for i in range(PAIRS)]
    tables = [dot(kv_ref[:, HD:], two_heads(grad_ref[:, pair]), NT) for pair in pairs]
    for i, (pair, dprobs) in enumerate(zip(pairs, tables)):
        queries = two_heads(q_ref[:, pair])
        grads = two_heads(grad_ref[:, pair])
        outs = two_heads(out_ref[:, pair])
        probs = probs_ref[i]
        delta = jnp.sum((grads.astype(F32) * outs.astype(F32)).T, axis=0, keepdims=True)
        dscores = (probs.astype(F32) * (dprobs - delta)).astype(BF)
        dqueries = (dot(kv_ref[:, :HD], dscores, TN).T * SCALE).astype(BF)
        dq_ref[:, pair] = jnp.concatenate([dqueries[:ROW], dqueries[ROW:]], axis=1)
        dk[...] += dot(dscores, queries)
        dv[...] += dot(probs, grads)

    @pl.when(step == HEADS // 2 // PAIRS - 1)
    def _():
        for home, rows in zip(homes, HOME_ROWS):
            home[:, :HD] = (dk[rows, :] * SCALE).astype(BF)
            home[:, HD:] = dv[rows, :].astype(BF)


def attend_back(queries, keyval, attended, grads, probs, needs):
    pair = pl.BlockSpec((ROW, 2 * HD * PAIRS), lambda h: (0, h))
    table = pl.BlockSpec((KEYS, 2 * HD), lambda h: (0, 0))

    def home(rows):
        return pl.BlockSpec((rows, 2 * HD), lambda h: (0, 0))

    return call(
        attend_back_kernel,
        "attend_back",
        [((ROW, HEADS * HD), BF), ((64, 2 * HD), BF)] + [((ROW, 2 * HD), BF)] * 6,
        [queries, keyval, attended, grads, probs],
        needs=needs,
        micros=0.01,
        grid=(HEADS // 2 // PAIRS,),
        in_specs=[pair, table, pair, pair, pl.BlockSpec((PAIRS, KEYS, 2 * ROW), lambda h: (h, 0, 0))],
        out_specs=[pair, home(64)] + [home(ROW)] * 6,
        scratch=[pltpu.VMEM((KEYS, HD), F32), pltpu.VMEM((KEYS, HD), F32)],
    )


def down_back_kernel(cots, down_a, down_b, out_ref):
    out_ref[...] = dot(cots[:, :768], down_a[...]) + dot(cots[:, 768:], down_b[...])


def down_back(cots, rest_mine, rest_other):
    down = pl.BlockSpec((768, FF_TILE), lambda f: (0, 10 + f))
    return call(
        down_back_kernel,
        "down_back",
        [((RING, FF), F32)],
        [cots, rest_mine, rest_other],
        micros=6.0,
        grid=(FF_TILES,),
        in_specs=[pl.BlockSpec((RING, 1536), lambda f: (0, 0)), down, down],
        out_specs=[pl.BlockSpec((RING, FF_TILE), lambda f: (0, f))],
    )[0]


def ring_rows(ring, back):
    return pl.ds(pl.multiple_of(lax.rem(ring + 4 - back, 4) * ROW, ROW), ROW)


BACKS = (0, 1, 3, 2)


def mlp_kernel(
    ring_ref, zero, one, three, two, dhidden_ref, pair_a, pair_b, hidden_ref, dpair_ref, rows, rows_b, second_ref,
    second_sum
):
    @pl.when(pl.program_id(0) == 0)
    def _():
        for block, back in zip((zero, one, three, two), BACKS):
            rows[ring_rows(ring_ref[0], back), :] = block[...]
            rows_b[ring_rows(ring_ref[0], back), :] = block[:, 768:]

    step = pl.program_id(0)
    low, high = slice(0, 768), slice(768, 1536)
    both = dot(rows[:, low], pair_a[...]) + dot(rows[:, high], pair_b[...])
    gate, up = both[:, :FF_TILE], both[:, FF_TILE:]
    dhidden = dhidden_ref[...]
    square = gate * gate
    wave = jnp.tanh(gate * (GELU_A + GELU_B * square))
    half = 0.5 + 0.5 * wave
    gelu = gate * half
    slope = half + gate * (0.5 - 0.5 * wave * wave) * (GELU_A + 3.0 * GELU_B * square)
    hidden_ref[...] = (gelu * up).astype(BF)
    dpair = jnp.concatenate([(dhidden * up * slope).astype(BF), (dhidden * gelu).astype(BF)], axis=1)
    dpair_ref[...] = dpair
    part_a = dot(dpair, pair_a[...], NT)
    part_b = dot(dpair, pair_b[...], NT)

    @pl.when(step == 0)
    def _():
        second_sum[:, low] = part_a
        second_sum[:, high] = part_b

    @pl.when((step > 0) & (step < FF_TILES - 1))
    def _():
        second_sum[:, low] += part_a
        second_sum[:, high] += part_b

    @pl.when(step == FF_TILES - 1)
    def _():
        second_ref[:, low] = (second_sum[:, low] + part_a).astype(BF)
        second_ref[:, high] = (second_sum[:, high] + part_b).astype(BF)


def mlp(ring, blocks, dhidden, rest_mine, rest_other):
    whole = pl.BlockSpec((ROW, 1536), lambda f, r: (0, 0))
    table = pl.BlockSpec((RING, 1536), lambda f, r: (0, 0))
    half = pl.BlockSpec((RING, 768), lambda f, r: (0, 0))
    unit = pl.BlockSpec((RING, FF_TILE), lambda f, r: (0, f))
    pair_unit = pl.BlockSpec((RING, 2 * FF_TILE), lambda f, r: (0, f))
    pair = pl.BlockSpec((768, 2 * FF_TILE), lambda f, r: (0, 2 + f))
    return call(
        mlp_kernel,
        "mlp",
        [((RING, FF), BF), ((RING, 2 * FF), BF), ((RING, 1536), BF), ((RING, 768), BF), ((RING, 1536), BF)],
        [ring, *blocks, dhidden, rest_mine, rest_other],
        micros=20.0,
        grid=(FF_TILES,),
        in_specs=[whole] * 4 + [unit, pair, pair],
        out_specs=[unit, pair_unit, table, half, table],
        scratch=[pltpu.VMEM((RING, 1536), F32)],
        scalars=1,
    )


def down_project_kernel(hidden_ref, down_a, down_b, out_ref):
    out_ref[:, :768] = dot(hidden_ref[...], down_a[...], NT).astype(BF)
    out_ref[:, 768:] = dot(hidden_ref[...], down_b[...], NT).astype(BF)


def down_project(hidden, rest_mine, rest_other):
    down = pl.BlockSpec((pl.Element(768), pl.Element(FF)), lambda f: (0, 1536 + 2 * FF))
    table = pl.BlockSpec((RING, 1536), lambda f: (0, 0))
    return call(
        down_project_kernel,
        "down_project",
        [((RING, 1536), BF)],
        [hidden, rest_mine, rest_other],
        grid=(1,),
        in_specs=[pl.BlockSpec((RING, FF), lambda f: (0, 0)), down, down],
        out_specs=[table],
    )[0]


def out_grad_kernel(left, left_b, right, right_b, out_ref):
    lefts = jnp.concatenate([left[...], left_b[...]], axis=0)
    rights = jnp.concatenate([right[...], right_b[...]], axis=0)
    out_ref[...] = dot(lefts, rights, TN).astype(BF)


def out_grad(left, left_b, right, right_b, total):
    lefts = pl.BlockSpec((ROW, 768), lambda i: (0, 0))
    rights = pl.BlockSpec((ROW, 384), lambda i: (0, i))
    return pl.pallas_call(
        lambda *refs: out_grad_kernel(*refs[:4], refs[5]),
        grid=(4,),
        in_specs=[lefts, lefts, rights, rights, ANY],
        out_specs=pl.BlockSpec((768, 384), lambda i: (0, 3 * FF // 384 + i)),
        out_shape=jax.ShapeDtypeStruct(total.shape, BF),
        input_output_aliases={4: 0},
        compiler_params=pltpu.CompilerParams(vmem_limit_bytes=VMEM_BYTES),
        cost_estimate=cost(0.01),
        name="out_grad",
    )(left, left_b, right, right_b, total)


def unit_grad_kernel(left, left_b, cot, cot_b, dpair, dpair_b, hidden, hidden_b, out_ref):
    pair = dot(left[...], dpair[...], TN) + dot(left_b[...], dpair_b[...], TN)
    down = dot(cot[...], hidden[...], TN) + dot(cot_b[...], hidden_b[...], TN)
    out_ref[:, : 2 * FF] = pair.astype(BF)
    out_ref[:, 2 * FF :] = down.astype(BF)


def unit_grad(args, needs):
    tile = 256
    left = pl.BlockSpec((RING, tile), lambda i: (0, i))
    return call(
        unit_grad_kernel,
        "unit_grad",
        [((768, 3 * FF + 1536), BF)],
        args,
        needs=needs,
        micros=6.0,
        grid=(768 // tile,),
        in_specs=[left] * 4 + [pl.BlockSpec(a.shape, lambda i: (0, 0)) for a in args[4:]],
        out_specs=[pl.BlockSpec((tile, 3 * FF), lambda i: (i, 0))],
    )


def merge_kernel(*refs):
    out_ref = refs[-1]
    start = 0
    for mine, other in zip(refs[:-1:2], refs[1:-1:2]):
        width = mine.shape[1]
        out_ref[:, start : start + width] = (mine[...].astype(F32) + other[...].astype(F32)).astype(BF)
        start += width


def merge(*pairs, needs=()):
    width = sum(mine.shape[1] for mine, _ in pairs)
    return call(merge_kernel, "merge", [((768, width), BF)], [array for pair in pairs for array in pair], needs)[0]


def normed(rows):
    values = rows.astype(F32)
    inverse = lax.rsqrt(jnp.mean(values * values, axis=-1, keepdims=True) + EPSILON)
    return values, values * inverse, inverse


def norm_back(grad, gain, n, inverse):
    scaled = grad * gain
    return inverse * (scaled - n * jnp.mean(scaled * n, axis=-1, keepdims=True))


def keyval_kernel(ids, own, one, three, mine_ref, other_ref, gain_ref, token_ref, first_ref, keyval_ref):
    head, core = ids[0], ids[1]
    gain_ref[:, :768] = mine_ref[:, 640:].astype(F32).T[:8]
    gain_ref[:, 768:] = other_ref[:, 640:].astype(F32).T[:8]

    def local(block):
        return local_order(block[...].astype(F32), core)

    def project(block):
        first = (normed(block)[1] * gain_ref[0:1, :]).astype(BF)
        total = dot(first[:, :768], mine_ref[:, 384:640]) + dot(first[:, 768:], other_ref[:, 384:640])
        return first, total.astype(BF)

    token = local(own)
    token_ref[...] = token.astype(BF)
    first, total = project(token)
    first_ref[...] = first

    @pl.when(head == 0)
    def _():
        keyval_ref[:ROW, :] = total
        keyval_ref[ROW:, :] = project(local(three))[1]

    @pl.when(head == 1)
    def _():
        keyval_ref[:ROW, :] = project(local(one))[1]
        keyval_ref[ROW:, :] = total


def local_order(rows, core):
    low = jnp.concatenate([rows[:, 384 * z : 384 * z + 192] for z in range(4)], axis=1)
    high = jnp.concatenate([rows[:, 384 * z + 192 : 384 * z + 384] for z in range(4)], axis=1)
    return jnp.concatenate([jnp.where(core == 0, low, high), jnp.where(core == 0, high, low)], axis=1)


def true_order(rows, core):
    low = jnp.where(core == 0, rows[:, :768], rows[:, 768:])
    high = jnp.where(core == 0, rows[:, 768:], rows[:, :768])
    cuts = [half[:, 192 * z : 192 * (z + 1)] for z in range(4) for half in (low, high)]
    return jnp.concatenate(cuts, axis=1)


def order_kernel(core_ref, rows_ref, out_ref, copies):
    rows = local_order(rows_ref[...].astype(F32), core_ref[0]).astype(BF)
    out_ref[...] = rows
    for i in range(4):
        copies[i] = rows


def table_kernel(core_ref, mine_ref, other_ref, table_ref, last_ref):
    @pl.when(core_ref[0] == 0)
    def _():
        table_ref[: 2 * ROW, :] = mine_ref[...]
        table_ref[2 * ROW :, :] = other_ref[...]

    @pl.when(core_ref[0] == 1)
    def _():
        table_ref[: 2 * ROW, :] = other_ref[...]
        table_ref[2 * ROW :, :] = mine_ref[...]

    last_ref[...] = table_ref[512:, :]


def ring_cols(ring, ahead):
    return pl.ds(pl.multiple_of(lax.rem(ring + ahead, 4) * 384, 384), 384)


def turn_kernel(ring_ref, zero, one, two, three, out_ref):
    for ahead, block in enumerate((zero, one, two, three)):
        out_ref[:, ring_cols(ring_ref[0], ahead)] = block[...]


def cut_kernel(rows_ref, out_ref):
    for i in range(4):
        out_ref[i] = rows_ref[:, 384 * i : 384 * (i + 1)]


def query_kernel(ids, first_ref, one, three, two, gain_ref, mine_ref, other_ref, all_ref, *outs_total):
    outs, total = outs_total[:4], outs_total[4]
    core, ring = ids[0], ids[1]
    all_ref[ring_rows(ring, 0), :] = first_ref[...]
    for back, block in ((1, one), (3, three), (2, two)):
        first = normed(local_order(block[...].astype(F32), core))[1] * gain_ref[0:1, :]
        all_ref[ring_rows(ring, back), :] = first.astype(BF)
    rows = all_ref[...]
    total[...] = (dot(rows[:, :768], mine_ref[:, :384]) + dot(rows[:, 768:], other_ref[:, :384])).astype(BF)
    for out, back in zip(outs, BACKS):
        out[...] = total[ring_rows(ring, back), :]


def middle_kernel(attended_ref, mine_ref, other_ref, token_ref, gain_ref, middle_ref, second_ref):
    attended = attended_ref[...]
    branch = jnp.concatenate([dot(attended, mine_ref[...], NT), dot(attended, other_ref[...], NT)], axis=1)
    middle = token_ref[...].astype(F32) + branch
    middle_ref[...] = middle
    second_ref[...] = (normed(middle)[1] * gain_ref[1:2, :]).astype(BF)


def middle_back_kernel(
    parts, middle_ref, cot_ref, gain_ref, mine_ref, other_ref, grad_ref, low_ref, high_ref, terms_ref, attended_ref
):
    grad_second = sum(parts[i].astype(F32) for i in range(4))
    _, n2, rs2 = normed(middle_ref[...])
    grad_middle = cot_ref[...].astype(F32) + norm_back(grad_second, gain_ref[1:2, :], n2, rs2)
    grad_ref[...] = grad_middle
    low = grad_middle.astype(BF)
    low_ref[...] = low[:, :768]
    high_ref[...] = low[:, 768:]
    terms_ref[...] = (grad_second * n2).astype(BF)
    attended_ref[...] = (dot(low[:, :768], mine_ref[...]) + dot(low[:, 768:], other_ref[...])).astype(BF)


def first_back_kernel(
    ring_ref, dqueries, home_6, home_5, home_4, home_3, home_2, home_1, home_0, rest_a, rest_b, first_ref,
    second_terms, mlp_out, own_ref, one, three, two, tail_a, tail_b, sums, partial,
):
    ring = ring_ref[0]
    dquery = jnp.concatenate([dqueries[i] for i in range(4)], axis=0)
    sums[...] = sum(home[...].astype(F32) for home in (home_5, home_4, home_3, home_2, home_1, home_0))
    sums[128:, :] += home_6[...].astype(F32)
    dkeyval = sums[...].astype(BF)
    column = lax.broadcasted_iota(jnp.int32, (RING + ROW, 128), 1)
    row = lax.broadcasted_iota(jnp.int32, (RING + ROW, 128), 0)
    picks = jnp.where(column == (row >= RING).astype(jnp.int32), 1.0, 0.0).astype(BF)
    own_rows = ring_rows(ring, 0)
    for cols, rest, tail in ((slice(0, 768), rest_a, tail_a), (slice(768, 1536), rest_b, tail_b)):
        partial[...] = dot(dquery, rest[:, :384], NT)
        partial[own_rows, :] += dot(dkeyval, rest[:, 384:640], NT)
        own_ref[:, cols] = partial[own_rows, :]
        for back, ref in ((1, one), (3, three), (2, two)):
            ref[0, :, cols] = partial[ring_rows(ring, back), :].astype(BF)
            ref[1, :, cols] = mlp_out[ring_rows(ring, back), cols]
        first = first_ref[:, cols]
        terms = jnp.concatenate([(partial[...] * first.astype(F32)).astype(BF), second_terms[:, cols]], axis=0)
        tail[:, :384] = dot(first, dquery, TN).astype(BF)
        tail[:, 384:640] = dot(first_ref[own_rows, cols], dkeyval, TN).astype(BF)
        tail[:, 640:] = dot(terms, picks, TN).astype(BF)


def finish_kernel(
    ids, own_ref, one, three, two, token_ref, gain_ref, grad_ref, middle_ref, mlp_ref, input_ref, block_ref
):
    core, ring = ids[0], ids[1]
    grad_first = own_ref[...] + sum(part[0].astype(F32) for part in (one, three, two))
    _, n1, rs1 = normed(token_ref[...])
    total = grad_ref[...] + norm_back(grad_first, gain_ref[0:1, :], n1, rs1)
    input_ref[...] = true_order(total, core).astype(BF)
    total = middle_ref[...] + mlp_ref[ring_rows(ring, 0), :].astype(F32)
    total = total + sum(part[1].astype(F32) for part in (one, three, two))
    block_ref[...] = true_order(total, core).astype(BF)


def tail_kernel(core_ref, parts, out_ref):
    total = sum(parts[i].astype(F32) for i in range(16))
    out_ref[...] = jnp.zeros_like(out_ref)
    for xh in range(2):
        keep = jnp.where(core_ref[0] == xh, 1.0, 0.0)
        for i in range(4):
            out_ref[4 * xh + i, :12, :768] = (total[12 * i : 12 * (i + 1)] * keep).astype(BF)


def deal_kernel(ids, owned_ref, give_a, give_b, cross_a, cross_b):
    head, xh = ids[0], ids[1]
    start = 3 * FF

    def rows(cols, flip):
        block = owned_ref[:, cols].astype(F32)
        return jnp.where((xh == 0) != flip, block[:24], block[24:]).astype(BF)

    def part(chip):
        return pl.ds(pl.multiple_of(start + 384 * chip, 384), 384)

    for flip, give, cross in ((False, give_a, cross_a), (True, give_b, cross_b)):
        give[:, :start] = rows(slice(0, start), flip)
        for i in range(2):
            give[:, start + 384 * i : start + 384 * (i + 1)] = rows(part(2 * i + head), flip)
            cross[:, 384 * i : 384 * (i + 1)] = rows(part(2 * i + 1 - head), flip)


def final_kernel(ids, tail, got_a, got_b, cross_a, cross_b, gain_own, query_ref, key_ref, value_ref, gain_ref, out_ref, gate_ref,
                 up_ref, down_ref):
    core, xh = ids[0], ids[1]
    total = jnp.zeros((12, 384), F32)
    for xh_from in range(2):
        for head in range(2):
            block = tail[4 * xh_from + 2 * xh + head].astype(F32)[:12]
            quarter = 2 * head + xh_from
            query_ref[:, 384 * quarter : 384 * (quarter + 1)] = block[:, :384]
            total = total + block[:, 384:768]
    key_ref[...] = total[:, :HD]
    value_ref[...] = total[:, HD : 2 * HD]
    sums = jnp.concatenate([total[:, 2 * HD :], jnp.zeros((4, HD), F32)], axis=0).T
    gain_ref[0:1, :] = sums[0:1, :12] / gain_own[...]
    gain_ref[1:2, :] = sums[1:2, :12]
    first, second = got_a[...].astype(F32), got_b[...].astype(F32)
    halves = (jnp.where(core == 0, first, second), jnp.where(core == 0, second, first))
    for i, half in enumerate(halves):
        for f in range(FF_TILES):
            place = slice(FF * i + FF_TILE * f, FF * i + FF_TILE * (f + 1))
            gate_ref[:, place] = half[:, 2 * FF_TILE * f : 2 * FF_TILE * f + FF_TILE]
            up_ref[:, place] = half[:, 2 * FF_TILE * f + FF_TILE : 2 * FF_TILE * (f + 1)]
        down_ref[:, FF * i : FF * (i + 1)] = half[:, 2 * FF : 3 * FF]
    out_ref[...] = (
        halves[0][:, 3 * FF :] + halves[1][:, 3 * FF :] + cross_a[...].astype(F32) + cross_b[...].astype(F32)
    )


def turn_xc(block, flip, cross, back=False):
    route = []
    for xh in range(2):
        for core in range(2):
            for head in range(2):
                target = (core ^ flip) * 4 + xh * 2 + (head ^ cross)
                source = xh * 4 + core * 2 + head
                route.append((target, source) if back else (source, target))
    return lax.ppermute(block, ("xh", "core", "head"), route)


def shift_all(block, distance):
    count = 128
    route = [(i, i + distance) for i in range(count) if 0 <= i + distance < count]
    return lax.ppermute(block, AXES, route)


def shift_groups(block, distance):
    return lax.ppermute(block, ("z", "xh", "y"), [(i, i + distance) for i in range(32 - distance)])


def shift_x(block, distance):
    return lax.ppermute(block, CHIPS_X, [(i, (i + distance) % 4) for i in range(4)])


def swap(block, axis):
    return lax.ppermute(block, axis, [(0, 1), (1, 0)])


def shards(tokens, cotangent, w_query, w_key, w_value, w_out, w_gate, w_up, w_down, gain_attn, gain_mlp):
    core = lax.axis_index("core")
    xh = lax.axis_index("xh")
    head = lax.axis_index("head")
    ring = 2 * xh + head
    place = jnp.stack([lax.axis_index(AXES), 2 * core + head]).astype(jnp.int32)
    ring_scalar, core_scalar, head_scalar = (i.astype(jnp.int32).reshape(1) for i in (ring, core, head))
    eight = ("xh", "core", "head")

    def ordered(index, first, second, axis):
        return jnp.concatenate(
            [jnp.where(index == 0, first, second), jnp.where(index == 0, second, first)], axis=axis
        )

    def spread(piece):
        sent = jnp.broadcast_to(piece[None], (16,) + piece.shape)
        return lax.all_to_all(sent, PLANE, 0, 0, tiled=True).reshape(768, -1)

    def gather(piece):
        return lax.all_gather(piece, PLANE, axis=0, tiled=True)

    gains = jnp.pad(jnp.stack([gain_attn, gain_mlp], axis=1), ((0, 0), (0, 126)))
    query_cut = w_query.reshape(12, 2, 2, 384).transpose(2, 1, 0, 3)
    common = jnp.broadcast_to(jnp.concatenate([w_key, w_value, gains], axis=1), (2, 2, 12, 384))
    own_qkv = jnp.concatenate([query_cut, common], axis=3)
    own_qkv = jnp.broadcast_to(own_qkv[:, None], (2, 2, 2, 12, 768)).reshape(8, 12, 768)
    got = lax.all_to_all(own_qkv, eight, 0, 0, tiled=True)
    qkv_piece = lax.dynamic_slice_in_dim(got, core * 4, 4, 0).reshape(48, 768)
    token_1, token_3, token_2 = (shift_x(tokens, k) for k in (1, 3, 2))
    qkv_mine = spread(qkv_piece)
    cot_own, cot_sent = call(
        order_kernel,
        "order",
        [((ROW, 1536), BF), ((4, ROW, 1536), BF)],
        [core_scalar, cotangent],
        scalars=1,
    )
    (cot_sent,) = after([cot_sent], qkv_mine)
    cots = lax.all_to_all(cot_sent, CHIPS_X, 0, 0, tiled=True).reshape(RING, 1536)
    (qkv_mine,) = after([qkv_mine], token_1, token_3, token_2)

    pair_cut = jnp.stack([w_gate, w_up], axis=1).reshape(24, 2, 2, FF_TILES, FF_TILE)
    pair_cut = pair_cut.transpose(2, 0, 3, 1, 4).reshape(2, 24, 2 * FF)
    down_cut = w_down.T.reshape(24, 2, FF).transpose(1, 0, 2)
    own_mlp = jnp.concatenate([pair_cut, down_cut], axis=2)
    sent_a = jnp.where(core == 0, own_mlp[0], own_mlp[1])
    sent_b = jnp.where(core == 0, own_mlp[1], own_mlp[0])
    out_low = w_out.T
    got_a = turn_xc(jnp.concatenate([out_low, sent_a], axis=1), False, False)
    got_b = turn_xc(jnp.concatenate([out_low, sent_b], axis=1), True, False)
    cross_a, cross_b = turn_xc(out_low, False, True), turn_xc(out_low, True, True)
    out_same = ordered(xh, got_a[:, :768], got_b[:, :768], 0).reshape(48, 2, 1, 384)
    out_cross = ordered(xh, cross_a, cross_b, 0).reshape(48, 2, 1, 384)
    out_piece = ordered(head, out_same, out_cross, 2).reshape(48, 1536)
    mlp_piece = ordered(xh, got_a[:, 768:], got_b[:, 768:], 0)
    (rest_piece,) = after([jnp.concatenate([out_piece, mlp_piece], axis=1)], qkv_piece)
    rest_mine = gather(rest_piece)

    qkv_other = swap(qkv_mine, "core")
    gain_rows, token_own, first_own, keyval_pair = call(
        keyval_kernel,
        "keyval",
        [((8, 1536), F32), ((ROW, 1536), BF), ((ROW, 1536), BF), ((2 * ROW, 256), BF)],
        [jnp.concatenate([head_scalar, core_scalar]), tokens, token_1, token_3, qkv_mine, qkv_other],
        scalars=1,
    )
    here, last = call(
        table_kernel,
        "table",
        [((768, 256), BF), ((256, 256), BF)],
        [core_scalar, keyval_pair, swap(keyval_pair, "core")],
        scalars=1,
    )
    near, far = shift_groups(here, 1), shift_groups(last, 2)
    first_all, query_0, ring_1, ring_3, ring_2 = call(
        query_kernel,
        "query",
        [((RING, 1536), BF)] + [((ROW, 384), BF)] * 4,
        [jnp.concatenate([core_scalar, ring_scalar]), first_own, token_1, token_3, token_2, gain_rows, qkv_mine, qkv_other],
        scratch=[pltpu.VMEM((RING, 384), BF)],
        scalars=1,
        needs=[here],
    )
    query_1, query_3, query_2 = shift_x(ring_1, -1), shift_x(ring_3, -3), shift_x(ring_2, -2)
    (queries,) = call(
        turn_kernel, "turn", [((ROW, 1536), BF)], [ring_scalar, query_0, query_1, query_2, query_3], scalars=1
    )
    (rest_mine,) = after([rest_mine], queries, near, far, cots)
    out_mine = rest_mine[:, :1536]
    attended, probs, keyval = attend(place, queries, far, near, here, [out_mine])

    out_other = swap(out_mine, "core")
    middle, second_own = call(
        middle_kernel,
        "middle",
        [((ROW, 1536), F32), ((ROW, 1536), BF)],
        [attended, out_mine, out_other, token_own, gain_rows],
    )
    blocks = [second_own] + [shift_x(second_own, k) for k in (1, 3, 2)]
    (rest_mine,) = after([rest_mine], attended, out_other)
    rest_other = swap(rest_mine, "core")
    dhidden = down_back(cots, rest_mine, rest_other)

    hidden, dpair, seconds, seconds_b, second_part = mlp(ring_scalar, blocks, dhidden, rest_mine, rest_other)
    second_home = lax.all_to_all(second_part.reshape(4, ROW, 1536), CHIPS_X, 0, 0, tiled=True)

    def planes(total):
        got = lax.all_to_all(total.reshape(16, 48, -1), PLANE, 0, 0, tiled=True)
        return jnp.sum(got.astype(F32), axis=0).astype(BF)

    mlp_out = down_project(hidden, rest_mine, rest_other)
    (unit_total,) = unit_grad(
        [seconds, swap(seconds_b, "core"), cots, swap(cots[:, 768:], "core")]
        + [dpair, swap(dpair, "core"), hidden, swap(hidden, "core")],
        [mlp_out],
    )
    grad_middle, branch_a, branch_b, second_terms, grad_attended = call(
        middle_back_kernel,
        "middle_back",
        [((ROW, 1536), F32), ((ROW, 768), BF), ((ROW, 768), BF), ((ROW, 1536), BF), ((ROW, 1536), BF)],
        [second_home, middle, cot_own, gain_rows, out_mine, out_other],
        needs=[unit_total],
    )
    dqueries, *homes = attend_back(queries, keyval, attended, grad_attended, probs, [])

    (dquery_cut,) = call(cut_kernel, "cut", [((4, ROW, 384), BF)], [dqueries])
    dquery_ring = lax.all_to_all(dquery_cut, CHIPS_X, 0, 0, tiled=True)
    homes = [shift_all(home, -k) for home, k in zip(homes, (6, 5, 4, 3, 2, 1))] + [homes[6]]
    total = out_grad(branch_a, swap(branch_b, "core"), attended, swap(attended, "core"), unit_total)
    owned = lax.psum_scatter(total, PLANE, scatter_dimension=0, tiled=True)
    own_first, first_1, first_3, first_2, tail_mine, tail_other = call(
        first_back_kernel,
        "first_back",
        [((ROW, 1536), F32)] + [((2, ROW, 1536), BF)] * 3 + [((768, 768), BF)] * 2,
        [
            ring_scalar, dquery_ring, *homes, qkv_mine, qkv_other, first_all, second_terms,
            mlp_out,
        ],
        scratch=[pltpu.VMEM((ROW, 256), F32), pltpu.VMEM((RING, 768), F32)],
        scalars=1,
    )
    tail_total = merge((tail_mine, swap(tail_other, "core")))
    tail_parts = lax.all_to_all(tail_total.reshape(16, 48, 768), PLANE, 0, 0, tiled=True)
    first_1, first_3, first_2 = shift_x(first_1, -1), shift_x(first_3, -3), shift_x(first_2, -2)
    input_grad, block_out = call(
        finish_kernel,
        "finish",
        [((ROW, 1536), BF)] * 2,
        [jnp.concatenate([core_scalar, ring_scalar]), own_first, first_1, first_3, first_2, token_own, gain_rows]
        + [grad_middle, middle, mlp_out],
        scalars=1,
    )
    (tail_sent,) = call(tail_kernel, "tail", [((8, 16, 1024), BF)], [core_scalar, tail_parts], scalars=1)
    tail_got = lax.all_to_all(tail_sent, eight, 0, 0, tiled=True)
    give_a, give_b, cross_a, cross_b = call(
        deal_kernel,
        "deal",
        [((24, 3 * FF + 768), BF)] * 2 + [((24, 768), BF)] * 2,
        [jnp.concatenate([head_scalar, xh.astype(jnp.int32).reshape(1)]), owned],
        needs=[first_1, first_3, first_2],
        micros=10.0,
        scalars=1,
    )
    got_a, got_b = turn_xc(give_a, False, False, True), turn_xc(give_b, True, False, True)
    cross_a, cross_b = turn_xc(cross_a, False, True, True), turn_xc(cross_b, True, True, True)
    query_grad, key_grad, value_grad, gain_grads, out_grad_own, gate_grad, up_grad, down_grad = call(
        final_kernel,
        "final",
        [((12, 1536), F32)] + [((12, 128), F32)] * 2 + [((2, 12), F32), ((24, 768), F32)] + [((24, 2 * FF), F32)] * 3,
        [jnp.concatenate([core_scalar, xh.astype(jnp.int32).reshape(1)]), tail_got, got_a, got_b, cross_a, cross_b]
        + [gain_attn.astype(F32).reshape(1, 12)],
        needs=[input_grad, block_out],
        scalars=1,
    )
    return (
        block_out,
        input_grad,
        query_grad,
        key_grad,
        value_grad,
        out_grad_own.T,
        gate_grad,
        up_grad,
        down_grad.T,
        gain_grads[0],
        gain_grads[1],
    )


def solution(mesh):
    grid = Mesh(mesh.devices.reshape(SIZES), AXES)
    seq = ("z", "xh", "y", "core")
    rows, both, cols = P(AXES, None), P(seq, "head"), P("head", seq)
    in_specs = (rows, rows, rows, rows, rows, cols, both, both, cols, P(AXES), P(AXES))
    out_specs = (rows, rows, rows, rows, rows, cols, both, both, cols, P(AXES), P(AXES))
    return jax.shard_map(shards, mesh=grid, in_specs=in_specs, out_specs=out_specs, check_vma=False)
```

```python
import functools
import jax
import jax.numpy as jnp
from jax import lax
from jax.experimental import pallas as pl
from jax.experimental.pallas import tpu as pltpu
from jax.sharding import Mesh
from jax.sharding import PartitionSpec as P

WINDOW = 1024
EPSILON = 1e-06
AXES = ("z", "xh", "y", "core", "head")
SIZES = (4, 2, 4, 2, 2)
CHIPS_X = ("xh", "head")
PLANE = ("z", "y")
ROW = 192
KEYS = 1216
HEADS = 12
PAIRS = 2
HD = 128
BF = jnp.bfloat16
F32 = jnp.float32
NEG = -1e30
SCALE = HD ** (-0.5)
LOG2E = 1.4426950408889634
VMEM_BYTES = 56 * 1024 * 1024
FF = 1152
FF_TILES = 3
FF_TILE = 384
RING = 768
GELU_A = 0.7978845608028654
GELU_B = GELU_A * 0.044715

NN = (((1,), (0,)), ((), ()))
NT = (((1,), (1,)), ((), ()))
TN = (((0,), (0,)), ((), ()))


def dot(a, b, dims=NN):
    return lax.dot_general(a, b, dims, preferred_element_type=F32)


ANY = pl.BlockSpec(memory_space=pl.ANY)


def cost(micros):
    return pl.CostEstimate(flops=int(micros * 1.0e9), bytes_accessed=1000000, transcendentals=0)


def call(kernel, name, outs, args, needs=(), micros=0.01, grid=None, in_specs=None, out_specs=None, scratch=(), scalars=0):
    count = len(args)

    def body(*refs):
        kernel(*refs[:count], *refs[count + len(needs) :])

    if in_specs is None:
        whole = pl.BlockSpec(memory_space=pltpu.VMEM)
        in_specs = [pl.BlockSpec(memory_space=pltpu.SMEM)] * scalars + [whole] * (count - scalars)
        out_specs = [whole] * len(outs)
        spec = dict(in_specs=in_specs + [ANY] * len(needs), out_specs=out_specs, scratch_shapes=list(scratch))
    else:
        spec = dict(
            grid_spec=pltpu.PrefetchScalarGridSpec(
                num_scalar_prefetch=scalars,
                grid=grid,
                in_specs=in_specs + [ANY] * len(needs),
                out_specs=out_specs,
                scratch_shapes=list(scratch),
            )
        )
    return pl.pallas_call(
        body,
        out_shape=[jax.ShapeDtypeStruct(shape, kind) for shape, kind in outs],
        compiler_params=pltpu.CompilerParams(vmem_limit_bytes=VMEM_BYTES),
        cost_estimate=cost(micros),
        name=name,
        **spec,
    )(*args, *needs)


def after(values, *needs):
    count = len(values)
    return pl.pallas_call(
        lambda *refs: None,
        in_specs=[ANY] * (count + len(needs)),
        out_specs=[ANY] * count,
        out_shape=[jax.ShapeDtypeStruct(value.shape, value.dtype) for value in values],
        input_output_aliases={i: i for i in range(count)},
        cost_estimate=cost(0.01),
        name="after",
    )(*values, *needs)


def two_heads(pair):
    return jnp.concatenate([pair[:, :HD], pair[:, HD:]], axis=0)


def attend_kernel(place_ref, q_ref, far_ref, near_ref, here_ref, out_ref, probs_ref, kv_ref, bias, table):
    @pl.when(pl.program_id(0) == 0)
    def _():
        key = lax.broadcasted_iota(jnp.int32, (KEYS, ROW), 0)
        query = lax.broadcasted_iota(jnp.int32, (KEYS, ROW), 1)
        first = WINDOW - ROW * place_ref[0]
        inside = (key > query) & (key <= query + WINDOW) & (key >= first)
        one = jnp.where(inside, 0.0, NEG)
        bias[:, :] = jnp.concatenate([one, one], axis=1)
        table[:256, :] = far_ref[...]
        table[256:1024, :] = near_ref[...]
        table[1024:, :] = here_ref[...]
        kv_ref[...] = table[pl.ds(pl.multiple_of(place_ref[1] * ROW, ROW), KEYS), :]

    tables = [
        dot(kv_ref[:, :HD], two_heads(q_ref[:, 2 * HD * i : 2 * HD * (i + 1)]), NT) for i in range(PAIRS)
    ]
    for i, table in enumerate(tables):
        scores = table + bias[...]
        highest = jnp.max(scores, axis=0, keepdims=True)
        powers = jnp.exp2((scores - highest) * (SCALE * LOG2E))
        total = jnp.sum(powers, axis=0, keepdims=True)
        probs = (powers * (1.0 / total)).astype(BF)
        probs_ref[i] = probs
        mixed = dot(kv_ref[:, HD:], probs, TN).T.astype(BF)
        out_ref[:, 2 * HD * i : 2 * HD * (i + 1)] = jnp.concatenate([mixed[:ROW], mixed[ROW:]], axis=1)


def attend(place, queries, far, near, here, needs):
    pair = pl.BlockSpec((ROW, 2 * HD * PAIRS), lambda h, b: (0, h))

    def fixed(rows):
        return pl.BlockSpec((rows, 2 * HD), lambda h, b: (0, 0))

    return call(
        attend_kernel,
        "attend",
        [((ROW, HEADS * HD), BF), ((HEADS // 2, KEYS, 2 * ROW), BF), ((KEYS, 2 * HD), BF)],
        [place, queries, far, near, here],
        needs=needs,
        micros=10.0,
        grid=(HEADS // 2 // PAIRS,),
        in_specs=[pair, fixed(256), fixed(768), fixed(768)],
        out_specs=[pair, pl.BlockSpec((PAIRS, KEYS, 2 * ROW), lambda h, b: (h, 0, 0)), fixed(KEYS)],
        scratch=[pltpu.VMEM((KEYS, 2 * ROW), F32), pltpu.VMEM((1792, 2 * HD), BF)],
        scalars=1,
    )


HOME_ROWS = [slice(0, 64)] + [slice(64 + ROW * i, 64 + ROW * (i + 1)) for i in range(6)]


def attend_back_kernel(q_ref, kv_ref, out_ref, grad_ref, probs_ref, dq_ref, *rest):
    homes, (dk, dv) = rest[:7], rest[7:]
    step = pl.program_id(0)

    @pl.when(step == 0)
    def _():
        dk[...] = jnp.zeros_like(dk)
        dv[...] = jnp.zeros_like(dv)

    pairs = [slice(2 * HD * i, 2 * HD * (i + 1)) for i in range(PAIRS)]
    tables = [dot(kv_ref[:, HD:], two_heads(grad_ref[:, pair]), NT) for pair in pairs]
    for i, (pair, dprobs) in enumerate(zip(pairs, tables)):
        queries = two_heads(q_ref[:, pair])
        grads = two_heads(grad_ref[:, pair])
        outs = two_heads(out_ref[:, pair])
        probs = probs_ref[i]
        delta = jnp.sum((grads.astype(F32) * outs.astype(F32)).T, axis=0, keepdims=True)
        dscores = (probs.astype(F32) * (dprobs - delta)).astype(BF)
        dqueries = (dot(kv_ref[:, :HD], dscores, TN).T * SCALE).astype(BF)
        dq_ref[:, pair] = jnp.concatenate([dqueries[:ROW], dqueries[ROW:]], axis=1)
        dk[...] += dot(dscores, queries)
        dv[...] += dot(probs, grads)

    @pl.when(step == HEADS // 2 // PAIRS - 1)
    def _():
        for home, rows in zip(homes, HOME_ROWS):
            home[:, :HD] = (dk[rows, :] * SCALE).astype(BF)
            home[:, HD:] = dv[rows, :].astype(BF)


def attend_back(queries, keyval, attended, grads, probs, needs):
    pair = pl.BlockSpec((ROW, 2 * HD * PAIRS), lambda h: (0, h))
    table = pl.BlockSpec((KEYS, 2 * HD), lambda h: (0, 0))

    def home(rows):
        return pl.BlockSpec((rows, 2 * HD), lambda h: (0, 0))

    return call(
        attend_back_kernel,
        "attend_back",
        [((ROW, HEADS * HD), BF), ((64, 2 * HD), BF)] + [((ROW, 2 * HD), BF)] * 6,
        [queries, keyval, attended, grads, probs],
        needs=needs,
        micros=0.01,
        grid=(HEADS // 2 // PAIRS,),
        in_specs=[pair, table, pair, pair, pl.BlockSpec((PAIRS, KEYS, 2 * ROW), lambda h: (h, 0, 0))],
        out_specs=[pair, home(64)] + [home(ROW)] * 6,
        scratch=[pltpu.VMEM((KEYS, HD), F32), pltpu.VMEM((KEYS, HD), F32)],
    )


def down_back_kernel(cots, down_a, down_b, out_ref):
    out_ref[...] = dot(cots[:, :768], down_a[...]) + dot(cots[:, 768:], down_b[...])


def down_back(cots, rest_mine, rest_other):
    down = pl.BlockSpec((768, FF_TILE), lambda f: (0, 10 + f))
    return call(
        down_back_kernel,
        "down_back",
        [((RING, FF), F32)],
        [cots, rest_mine, rest_other],
        micros=6.0,
        grid=(FF_TILES,),
        in_specs=[pl.BlockSpec((RING, 1536), lambda f: (0, 0)), down, down],
        out_specs=[pl.BlockSpec((RING, FF_TILE), lambda f: (0, f))],
    )[0]


def ring_rows(ring, back):
    return pl.ds(pl.multiple_of(lax.rem(ring + 4 - back, 4) * ROW, ROW), ROW)


BACKS = (0, 1, 3, 2)


def mlp_kernel(
    ring_ref, zero, one, three, two, dhidden_ref, pair_a, pair_b, hidden_ref, dpair_ref, rows, rows_b, second_ref,
    second_sum
):
    @pl.when(pl.program_id(0) == 0)
    def _():
        for block, back in zip((zero, one, three, two), BACKS):
            rows[ring_rows(ring_ref[0], back), :] = block[...]
            rows_b[ring_rows(ring_ref[0], back), :] = block[:, 768:]

    step = pl.program_id(0)
    low, high = slice(0, 768), slice(768, 1536)
    both = dot(rows[:, low], pair_a[...]) + dot(rows[:, high], pair_b[...])
    gate, up = both[:, :FF_TILE], both[:, FF_TILE:]
    dhidden = dhidden_ref[...]
    square = gate * gate
    wave = jnp.tanh(gate * (GELU_A + GELU_B * square))
    half = 0.5 + 0.5 * wave
    gelu = gate * half
    slope = half + gate * (0.5 - 0.5 * wave * wave) * (GELU_A + 3.0 * GELU_B * square)
    hidden_ref[...] = (gelu * up).astype(BF)
    dpair = jnp.concatenate([(dhidden * up * slope).astype(BF), (dhidden * gelu).astype(BF)], axis=1)
    dpair_ref[...] = dpair
    part_a = dot(dpair, pair_a[...], NT)
    part_b = dot(dpair, pair_b[...], NT)

    @pl.when(step == 0)
    def _():
        second_sum[:, low] = part_a
        second_sum[:, high] = part_b

    @pl.when((step > 0) & (step < FF_TILES - 1))
    def _():
        second_sum[:, low] += part_a
        second_sum[:, high] += part_b

    @pl.when(step == FF_TILES - 1)
    def _():
        second_ref[:, low] = (second_sum[:, low] + part_a).astype(BF)
        second_ref[:, high] = (second_sum[:, high] + part_b).astype(BF)


def mlp(ring, blocks, dhidden, rest_mine, rest_other):
    whole = pl.BlockSpec((ROW, 1536), lambda f, r: (0, 0))
    table = pl.BlockSpec((RING, 1536), lambda f, r: (0, 0))
    half = pl.BlockSpec((RING, 768), lambda f, r: (0, 0))
    unit = pl.BlockSpec((RING, FF_TILE), lambda f, r: (0, f))
    pair_unit = pl.BlockSpec((RING, 2 * FF_TILE), lambda f, r: (0, f))
    pair = pl.BlockSpec((768, 2 * FF_TILE), lambda f, r: (0, 2 + f))
    return call(
        mlp_kernel,
        "mlp",
        [((RING, FF), BF), ((RING, 2 * FF), BF), ((RING, 1536), BF), ((RING, 768), BF), ((RING, 1536), BF)],
        [ring, *blocks, dhidden, rest_mine, rest_other],
        micros=20.0,
        grid=(FF_TILES,),
        in_specs=[whole] * 4 + [unit, pair, pair],
        out_specs=[unit, pair_unit, table, half, table],
        scratch=[pltpu.VMEM((RING, 1536), F32)],
        scalars=1,
    )


def down_project_kernel(hidden_ref, down_a, down_b, out_ref):
    out_ref[:, :768] = dot(hidden_ref[...], down_a[...], NT).astype(BF)
    out_ref[:, 768:] = dot(hidden_ref[...], down_b[...], NT).astype(BF)


def down_project(hidden, rest_mine, rest_other):
    down = pl.BlockSpec((pl.Element(768), pl.Element(FF)), lambda f: (0, 1536 + 2 * FF))
    table = pl.BlockSpec((RING, 1536), lambda f: (0, 0))
    return call(
        down_project_kernel,
        "down_project",
        [((RING, 1536), BF)],
        [hidden, rest_mine, rest_other],
        grid=(1,),
        in_specs=[pl.BlockSpec((RING, FF), lambda f: (0, 0)), down, down],
        out_specs=[table],
    )[0]


def out_grad_kernel(left, left_b, right, right_b, out_ref):
    lefts = jnp.concatenate([left[...], left_b[...]], axis=0)
    rights = jnp.concatenate([right[...], right_b[...]], axis=0)
    out_ref[...] = dot(lefts, rights, TN).astype(BF)


def out_grad(left, left_b, right, right_b, total):
    lefts = pl.BlockSpec((ROW, 768), lambda i: (0, 0))
    rights = pl.BlockSpec((ROW, 384), lambda i: (0, i))
    return pl.pallas_call(
        lambda *refs: out_grad_kernel(*refs[:4], refs[5]),
        grid=(4,),
        in_specs=[lefts, lefts, rights, rights, ANY],
        out_specs=pl.BlockSpec((768, 384), lambda i: (0, 3 * FF // 384 + i)),
        out_shape=jax.ShapeDtypeStruct(total.shape, BF),
        input_output_aliases={4: 0},
        compiler_params=pltpu.CompilerParams(vmem_limit_bytes=VMEM_BYTES),
        cost_estimate=cost(0.01),
        name="out_grad",
    )(left, left_b, right, right_b, total)


def unit_grad_kernel(left, left_b, cot, cot_b, dpair, dpair_b, hidden, hidden_b, out_ref):
    pair = dot(left[...], dpair[...], TN) + dot(left_b[...], dpair_b[...], TN)
    down = dot(cot[...], hidden[...], TN) + dot(cot_b[...], hidden_b[...], TN)
    out_ref[:, : 2 * FF] = pair.astype(BF)
    out_ref[:, 2 * FF :] = down.astype(BF)


def unit_grad(args, needs):
    tile = 256
    left = pl.BlockSpec((RING, tile), lambda i: (0, i))
    return call(
        unit_grad_kernel,
        "unit_grad",
        [((768, 3 * FF + 1536), BF)],
        args,
        needs=needs,
        micros=6.0,
        grid=(768 // tile,),
        in_specs=[left] * 4 + [pl.BlockSpec(a.shape, lambda i: (0, 0)) for a in args[4:]],
        out_specs=[pl.BlockSpec((tile, 3 * FF), lambda i: (i, 0))],
    )


def merge_kernel(*refs):
    out_ref = refs[-1]
    start = 0
    for mine, other in zip(refs[:-1:2], refs[1:-1:2]):
        width = mine.shape[1]
        out_ref[:, start : start + width] = (mine[...].astype(F32) + other[...].astype(F32)).astype(BF)
        start += width


def merge(*pairs, needs=()):
    width = sum(mine.shape[1] for mine, _ in pairs)
    return call(merge_kernel, "merge", [((768, width), BF)], [array for pair in pairs for array in pair], needs)[0]


def normed(rows):
    values = rows.astype(F32)
    inverse = lax.rsqrt(jnp.mean(values * values, axis=-1, keepdims=True) + EPSILON)
    return values, values * inverse, inverse


def norm_back(grad, gain, n, inverse):
    scaled = grad * gain
    return inverse * (scaled - n * jnp.mean(scaled * n, axis=-1, keepdims=True))


def keyval_kernel(ids, own, one, three, mine_ref, other_ref, gain_ref, token_ref, first_ref, keyval_ref):
    head, core = ids[0], ids[1]
    gain_ref[:, :768] = mine_ref[:, 640:].astype(F32).T[:8]
    gain_ref[:, 768:] = other_ref[:, 640:].astype(F32).T[:8]

    def local(block):
        return local_order(block[...].astype(F32), core)

    def project(block):
        first = (normed(block)[1] * gain_ref[0:1, :]).astype(BF)
        total = dot(first[:, :768], mine_ref[:, 384:640]) + dot(first[:, 768:], other_ref[:, 384:640])
        return first, total.astype(BF)

    token = local(own)
    token_ref[...] = token.astype(BF)
    first, total = project(token)
    first_ref[...] = first

    @pl.when(head == 0)
    def _():
        keyval_ref[:ROW, :] = total
        keyval_ref[ROW:, :] = project(local(three))[1]

    @pl.when(head == 1)
    def _():
        keyval_ref[:ROW, :] = project(local(one))[1]
        keyval_ref[ROW:, :] = total


def local_order(rows, core):
    low = jnp.concatenate([rows[:, 384 * z : 384 * z + 192] for z in range(4)], axis=1)
    high = jnp.concatenate([rows[:, 384 * z + 192 : 384 * z + 384] for z in range(4)], axis=1)
    return jnp.concatenate([jnp.where(core == 0, low, high), jnp.where(core == 0, high, low)], axis=1)


def true_order(rows, core):
    low = jnp.where(core == 0, rows[:, :768], rows[:, 768:])
    high = jnp.where(core == 0, rows[:, 768:], rows[:, :768])
    cuts = [half[:, 192 * z : 192 * (z + 1)] for z in range(4) for half in (low, high)]
    return jnp.concatenate(cuts, axis=1)


def order_kernel(core_ref, rows_ref, out_ref, copies):
    rows = local_order(rows_ref[...].astype(F32), core_ref[0]).astype(BF)
    out_ref[...] = rows
    for i in range(4):
        copies[i] = rows


def table_kernel(core_ref, mine_ref, other_ref, table_ref, last_ref):
    @pl.when(core_ref[0] == 0)
    def _():
        table_ref[: 2 * ROW, :] = mine_ref[...]
        table_ref[2 * ROW :, :] = other_ref[...]

    @pl.when(core_ref[0] == 1)
    def _():
        table_ref[: 2 * ROW, :] = other_ref[...]
        table_ref[2 * ROW :, :] = mine_ref[...]

    last_ref[...] = table_ref[512:, :]


def ring_cols(ring, ahead):
    return pl.ds(pl.multiple_of(lax.rem(ring + ahead, 4) * 384, 384), 384)


def turn_kernel(ring_ref, zero, one, two, three, out_ref):
    for ahead, block in enumerate((zero, one, two, three)):
        out_ref[:, ring_cols(ring_ref[0], ahead)] = block[...]


def cut_kernel(rows_ref, out_ref):
    for i in range(4):
        out_ref[i] = rows_ref[:, 384 * i : 384 * (i + 1)]


def query_kernel(ids, first_ref, one, three, two, gain_ref, mine_ref, other_ref, all_ref, *outs_total):
    outs, total = outs_total[:4], outs_total[4]
    core, ring = ids[0], ids[1]
    all_ref[ring_rows(ring, 0), :] = first_ref[...]
    for back, block in ((1, one), (3, three), (2, two)):
        first = normed(local_order(block[...].astype(F32), core))[1] * gain_ref[0:1, :]
        all_ref[ring_rows(ring, back), :] = first.astype(BF)
    rows = all_ref[...]
    total[...] = (dot(rows[:, :768], mine_ref[:, :384]) + dot(rows[:, 768:], other_ref[:, :384])).astype(BF)
    for out, back in zip(outs, BACKS):
        out[...] = total[ring_rows(ring, back), :]


def middle_kernel(attended_ref, mine_ref, other_ref, token_ref, gain_ref, middle_ref, second_ref):
    attended = attended_ref[...]
    branch = jnp.concatenate([dot(attended, mine_ref[...], NT), dot(attended, other_ref[...], NT)], axis=1)
    middle = token_ref[...].astype(F32) + branch
    middle_ref[...] = middle
    second_ref[...] = (normed(middle)[1] * gain_ref[1:2, :]).astype(BF)


def middle_back_kernel(
    parts, middle_ref, cot_ref, gain_ref, mine_ref, other_ref, grad_ref, low_ref, high_ref, terms_ref, attended_ref
):
    grad_second = sum(parts[i].astype(F32) for i in range(4))
    _, n2, rs2 = normed(middle_ref[...])
    grad_middle = cot_ref[...].astype(F32) + norm_back(grad_second, gain_ref[1:2, :], n2, rs2)
    grad_ref[...] = grad_middle
    low = grad_middle.astype(BF)
    low_ref[...] = low[:, :768]
    high_ref[...] = low[:, 768:]
    terms_ref[...] = (grad_second * n2).astype(BF)
    attended_ref[...] = (dot(low[:, :768], mine_ref[...]) + dot(low[:, 768:], other_ref[...])).astype(BF)


def first_back_kernel(
    ring_ref, dqueries, home_6, home_5, home_4, home_3, home_2, home_1, home_0, rest_a, rest_b, first_ref,
    second_terms, mlp_out, own_ref, one, three, two, tail_a, tail_b, sums, partial,
):
    ring = ring_ref[0]
    dquery = jnp.concatenate([dqueries[i] for i in range(4)], axis=0)
    sums[...] = sum(home[...].astype(F32) for home in (home_5, home_4, home_3, home_2, home_1, home_0))
    sums[128:, :] += home_6[...].astype(F32)
    dkeyval = sums[...].astype(BF)
    column = lax.broadcasted_iota(jnp.int32, (RING + ROW, 128), 1)
    row = lax.broadcasted_iota(jnp.int32, (RING + ROW, 128), 0)
    picks = jnp.where(column == (row >= RING).astype(jnp.int32), 1.0, 0.0).astype(BF)
    own_rows = ring_rows(ring, 0)
    for cols, rest, tail in ((slice(0, 768), rest_a, tail_a), (slice(768, 1536), rest_b, tail_b)):
        partial[...] = dot(dquery, rest[:, :384], NT)
        partial[own_rows, :] += dot(dkeyval, rest[:, 384:640], NT)
        own_ref[:, cols] = partial[own_rows, :]
        for back, ref in ((1, one), (3, three), (2, two)):
            ref[0, :, cols] = partial[ring_rows(ring, back), :].astype(BF)
            ref[1, :, cols] = mlp_out[ring_rows(ring, back), cols]
        first = first_ref[:, cols]
        terms = jnp.concatenate([(partial[...] * first.astype(F32)).astype(BF), second_terms[:, cols]], axis=0)
        tail[:, :384] = dot(first, dquery, TN).astype(BF)
        tail[:, 384:640] = dot(first_ref[own_rows, cols], dkeyval, TN).astype(BF)
        tail[:, 640:] = dot(terms, picks, TN).astype(BF)


def finish_kernel(
    ids, own_ref, one, three, two, token_ref, gain_ref, grad_ref, middle_ref, mlp_ref, input_ref, block_ref
):
    core, ring = ids[0], ids[1]
    grad_first = own_ref[...] + sum(part[0].astype(F32) for part in (one, three, two))
    _, n1, rs1 = normed(token_ref[...])
    total = grad_ref[...] + norm_back(grad_first, gain_ref[0:1, :], n1, rs1)
    input_ref[...] = true_order(total, core).astype(BF)
    total = middle_ref[...] + mlp_ref[ring_rows(ring, 0), :].astype(F32)
    total = total + sum(part[1].astype(F32) for part in (one, three, two))
    block_ref[...] = true_order(total, core).astype(BF)


def tail_kernel(core_ref, parts, out_ref):
    total = sum(parts[i].astype(F32) for i in range(16))
    out_ref[...] = jnp.zeros_like(out_ref)
    for xh in range(2):
        keep = jnp.where(core_ref[0] == xh, 1.0, 0.0)
        for i in range(4):
            out_ref[4 * xh + i, :12, :768] = (total[12 * i : 12 * (i + 1)] * keep).astype(BF)


def deal_kernel(ids, owned_ref, give_a, give_b, cross_a, cross_b):
    head, xh = ids[0], ids[1]
    start = 3 * FF

    def rows(cols, flip):
        block = owned_ref[:, cols].astype(F32)
        return jnp.where((xh == 0) != flip, block[:24], block[24:]).astype(BF)

    def part(chip):
        return pl.ds(pl.multiple_of(start + 384 * chip, 384), 384)

    for flip, give, cross in ((False, give_a, cross_a), (True, give_b, cross_b)):
        give[:, :start] = rows(slice(0, start), flip)
        for i in range(2):
            give[:, start + 384 * i : start + 384 * (i + 1)] = rows(part(2 * i + head), flip)
            cross[:, 384 * i : 384 * (i + 1)] = rows(part(2 * i + 1 - head), flip)


def final_kernel(ids, tail, got_a, got_b, cross_a, cross_b, gain_own, query_ref, key_ref, value_ref, gain_ref, out_ref, gate_ref,
                 up_ref, down_ref):
    core, xh = ids[0], ids[1]
    total = jnp.zeros((12, 384), F32)
    for xh_from in range(2):
        for head in range(2):
            block = tail[4 * xh_from + 2 * xh + head].astype(F32)[:12]
            quarter = 2 * head + xh_from
            query_ref[:, 384 * quarter : 384 * (quarter + 1)] = block[:, :384]
            total = total + block[:, 384:768]
    key_ref[...] = total[:, :HD]
    value_ref[...] = total[:, HD : 2 * HD]
    sums = jnp.concatenate([total[:, 2 * HD :], jnp.zeros((4, HD), F32)], axis=0).T
    gain_ref[0:1, :] = sums[0:1, :12] / gain_own[...]
    gain_ref[1:2, :] = sums[1:2, :12]
    first, second = got_a[...].astype(F32), got_b[...].astype(F32)
    halves = (jnp.where(core == 0, first, second), jnp.where(core == 0, second, first))
    for i, half in enumerate(halves):
        for f in range(FF_TILES):
            place = slice(FF * i + FF_TILE * f, FF * i + FF_TILE * (f + 1))
            gate_ref[:, place] = half[:, 2 * FF_TILE * f : 2 * FF_TILE * f + FF_TILE]
            up_ref[:, place] = half[:, 2 * FF_TILE * f + FF_TILE : 2 * FF_TILE * (f + 1)]
        down_ref[:, FF * i : FF * (i + 1)] = half[:, 2 * FF : 3 * FF]
    out_ref[...] = (
        halves[0][:, 3 * FF :] + halves[1][:, 3 * FF :] + cross_a[...].astype(F32) + cross_b[...].astype(F32)
    )


def turn_xc(block, flip, cross, back=False):
    route = []
    for xh in range(2):
        for core in range(2):
            for head in range(2):
                target = (core ^ flip) * 4 + xh * 2 + (head ^ cross)
                source = xh * 4 + core * 2 + head
                route.append((target, source) if back else (source, target))
    return lax.ppermute(block, ("xh", "core", "head"), route)


def shift_all(block, distance):
    count = 128
    route = [(i, i + distance) for i in range(count) if 0 <= i + distance < count]
    return lax.ppermute(block, AXES, route)


def shift_groups(block, distance):
    return lax.ppermute(block, ("z", "xh", "y"), [(i, i + distance) for i in range(32 - distance)])


def shift_x(block, distance):
    return lax.ppermute(block, CHIPS_X, [(i, (i + distance) % 4) for i in range(4)])


def swap(block, axis):
    return lax.ppermute(block, axis, [(0, 1), (1, 0)])


def shards(tokens, cotangent, w_query, w_key, w_value, w_out, w_gate, w_up, w_down, gain_attn, gain_mlp):
    core = lax.axis_index("core")
    xh = lax.axis_index("xh")
    head = lax.axis_index("head")
    ring = 2 * xh + head
    place = jnp.stack([lax.axis_index(AXES), 2 * core + head]).astype(jnp.int32)
    ring_scalar, core_scalar, head_scalar = (i.astype(jnp.int32).reshape(1) for i in (ring, core, head))
    eight = ("xh", "core", "head")

    def ordered(index, first, second, axis):
        return jnp.concatenate(
            [jnp.where(index == 0, first, second), jnp.where(index == 0, second, first)], axis=axis
        )

    def spread(piece):
        sent = jnp.broadcast_to(piece[None], (16,) + piece.shape)
        return lax.all_to_all(sent, PLANE, 0, 0, tiled=True).reshape(768, -1)

    def gather(piece):
        return lax.all_gather(piece, PLANE, axis=0, tiled=True)

    gains = jnp.pad(jnp.stack([gain_attn, gain_mlp], axis=1), ((0, 0), (0, 126)))
    query_cut = w_query.reshape(12, 2, 2, 384).transpose(2, 1, 0, 3)
    common = jnp.broadcast_to(jnp.concatenate([w_key, w_value, gains], axis=1), (2, 2, 12, 384))
    own_qkv = jnp.concatenate([query_cut, common], axis=3)
    own_qkv = jnp.broadcast_to(own_qkv[:, None], (2, 2, 2, 12, 768)).reshape(8, 12, 768)
    got = lax.all_to_all(own_qkv, eight, 0, 0, tiled=True)
    qkv_piece = lax.dynamic_slice_in_dim(got, core * 4, 4, 0).reshape(48, 768)
    token_1, token_3, token_2 = (shift_x(tokens, k) for k in (1, 3, 2))
    qkv_mine = spread(qkv_piece)
    cot_own, cot_sent = call(
        order_kernel,
        "order",
        [((ROW, 1536), BF), ((4, ROW, 1536), BF)],
        [core_scalar, cotangent],
        scalars=1,
    )
    (cot_sent,) = after([cot_sent], qkv_mine)
    cots = lax.all_to_all(cot_sent, CHIPS_X, 0, 0, tiled=True).reshape(RING, 1536)
    (qkv_mine,) = after([qkv_mine], token_1, token_3, token_2)

    pair_cut = jnp.stack([w_gate, w_up], axis=1).reshape(24, 2, 2, FF_TILES, FF_TILE)
    pair_cut = pair_cut.transpose(2, 0, 3, 1, 4).reshape(2, 24, 2 * FF)
    down_cut = w_down.T.reshape(24, 2, FF).transpose(1, 0, 2)
    own_mlp = jnp.concatenate([pair_cut, down_cut], axis=2)
    sent_a = jnp.where(core == 0, own_mlp[0], own_mlp[1])
    sent_b = jnp.where(core == 0, own_mlp[1], own_mlp[0])
    out_low = w_out.T
    got_a = turn_xc(jnp.concatenate([out_low, sent_a], axis=1), False, False)
    got_b = turn_xc(jnp.concatenate([out_low, sent_b], axis=1), True, False)
    cross_a, cross_b = turn_xc(out_low, False, True), turn_xc(out_low, True, True)
    out_same = ordered(xh, got_a[:, :768], got_b[:, :768], 0).reshape(48, 2, 1, 384)
    out_cross = ordered(xh, cross_a, cross_b, 0).reshape(48, 2, 1, 384)
    out_piece = ordered(head, out_same, out_cross, 2).reshape(48, 1536)
    mlp_piece = ordered(xh, got_a[:, 768:], got_b[:, 768:], 0)
    (rest_piece,) = after([jnp.concatenate([out_piece, mlp_piece], axis=1)], qkv_piece)
    rest_mine = gather(rest_piece)

    qkv_other = swap(qkv_mine, "core")
    gain_rows, token_own, first_own, keyval_pair = call(
        keyval_kernel,
        "keyval",
        [((8, 1536), F32), ((ROW, 1536), BF), ((ROW, 1536), BF), ((2 * ROW, 256), BF)],
        [jnp.concatenate([head_scalar, core_scalar]), tokens, token_1, token_3, qkv_mine, qkv_other],
        scalars=1,
    )
    here, last = call(
        table_kernel,
        "table",
        [((768, 256), BF), ((256, 256), BF)],
        [core_scalar, keyval_pair, swap(keyval_pair, "core")],
        scalars=1,
    )
    near, far = shift_groups(here, 1), shift_groups(last, 2)
    first_all, query_0, ring_1, ring_3, ring_2 = call(
        query_kernel,
        "query",
        [((RING, 1536), BF)] + [((ROW, 384), BF)] * 4,
        [jnp.concatenate([core_scalar, ring_scalar]), first_own, token_1, token_3, token_2, gain_rows, qkv_mine, qkv_other],
        scratch=[pltpu.VMEM((RING, 384), BF)],
        scalars=1,
        needs=[here],
    )
    query_1, query_3, query_2 = shift_x(ring_1, -1), shift_x(ring_3, -3), shift_x(ring_2, -2)
    (queries,) = call(
        turn_kernel, "turn", [((ROW, 1536), BF)], [ring_scalar, query_0, query_1, query_2, query_3], scalars=1
    )
    (rest_mine,) = after([rest_mine], queries, near, far, cots)
    out_mine = rest_mine[:, :1536]
    attended, probs, keyval = attend(place, queries, far, near, here, [out_mine])

    out_other = swap(out_mine, "core")
    middle, second_own = call(
        middle_kernel,
        "middle",
        [((ROW, 1536), F32), ((ROW, 1536), BF)],
        [attended, out_mine, out_other, token_own, gain_rows],
    )
    blocks = [second_own] + [shift_x(second_own, k) for k in (1, 3, 2)]
    (rest_mine,) = after([rest_mine], attended, out_other)
    rest_other = swap(rest_mine, "core")
    dhidden = down_back(cots, rest_mine, rest_other)

    hidden, dpair, seconds, seconds_b, second_part = mlp(ring_scalar, blocks, dhidden, rest_mine, rest_other)
    second_home = lax.all_to_all(second_part.reshape(4, ROW, 1536), CHIPS_X, 0, 0, tiled=True)

    def planes(total):
        got = lax.all_to_all(total.reshape(16, 48, -1), PLANE, 0, 0, tiled=True)
        return jnp.sum(got.astype(F32), axis=0).astype(BF)

    mlp_out = down_project(hidden, rest_mine, rest_other)
    (unit_total,) = unit_grad(
        [seconds, swap(seconds_b, "core"), cots, swap(cots[:, 768:], "core")]
        + [dpair, swap(dpair, "core"), hidden, swap(hidden, "core")],
        [mlp_out],
    )
    grad_middle, branch_a, branch_b, second_terms, grad_attended = call(
        middle_back_kernel,
        "middle_back",
        [((ROW, 1536), F32), ((ROW, 768), BF), ((ROW, 768), BF), ((ROW, 1536), BF), ((ROW, 1536), BF)],
        [second_home, middle, cot_own, gain_rows, out_mine, out_other],
        needs=[unit_total],
    )
    dqueries, *homes = attend_back(queries, keyval, attended, grad_attended, probs, [])

    (dquery_cut,) = call(cut_kernel, "cut", [((4, ROW, 384), BF)], [dqueries])
    dquery_ring = lax.all_to_all(dquery_cut, CHIPS_X, 0, 0, tiled=True)
    homes = [shift_all(home, -k) for home, k in zip(homes, (6, 5, 4, 3, 2, 1))] + [homes[6]]
    total = out_grad(branch_a, swap(branch_b, "core"), attended, swap(attended, "core"), unit_total)
    owned = lax.psum_scatter(total, PLANE, scatter_dimension=0, tiled=True)
    own_first, first_1, first_3, first_2, tail_mine, tail_other = call(
        first_back_kernel,
        "first_back",
        [((ROW, 1536), F32)] + [((2, ROW, 1536), BF)] * 3 + [((768, 768), BF)] * 2,
        [
            ring_scalar, dquery_ring, *homes, qkv_mine, qkv_other, first_all, second_terms,
            mlp_out,
        ],
        scratch=[pltpu.VMEM((ROW, 256), F32), pltpu.VMEM((RING, 768), F32)],
        scalars=1,
    )
    tail_total = merge((tail_mine, swap(tail_other, "core")))
    tail_parts = lax.all_to_all(tail_total.reshape(16, 48, 768), PLANE, 0, 0, tiled=True)
    first_1, first_3, first_2 = shift_x(first_1, -1), shift_x(first_3, -3), shift_x(first_2, -2)
    input_grad, block_out = call(
        finish_kernel,
        "finish",
        [((ROW, 1536), BF)] * 2,
        [jnp.concatenate([core_scalar, ring_scalar]), own_first, first_1, first_3, first_2, token_own, gain_rows]
        + [grad_middle, middle, mlp_out],
        micros=20.0,
        scalars=1,
    )
    (tail_sent,) = call(tail_kernel, "tail", [((8, 16, 1024), BF)], [core_scalar, tail_parts], scalars=1)
    tail_got = lax.all_to_all(tail_sent, eight, 0, 0, tiled=True)
    give_a, give_b, cross_a, cross_b = call(
        deal_kernel,
        "deal",
        [((24, 3 * FF + 768), BF)] * 2 + [((24, 768), BF)] * 2,
        [jnp.concatenate([head_scalar, xh.astype(jnp.int32).reshape(1)]), owned],
        needs=[tail_sent],
        scalars=1,
    )
    got_a, got_b = turn_xc(give_a, False, False, True), turn_xc(give_b, True, False, True)
    cross_a, cross_b = turn_xc(cross_a, False, True, True), turn_xc(cross_b, True, True, True)
    query_grad, key_grad, value_grad, gain_grads, out_grad_own, gate_grad, up_grad, down_grad = call(
        final_kernel,
        "final",
        [((12, 1536), F32)] + [((12, 128), F32)] * 2 + [((2, 12), F32), ((24, 768), F32)] + [((24, 2 * FF), F32)] * 3,
        [jnp.concatenate([core_scalar, xh.astype(jnp.int32).reshape(1)]), tail_got, got_a, got_b, cross_a, cross_b]
        + [gain_attn.astype(F32).reshape(1, 12)],
        needs=[input_grad, block_out],
        scalars=1,
    )
    return (
        block_out,
        input_grad,
        query_grad,
        key_grad,
        value_grad,
        out_grad_own.T,
        gate_grad,
        up_grad,
        down_grad.T,
        gain_grads[0],
        gain_grads[1],
    )


def solution(mesh):
    grid = Mesh(mesh.devices.reshape(SIZES), AXES)
    seq = ("z", "xh", "y", "core")
    rows, both, cols = P(AXES, None), P(seq, "head"), P("head", seq)
    in_specs = (rows, rows, rows, rows, rows, cols, both, both, cols, P(AXES), P(AXES))
    out_specs = (rows, rows, rows, rows, rows, cols, both, both, cols, P(AXES), P(AXES))
    return jax.shard_map(shards, mesh=grid, in_specs=in_specs, out_specs=out_specs, check_vma=False)
```

```python
import functools
import jax
import jax.numpy as jnp
from jax import lax
from jax.experimental import pallas as pl
from jax.experimental.pallas import tpu as pltpu
from jax.sharding import Mesh
from jax.sharding import PartitionSpec as P

WINDOW = 1024
EPSILON = 1e-06
AXES = ("z", "xh", "y", "core", "head")
SIZES = (4, 2, 4, 2, 2)
CHIPS_X = ("xh", "head")
PLANE = ("z", "y")
ROW = 192
KEYS = 1216
HEADS = 12
PAIRS = 2
HD = 128
BF = jnp.bfloat16
F32 = jnp.float32
NEG = -1e30
SCALE = HD ** (-0.5)
LOG2E = 1.4426950408889634
VMEM_BYTES = 56 * 1024 * 1024
FF = 1152
FF_TILES = 3
FF_TILE = 384
RING = 768
GELU_A = 0.7978845608028654
GELU_B = GELU_A * 0.044715

NN = (((1,), (0,)), ((), ()))
NT = (((1,), (1,)), ((), ()))
TN = (((0,), (0,)), ((), ()))


def dot(a, b, dims=NN):
    return lax.dot_general(a, b, dims, preferred_element_type=F32)


ANY = pl.BlockSpec(memory_space=pl.ANY)


def cost(micros):
    return pl.CostEstimate(flops=int(micros * 1.0e9), bytes_accessed=1000000, transcendentals=0)


def call(kernel, name, outs, args, needs=(), micros=0.01, grid=None, in_specs=None, out_specs=None, scratch=(), scalars=0):
    count = len(args)

    def body(*refs):
        kernel(*refs[:count], *refs[count + len(needs) :])

    if in_specs is None:
        whole = pl.BlockSpec(memory_space=pltpu.VMEM)
        in_specs = [pl.BlockSpec(memory_space=pltpu.SMEM)] * scalars + [whole] * (count - scalars)
        out_specs = [whole] * len(outs)
        spec = dict(in_specs=in_specs + [ANY] * len(needs), out_specs=out_specs, scratch_shapes=list(scratch))
    else:
        spec = dict(
            grid_spec=pltpu.PrefetchScalarGridSpec(
                num_scalar_prefetch=scalars,
                grid=grid,
                in_specs=in_specs + [ANY] * len(needs),
                out_specs=out_specs,
                scratch_shapes=list(scratch),
            )
        )
    return pl.pallas_call(
        body,
        out_shape=[jax.ShapeDtypeStruct(shape, kind) for shape, kind in outs],
        compiler_params=pltpu.CompilerParams(vmem_limit_bytes=VMEM_BYTES),
        cost_estimate=cost(micros),
        name=name,
        **spec,
    )(*args, *needs)


def after(values, *needs):
    count = len(values)
    return pl.pallas_call(
        lambda *refs: None,
        in_specs=[ANY] * (count + len(needs)),
        out_specs=[ANY] * count,
        out_shape=[jax.ShapeDtypeStruct(value.shape, value.dtype) for value in values],
        input_output_aliases={i: i for i in range(count)},
        cost_estimate=cost(0.01),
        name="after",
    )(*values, *needs)


def two_heads(pair):
    return jnp.concatenate([pair[:, :HD], pair[:, HD:]], axis=0)


def attend_kernel(place_ref, q_ref, far_ref, near_ref, here_ref, out_ref, probs_ref, kv_ref, bias, table):
    @pl.when(pl.program_id(0) == 0)
    def _():
        key = lax.broadcasted_iota(jnp.int32, (KEYS, ROW), 0)
        query = lax.broadcasted_iota(jnp.int32, (KEYS, ROW), 1)
        first = WINDOW - ROW * place_ref[0]
        inside = (key > query) & (key <= query + WINDOW) & (key >= first)
        one = jnp.where(inside, 0.0, NEG)
        bias[:, :] = jnp.concatenate([one, one], axis=1)
        table[:256, :] = far_ref[...]
        table[256:1024, :] = near_ref[...]
        table[1024:, :] = here_ref[...]
        kv_ref[...] = table[pl.ds(pl.multiple_of(place_ref[1] * ROW, ROW), KEYS), :]

    tables = [
        dot(kv_ref[:, :HD], two_heads(q_ref[:, 2 * HD * i : 2 * HD * (i + 1)]), NT) for i in range(PAIRS)
    ]
    for i, table in enumerate(tables):
        scores = table + bias[...]
        highest = jnp.max(scores, axis=0, keepdims=True)
        powers = jnp.exp2((scores - highest) * (SCALE * LOG2E))
        total = jnp.sum(powers, axis=0, keepdims=True)
        probs = (powers * (1.0 / total)).astype(BF)
        probs_ref[i] = probs
        mixed = dot(kv_ref[:, HD:], probs, TN).T.astype(BF)
        out_ref[:, 2 * HD * i : 2 * HD * (i + 1)] = jnp.concatenate([mixed[:ROW], mixed[ROW:]], axis=1)


def attend(place, queries, far, near, here, needs):
    pair = pl.BlockSpec((ROW, 2 * HD * PAIRS), lambda h, b: (0, h))

    def fixed(rows):
        return pl.BlockSpec((rows, 2 * HD), lambda h, b: (0, 0))

    return call(
        attend_kernel,
        "attend",
        [((ROW, HEADS * HD), BF), ((HEADS // 2, KEYS, 2 * ROW), BF), ((KEYS, 2 * HD), BF)],
        [place, queries, far, near, here],
        needs=needs,
        micros=10.0,
        grid=(HEADS // 2 // PAIRS,),
        in_specs=[pair, fixed(256), fixed(768), fixed(768)],
        out_specs=[pair, pl.BlockSpec((PAIRS, KEYS, 2 * ROW), lambda h, b: (h, 0, 0)), fixed(KEYS)],
        scratch=[pltpu.VMEM((KEYS, 2 * ROW), F32), pltpu.VMEM((1792, 2 * HD), BF)],
        scalars=1,
    )


HOME_ROWS = [slice(0, 64)] + [slice(64 + ROW * i, 64 + ROW * (i + 1)) for i in range(6)]


def attend_back_kernel(q_ref, kv_ref, out_ref, grad_ref, probs_ref, dq_ref, *rest):
    homes, (dk, dv) = rest[:7], rest[7:]
    step = pl.program_id(0)

    @pl.when(step == 0)
    def _():
        dk[...] = jnp.zeros_like(dk)
        dv[...] = jnp.zeros_like(dv)

    pairs = [slice(2 * HD * i, 2 * HD * (i + 1)) for i in range(PAIRS)]
    tables = [dot(kv_ref[:, HD:], two_heads(grad_ref[:, pair]), NT) for pair in pairs]
    for i, (pair, dprobs) in enumerate(zip(pairs, tables)):
        queries = two_heads(q_ref[:, pair])
        grads = two_heads(grad_ref[:, pair])
        outs = two_heads(out_ref[:, pair])
        probs = probs_ref[i]
        delta = jnp.sum((grads.astype(F32) * outs.astype(F32)).T, axis=0, keepdims=True)
        dscores = (probs.astype(F32) * (dprobs - delta)).astype(BF)
        dqueries = (dot(kv_ref[:, :HD], dscores, TN).T * SCALE).astype(BF)
        dq_ref[:, pair] = jnp.concatenate([dqueries[:ROW], dqueries[ROW:]], axis=1)
        dk[...] += dot(dscores, queries)
        dv[...] += dot(probs, grads)

    @pl.when(step == HEADS // 2 // PAIRS - 1)
    def _():
        for home, rows in zip(homes, HOME_ROWS):
            home[:, :HD] = (dk[rows, :] * SCALE).astype(BF)
            home[:, HD:] = dv[rows, :].astype(BF)


def attend_back(queries, keyval, attended, grads, probs, needs):
    pair = pl.BlockSpec((ROW, 2 * HD * PAIRS), lambda h: (0, h))
    table = pl.BlockSpec((KEYS, 2 * HD), lambda h: (0, 0))

    def home(rows):
        return pl.BlockSpec((rows, 2 * HD), lambda h: (0, 0))

    return call(
        attend_back_kernel,
        "attend_back",
        [((ROW, HEADS * HD), BF), ((64, 2 * HD), BF)] + [((ROW, 2 * HD), BF)] * 6,
        [queries, keyval, attended, grads, probs],
        needs=needs,
        micros=0.01,
        grid=(HEADS // 2 // PAIRS,),
        in_specs=[pair, table, pair, pair, pl.BlockSpec((PAIRS, KEYS, 2 * ROW), lambda h: (h, 0, 0))],
        out_specs=[pair, home(64)] + [home(ROW)] * 6,
        scratch=[pltpu.VMEM((KEYS, HD), F32), pltpu.VMEM((KEYS, HD), F32)],
    )


def down_back_kernel(cots, down_a, down_b, out_ref):
    out_ref[...] = dot(cots[:, :768], down_a[...]) + dot(cots[:, 768:], down_b[...])


def down_back(cots, rest_mine, rest_other):
    down = pl.BlockSpec((768, FF_TILE), lambda f: (0, 10 + f))
    return call(
        down_back_kernel,
        "down_back",
        [((RING, FF), F32)],
        [cots, rest_mine, rest_other],
        micros=6.0,
        grid=(FF_TILES,),
        in_specs=[pl.BlockSpec((RING, 1536), lambda f: (0, 0)), down, down],
        out_specs=[pl.BlockSpec((RING, FF_TILE), lambda f: (0, f))],
    )[0]


def ring_rows(ring, back):
    return pl.ds(pl.multiple_of(lax.rem(ring + 4 - back, 4) * ROW, ROW), ROW)


BACKS = (0, 1, 3, 2)


def mlp_kernel(
    ring_ref, zero, one, three, two, dhidden_ref, pair_a, pair_b, hidden_ref, dpair_ref, rows, rows_b, second_ref,
    second_sum
):
    @pl.when(pl.program_id(0) == 0)
    def _():
        for block, back in zip((zero, one, three, two), BACKS):
            rows[ring_rows(ring_ref[0], back), :] = block[...]
            rows_b[ring_rows(ring_ref[0], back), :] = block[:, 768:]

    step = pl.program_id(0)
    low, high = slice(0, 768), slice(768, 1536)
    both = dot(rows[:, low], pair_a[...]) + dot(rows[:, high], pair_b[...])
    gate, up = both[:, :FF_TILE], both[:, FF_TILE:]
    dhidden = dhidden_ref[...]
    square = gate * gate
    wave = jnp.tanh(gate * (GELU_A + GELU_B * square))
    half = 0.5 + 0.5 * wave
    gelu = gate * half
    slope = half + gate * (0.5 - 0.5 * wave * wave) * (GELU_A + 3.0 * GELU_B * square)
    hidden_ref[...] = (gelu * up).astype(BF)
    dpair = jnp.concatenate([(dhidden * up * slope).astype(BF), (dhidden * gelu).astype(BF)], axis=1)
    dpair_ref[...] = dpair
    part_a = dot(dpair, pair_a[...], NT)
    part_b = dot(dpair, pair_b[...], NT)

    @pl.when(step == 0)
    def _():
        second_sum[:, low] = part_a
        second_sum[:, high] = part_b

    @pl.when((step > 0) & (step < FF_TILES - 1))
    def _():
        second_sum[:, low] += part_a
        second_sum[:, high] += part_b

    @pl.when(step == FF_TILES - 1)
    def _():
        second_ref[:, low] = (second_sum[:, low] + part_a).astype(BF)
        second_ref[:, high] = (second_sum[:, high] + part_b).astype(BF)


def mlp(ring, blocks, dhidden, rest_mine, rest_other):
    whole = pl.BlockSpec((ROW, 1536), lambda f, r: (0, 0))
    table = pl.BlockSpec((RING, 1536), lambda f, r: (0, 0))
    half = pl.BlockSpec((RING, 768), lambda f, r: (0, 0))
    unit = pl.BlockSpec((RING, FF_TILE), lambda f, r: (0, f))
    pair_unit = pl.BlockSpec((RING, 2 * FF_TILE), lambda f, r: (0, f))
    pair = pl.BlockSpec((768, 2 * FF_TILE), lambda f, r: (0, 2 + f))
    return call(
        mlp_kernel,
        "mlp",
        [((RING, FF), BF), ((RING, 2 * FF), BF), ((RING, 1536), BF), ((RING, 768), BF), ((RING, 1536), BF)],
        [ring, *blocks, dhidden, rest_mine, rest_other],
        micros=20.0,
        grid=(FF_TILES,),
        in_specs=[whole] * 4 + [unit, pair, pair],
        out_specs=[unit, pair_unit, table, half, table],
        scratch=[pltpu.VMEM((RING, 1536), F32)],
        scalars=1,
    )


def down_project_kernel(hidden_ref, down_a, down_b, out_ref):
    out_ref[:, :768] = dot(hidden_ref[...], down_a[...], NT).astype(BF)
    out_ref[:, 768:] = dot(hidden_ref[...], down_b[...], NT).astype(BF)


def down_project(hidden, rest_mine, rest_other):
    down = pl.BlockSpec((pl.Element(768), pl.Element(FF)), lambda f: (0, 1536 + 2 * FF))
    table = pl.BlockSpec((RING, 1536), lambda f: (0, 0))
    return call(
        down_project_kernel,
        "down_project",
        [((RING, 1536), BF)],
        [hidden, rest_mine, rest_other],
        grid=(1,),
        in_specs=[pl.BlockSpec((RING, FF), lambda f: (0, 0)), down, down],
        out_specs=[table],
    )[0]


def out_grad_kernel(left, left_b, right, right_b, out_ref):
    lefts = jnp.concatenate([left[...], left_b[...]], axis=0)
    rights = jnp.concatenate([right[...], right_b[...]], axis=0)
    out_ref[...] = dot(lefts, rights, TN).astype(BF)


def out_grad(left, left_b, right, right_b, total):
    lefts = pl.BlockSpec((ROW, 768), lambda i: (0, 0))
    rights = pl.BlockSpec((ROW, 384), lambda i: (0, i))
    return pl.pallas_call(
        lambda *refs: out_grad_kernel(*refs[:4], refs[5]),
        grid=(4,),
        in_specs=[lefts, lefts, rights, rights, ANY],
        out_specs=pl.BlockSpec((768, 384), lambda i: (0, 3 * FF // 384 + i)),
        out_shape=jax.ShapeDtypeStruct(total.shape, BF),
        input_output_aliases={4: 0},
        compiler_params=pltpu.CompilerParams(vmem_limit_bytes=VMEM_BYTES),
        cost_estimate=cost(0.01),
        name="out_grad",
    )(left, left_b, right, right_b, total)


def unit_grad_kernel(left, left_b, cot, cot_b, dpair, dpair_b, hidden, hidden_b, out_ref):
    pair = dot(left[...], dpair[...], TN) + dot(left_b[...], dpair_b[...], TN)
    down = dot(cot[...], hidden[...], TN) + dot(cot_b[...], hidden_b[...], TN)
    out_ref[:, : 2 * FF] = pair.astype(BF)
    out_ref[:, 2 * FF :] = down.astype(BF)


def unit_grad(args, needs):
    tile = 256
    left = pl.BlockSpec((RING, tile), lambda i: (0, i))
    return call(
        unit_grad_kernel,
        "unit_grad",
        [((768, 3 * FF + 1536), BF)],
        args,
        needs=needs,
        micros=6.0,
        grid=(768 // tile,),
        in_specs=[left] * 4 + [pl.BlockSpec(a.shape, lambda i: (0, 0)) for a in args[4:]],
        out_specs=[pl.BlockSpec((tile, 3 * FF), lambda i: (i, 0))],
    )


def merge_kernel(*refs):
    out_ref = refs[-1]
    start = 0
    for mine, other in zip(refs[:-1:2], refs[1:-1:2]):
        width = mine.shape[1]
        out_ref[:, start : start + width] = (mine[...].astype(F32) + other[...].astype(F32)).astype(BF)
        start += width


def merge(*pairs, needs=()):
    width = sum(mine.shape[1] for mine, _ in pairs)
    return call(merge_kernel, "merge", [((768, width), BF)], [array for pair in pairs for array in pair], needs)[0]


def normed(rows):
    values = rows.astype(F32)
    inverse = lax.rsqrt(jnp.mean(values * values, axis=-1, keepdims=True) + EPSILON)
    return values, values * inverse, inverse


def norm_back(grad, gain, n, inverse):
    scaled = grad * gain
    return inverse * (scaled - n * jnp.mean(scaled * n, axis=-1, keepdims=True))


def keyval_kernel(ids, own, one, three, mine_ref, other_ref, gain_ref, token_ref, first_ref, keyval_ref):
    head, core = ids[0], ids[1]
    gain_ref[:, :768] = mine_ref[:, 640:].astype(F32).T[:8]
    gain_ref[:, 768:] = other_ref[:, 640:].astype(F32).T[:8]

    def local(block):
        return local_order(block[...].astype(F32), core)

    def project(block):
        first = (normed(block)[1] * gain_ref[0:1, :]).astype(BF)
        total = dot(first[:, :768], mine_ref[:, 384:640]) + dot(first[:, 768:], other_ref[:, 384:640])
        return first, total.astype(BF)

    token = local(own)
    token_ref[...] = token.astype(BF)
    first, total = project(token)
    first_ref[...] = first

    @pl.when(head == 0)
    def _():
        keyval_ref[:ROW, :] = total
        keyval_ref[ROW:, :] = project(local(three))[1]

    @pl.when(head == 1)
    def _():
        keyval_ref[:ROW, :] = project(local(one))[1]
        keyval_ref[ROW:, :] = total


def local_order(rows, core):
    low = jnp.concatenate([rows[:, 384 * z : 384 * z + 192] for z in range(4)], axis=1)
    high = jnp.concatenate([rows[:, 384 * z + 192 : 384 * z + 384] for z in range(4)], axis=1)
    return jnp.concatenate([jnp.where(core == 0, low, high), jnp.where(core == 0, high, low)], axis=1)


def true_order(rows, core):
    low = jnp.where(core == 0, rows[:, :768], rows[:, 768:])
    high = jnp.where(core == 0, rows[:, 768:], rows[:, :768])
    cuts = [half[:, 192 * z : 192 * (z + 1)] for z in range(4) for half in (low, high)]
    return jnp.concatenate(cuts, axis=1)


def order_kernel(core_ref, rows_ref, out_ref, copies):
    rows = local_order(rows_ref[...].astype(F32), core_ref[0]).astype(BF)
    out_ref[...] = rows
    for i in range(4):
        copies[i] = rows


def table_kernel(core_ref, mine_ref, other_ref, table_ref, last_ref):
    @pl.when(core_ref[0] == 0)
    def _():
        table_ref[: 2 * ROW, :] = mine_ref[...]
        table_ref[2 * ROW :, :] = other_ref[...]

    @pl.when(core_ref[0] == 1)
    def _():
        table_ref[: 2 * ROW, :] = other_ref[...]
        table_ref[2 * ROW :, :] = mine_ref[...]

    last_ref[...] = table_ref[512:, :]


def ring_cols(ring, ahead):
    return pl.ds(pl.multiple_of(lax.rem(ring + ahead, 4) * 384, 384), 384)


def turn_kernel(ring_ref, zero, one, two, three, out_ref):
    for ahead, block in enumerate((zero, one, two, three)):
        out_ref[:, ring_cols(ring_ref[0], ahead)] = block[...]


def cut_kernel(rows_ref, out_ref):
    for i in range(4):
        out_ref[i] = rows_ref[:, 384 * i : 384 * (i + 1)]


def query_kernel(ids, first_ref, one, three, two, gain_ref, mine_ref, other_ref, all_ref, *outs_total):
    outs, total = outs_total[:4], outs_total[4]
    core, ring = ids[0], ids[1]
    all_ref[ring_rows(ring, 0), :] = first_ref[...]
    for back, block in ((1, one), (3, three), (2, two)):
        first = normed(local_order(block[...].astype(F32), core))[1] * gain_ref[0:1, :]
        all_ref[ring_rows(ring, back), :] = first.astype(BF)
    rows = all_ref[...]
    total[...] = (dot(rows[:, :768], mine_ref[:, :384]) + dot(rows[:, 768:], other_ref[:, :384])).astype(BF)
    for out, back in zip(outs, BACKS):
        out[...] = total[ring_rows(ring, back), :]


def middle_kernel(attended_ref, mine_ref, other_ref, token_ref, gain_ref, middle_ref, second_ref):
    attended = attended_ref[...]
    branch = jnp.concatenate([dot(attended, mine_ref[...], NT), dot(attended, other_ref[...], NT)], axis=1)
    middle = token_ref[...].astype(F32) + branch
    middle_ref[...] = middle
    second_ref[...] = (normed(middle)[1] * gain_ref[1:2, :]).astype(BF)


def middle_back_kernel(
    parts, middle_ref, cot_ref, gain_ref, mine_ref, other_ref, grad_ref, low_ref, high_ref, terms_ref, attended_ref
):
    grad_second = sum(parts[i].astype(F32) for i in range(4))
    _, n2, rs2 = normed(middle_ref[...])
    grad_middle = cot_ref[...].astype(F32) + norm_back(grad_second, gain_ref[1:2, :], n2, rs2)
    grad_ref[...] = grad_middle
    low = grad_middle.astype(BF)
    low_ref[...] = low[:, :768]
    high_ref[...] = low[:, 768:]
    terms_ref[...] = (grad_second * n2).astype(BF)
    attended_ref[...] = (dot(low[:, :768], mine_ref[...]) + dot(low[:, 768:], other_ref[...])).astype(BF)


def first_back_kernel(
    ring_ref, dqueries, home_6, home_5, home_4, home_3, home_2, home_1, home_0, rest_a, rest_b, first_ref,
    second_terms, mlp_out, own_ref, one, three, two, tail_a, tail_b, sums, partial,
):
    ring = ring_ref[0]
    dquery = jnp.concatenate([dqueries[i] for i in range(4)], axis=0)
    sums[...] = sum(home[...].astype(F32) for home in (home_5, home_4, home_3, home_2, home_1, home_0))
    sums[128:, :] += home_6[...].astype(F32)
    dkeyval = sums[...].astype(BF)
    column = lax.broadcasted_iota(jnp.int32, (RING + ROW, 128), 1)
    row = lax.broadcasted_iota(jnp.int32, (RING + ROW, 128), 0)
    picks = jnp.where(column == (row >= RING).astype(jnp.int32), 1.0, 0.0).astype(BF)
    own_rows = ring_rows(ring, 0)
    for cols, rest, tail in ((slice(0, 768), rest_a, tail_a), (slice(768, 1536), rest_b, tail_b)):
        partial[...] = dot(dquery, rest[:, :384], NT)
        partial[own_rows, :] += dot(dkeyval, rest[:, 384:640], NT)
        own_ref[:, cols] = partial[own_rows, :]
        for back, ref in ((1, one), (3, three), (2, two)):
            ref[0, :, cols] = partial[ring_rows(ring, back), :].astype(BF)
            ref[1, :, cols] = mlp_out[ring_rows(ring, back), cols]
        first = first_ref[:, cols]
        terms = jnp.concatenate([(partial[...] * first.astype(F32)).astype(BF), second_terms[:, cols]], axis=0)
        tail[:, :384] = dot(first, dquery, TN).astype(BF)
        tail[:, 384:640] = dot(first_ref[own_rows, cols], dkeyval, TN).astype(BF)
        tail[:, 640:] = dot(terms, picks, TN).astype(BF)


def finish_kernel(
    ids, own_ref, one, three, two, token_ref, gain_ref, grad_ref, middle_ref, mlp_ref, input_ref, block_ref
):
    core = ids[0]
    grad_first = own_ref[...] + sum(part[0].astype(F32) for part in (one, three, two))
    _, n1, rs1 = normed(token_ref[...])
    total = grad_ref[...] + norm_back(grad_first, gain_ref[0:1, :], n1, rs1)
    input_ref[...] = true_order(total, core).astype(BF)
    total = middle_ref[...] + mlp_ref[...].astype(F32)
    total = total + sum(part[1].astype(F32) for part in (one, three, two))
    block_ref[...] = true_order(total, core).astype(BF)


def tail_kernel(core_ref, parts, out_ref):
    total = sum(parts[i].astype(F32) for i in range(16))
    out_ref[...] = jnp.zeros_like(out_ref)
    for xh in range(2):
        keep = jnp.where(core_ref[0] == xh, 1.0, 0.0)
        for i in range(4):
            out_ref[4 * xh + i, :12, :768] = (total[12 * i : 12 * (i + 1)] * keep).astype(BF)


def deal_kernel(ids, owned_ref, give_a, give_b, cross_a, cross_b):
    head, xh = ids[0], ids[1]
    start = 3 * FF

    def rows(cols, flip):
        block = owned_ref[:, cols].astype(F32)
        return jnp.where((xh == 0) != flip, block[:24], block[24:]).astype(BF)

    def part(chip):
        return pl.ds(pl.multiple_of(start + 384 * chip, 384), 384)

    for flip, give, cross in ((False, give_a, cross_a), (True, give_b, cross_b)):
        give[:, :start] = rows(slice(0, start), flip)
        for i in range(2):
            give[:, start + 384 * i : start + 384 * (i + 1)] = rows(part(2 * i + head), flip)
            cross[:, 384 * i : 384 * (i + 1)] = rows(part(2 * i + 1 - head), flip)


def final_kernel(ids, tail, got_a, got_b, cross_a, cross_b, gain_own, query_ref, key_ref, value_ref, gain_ref, out_ref, gate_ref,
                 up_ref, down_ref):
    core, xh = ids[0], ids[1]
    total = jnp.zeros((12, 384), F32)
    for xh_from in range(2):
        for head in range(2):
            block = tail[4 * xh_from + 2 * xh + head].astype(F32)[:12]
            quarter = 2 * head + xh_from
            query_ref[:, 384 * quarter : 384 * (quarter + 1)] = block[:, :384]
            total = total + block[:, 384:768]
    key_ref[...] = total[:, :HD]
    value_ref[...] = total[:, HD : 2 * HD]
    sums = jnp.concatenate([total[:, 2 * HD :], jnp.zeros((4, HD), F32)], axis=0).T
    gain_ref[0:1, :] = sums[0:1, :12] / gain_own[...]
    gain_ref[1:2, :] = sums[1:2, :12]
    first, second = got_a[...].astype(F32), got_b[...].astype(F32)
    halves = (jnp.where(core == 0, first, second), jnp.where(core == 0, second, first))
    for i, half in enumerate(halves):
        for f in range(FF_TILES):
            place = slice(FF * i + FF_TILE * f, FF * i + FF_TILE * (f + 1))
            gate_ref[:, place] = half[:, 2 * FF_TILE * f : 2 * FF_TILE * f + FF_TILE]
            up_ref[:, place] = half[:, 2 * FF_TILE * f + FF_TILE : 2 * FF_TILE * (f + 1)]
        down_ref[:, FF * i : FF * (i + 1)] = half[:, 2 * FF : 3 * FF]
    out_ref[...] = (
        halves[0][:, 3 * FF :] + halves[1][:, 3 * FF :] + cross_a[...].astype(F32) + cross_b[...].astype(F32)
    )


def turn_xc(block, flip, cross, back=False):
    route = []
    for xh in range(2):
        for core in range(2):
            for head in range(2):
                target = (core ^ flip) * 4 + xh * 2 + (head ^ cross)
                source = xh * 4 + core * 2 + head
                route.append((target, source) if back else (source, target))
    return lax.ppermute(block, ("xh", "core", "head"), route)


def shift_all(block, distance):
    count = 128
    route = [(i, i + distance) for i in range(count) if 0 <= i + distance < count]
    return lax.ppermute(block, AXES, route)


def shift_groups(block, distance):
    return lax.ppermute(block, ("z", "xh", "y"), [(i, i + distance) for i in range(32 - distance)])


def shift_x(block, distance):
    return lax.ppermute(block, CHIPS_X, [(i, (i + distance) % 4) for i in range(4)])


def swap(block, axis):
    return lax.ppermute(block, axis, [(0, 1), (1, 0)])


def shards(tokens, cotangent, w_query, w_key, w_value, w_out, w_gate, w_up, w_down, gain_attn, gain_mlp):
    core = lax.axis_index("core")
    xh = lax.axis_index("xh")
    head = lax.axis_index("head")
    ring = 2 * xh + head
    place = jnp.stack([lax.axis_index(AXES), 2 * core + head]).astype(jnp.int32)
    ring_scalar, core_scalar, head_scalar = (i.astype(jnp.int32).reshape(1) for i in (ring, core, head))
    eight = ("xh", "core", "head")

    def ordered(index, first, second, axis):
        return jnp.concatenate(
            [jnp.where(index == 0, first, second), jnp.where(index == 0, second, first)], axis=axis
        )

    def spread(piece):
        sent = jnp.broadcast_to(piece[None], (16,) + piece.shape)
        return lax.all_to_all(sent, PLANE, 0, 0, tiled=True).reshape(768, -1)

    def gather(piece):
        return lax.all_gather(piece, PLANE, axis=0, tiled=True)

    gains = jnp.pad(jnp.stack([gain_attn, gain_mlp], axis=1), ((0, 0), (0, 126)))
    query_cut = w_query.reshape(12, 2, 2, 384).transpose(2, 1, 0, 3)
    common = jnp.broadcast_to(jnp.concatenate([w_key, w_value, gains], axis=1), (2, 2, 12, 384))
    own_qkv = jnp.concatenate([query_cut, common], axis=3)
    own_qkv = jnp.broadcast_to(own_qkv[:, None], (2, 2, 2, 12, 768)).reshape(8, 12, 768)
    got = lax.all_to_all(own_qkv, eight, 0, 0, tiled=True)
    qkv_piece = lax.dynamic_slice_in_dim(got, core * 4, 4, 0).reshape(48, 768)
    token_1, token_3, token_2 = (shift_x(tokens, k) for k in (1, 3, 2))
    qkv_mine = spread(qkv_piece)
    cot_own, cot_sent = call(
        order_kernel,
        "order",
        [((ROW, 1536), BF), ((4, ROW, 1536), BF)],
        [core_scalar, cotangent],
        scalars=1,
    )
    (cot_sent,) = after([cot_sent], qkv_mine)
    cots = lax.all_to_all(cot_sent, CHIPS_X, 0, 0, tiled=True).reshape(RING, 1536)
    (qkv_mine,) = after([qkv_mine], token_1, token_3, token_2)

    pair_cut = jnp.stack([w_gate, w_up], axis=1).reshape(24, 2, 2, FF_TILES, FF_TILE)
    pair_cut = pair_cut.transpose(2, 0, 3, 1, 4).reshape(2, 24, 2 * FF)
    down_cut = w_down.T.reshape(24, 2, FF).transpose(1, 0, 2)
    own_mlp = jnp.concatenate([pair_cut, down_cut], axis=2)
    sent_a = jnp.where(core == 0, own_mlp[0], own_mlp[1])
    sent_b = jnp.where(core == 0, own_mlp[1], own_mlp[0])
    out_low = w_out.T
    got_a = turn_xc(jnp.concatenate([out_low, sent_a], axis=1), False, False)
    got_b = turn_xc(jnp.concatenate([out_low, sent_b], axis=1), True, False)
    cross_a, cross_b = turn_xc(out_low, False, True), turn_xc(out_low, True, True)
    out_same = ordered(xh, got_a[:, :768], got_b[:, :768], 0).reshape(48, 2, 1, 384)
    out_cross = ordered(xh, cross_a, cross_b, 0).reshape(48, 2, 1, 384)
    out_piece = ordered(head, out_same, out_cross, 2).reshape(48, 1536)
    mlp_piece = ordered(xh, got_a[:, 768:], got_b[:, 768:], 0)
    (rest_piece,) = after([jnp.concatenate([out_piece, mlp_piece], axis=1)], qkv_piece)
    rest_mine = gather(rest_piece)

    qkv_other = swap(qkv_mine, "core")
    gain_rows, token_own, first_own, keyval_pair = call(
        keyval_kernel,
        "keyval",
        [((8, 1536), F32), ((ROW, 1536), BF), ((ROW, 1536), BF), ((2 * ROW, 256), BF)],
        [jnp.concatenate([head_scalar, core_scalar]), tokens, token_1, token_3, qkv_mine, qkv_other],
        scalars=1,
    )
    here, last = call(
        table_kernel,
        "table",
        [((768, 256), BF), ((256, 256), BF)],
        [core_scalar, keyval_pair, swap(keyval_pair, "core")],
        scalars=1,
    )
    near, far = shift_groups(here, 1), shift_groups(last, 2)
    first_all, query_0, ring_1, ring_3, ring_2 = call(
        query_kernel,
        "query",
        [((RING, 1536), BF)] + [((ROW, 384), BF)] * 4,
        [jnp.concatenate([core_scalar, ring_scalar]), first_own, token_1, token_3, token_2, gain_rows, qkv_mine, qkv_other],
        scratch=[pltpu.VMEM((RING, 384), BF)],
        scalars=1,
        needs=[here],
    )
    query_1, query_3, query_2 = shift_x(ring_1, -1), shift_x(ring_3, -3), shift_x(ring_2, -2)
    (queries,) = call(
        turn_kernel, "turn", [((ROW, 1536), BF)], [ring_scalar, query_0, query_1, query_2, query_3], scalars=1
    )
    (rest_mine,) = after([rest_mine], queries, near, far, cots)
    out_mine = rest_mine[:, :1536]
    attended, probs, keyval = attend(place, queries, far, near, here, [out_mine])

    out_other = swap(out_mine, "core")
    middle, second_own = call(
        middle_kernel,
        "middle",
        [((ROW, 1536), F32), ((ROW, 1536), BF)],
        [attended, out_mine, out_other, token_own, gain_rows],
    )
    blocks = [second_own] + [shift_x(second_own, k) for k in (1, 3, 2)]
    (rest_mine,) = after([rest_mine], attended, out_other)
    rest_other = swap(rest_mine, "core")
    dhidden = down_back(cots, rest_mine, rest_other)

    hidden, dpair, seconds, seconds_b, second_part = mlp(ring_scalar, blocks, dhidden, rest_mine, rest_other)
    second_home = lax.all_to_all(second_part.reshape(4, ROW, 1536), CHIPS_X, 0, 0, tiled=True)

    def planes(total):
        got = lax.all_to_all(total.reshape(16, 48, -1), PLANE, 0, 0, tiled=True)
        return jnp.sum(got.astype(F32), axis=0).astype(BF)

    mlp_out = down_project(hidden, rest_mine, rest_other)
    (unit_total,) = unit_grad(
        [seconds, swap(seconds_b, "core"), cots, swap(cots[:, 768:], "core")]
        + [dpair, swap(dpair, "core"), hidden, swap(hidden, "core")],
        [mlp_out],
    )
    grad_middle, branch_a, branch_b, second_terms, grad_attended = call(
        middle_back_kernel,
        "middle_back",
        [((ROW, 1536), F32), ((ROW, 768), BF), ((ROW, 768), BF), ((ROW, 1536), BF), ((ROW, 1536), BF)],
        [second_home, middle, cot_own, gain_rows, out_mine, out_other],
        needs=[unit_total],
    )
    dqueries, *homes = attend_back(queries, keyval, attended, grad_attended, probs, [])

    (dquery_cut,) = call(cut_kernel, "cut", [((4, ROW, 384), BF)], [dqueries])
    dquery_ring = lax.all_to_all(dquery_cut, CHIPS_X, 0, 0, tiled=True)
    homes = [shift_all(home, -k) for home, k in zip(homes, (6, 5, 4, 3, 2, 1))] + [homes[6]]
    total = out_grad(branch_a, swap(branch_b, "core"), attended, swap(attended, "core"), unit_total)
    owned = lax.psum_scatter(total, PLANE, scatter_dimension=0, tiled=True)
    own_first, first_1, first_3, first_2, tail_mine, tail_other = call(
        first_back_kernel,
        "first_back",
        [((ROW, 1536), F32)] + [((2, ROW, 1536), BF)] * 3 + [((768, 768), BF)] * 2,
        [
            ring_scalar, dquery_ring, *homes, qkv_mine, qkv_other, first_all, second_terms,
            mlp_out,
        ],
        scratch=[pltpu.VMEM((ROW, 256), F32), pltpu.VMEM((RING, 768), F32)],
        scalars=1,
    )
    tail_total = merge((tail_mine, swap(tail_other, "core")))
    tail_parts = lax.all_to_all(tail_total.reshape(16, 48, 768), PLANE, 0, 0, tiled=True)
    first_1, first_3, first_2 = shift_x(first_1, -1), shift_x(first_3, -3), shift_x(first_2, -2)
    rows_of = pl.BlockSpec((64, 1536), lambda i, ids: (i, 0))
    parts_of = pl.BlockSpec((2, 64, 1536), lambda i, ids: (0, i, 0))
    input_grad, block_out = call(
        finish_kernel,
        "finish",
        [((ROW, 1536), BF)] * 2,
        [jnp.concatenate([core_scalar, ring_scalar]), own_first, first_1, first_3, first_2, token_own, gain_rows]
        + [grad_middle, middle, mlp_out],
        micros=20.0,
        scalars=1,
        grid=(3,),
        in_specs=[rows_of] + [parts_of] * 3 + [rows_of, pl.BlockSpec((8, 1536), lambda i, ids: (0, 0)), rows_of, rows_of]
        + [pl.BlockSpec((64, 1536), lambda i, ids: (3 * ids[1] + i, 0))],
        out_specs=[rows_of] * 2,
    )
    (tail_sent,) = call(tail_kernel, "tail", [((8, 16, 1024), BF)], [core_scalar, tail_parts], scalars=1)
    tail_got = lax.all_to_all(tail_sent, eight, 0, 0, tiled=True)
    give_a, give_b, cross_a, cross_b = call(
        deal_kernel,
        "deal",
        [((24, 3 * FF + 768), BF)] * 2 + [((24, 768), BF)] * 2,
        [jnp.concatenate([head_scalar, xh.astype(jnp.int32).reshape(1)]), owned],
        needs=[tail_sent],
        scalars=1,
    )
    got_a, got_b = turn_xc(give_a, False, False, True), turn_xc(give_b, True, False, True)
    cross_a, cross_b = turn_xc(cross_a, False, True, True), turn_xc(cross_b, True, True, True)
    query_grad, key_grad, value_grad, gain_grads, out_grad_own, gate_grad, up_grad, down_grad = call(
        final_kernel,
        "final",
        [((12, 1536), F32)] + [((12, 128), F32)] * 2 + [((2, 12), F32), ((24, 768), F32)] + [((24, 2 * FF), F32)] * 3,
        [jnp.concatenate([core_scalar, xh.astype(jnp.int32).reshape(1)]), tail_got, got_a, got_b, cross_a, cross_b]
        + [gain_attn.astype(F32).reshape(1, 12)],
        needs=[input_grad, block_out],
        scalars=1,
    )
    return (
        block_out,
        input_grad,
        query_grad,
        key_grad,
        value_grad,
        out_grad_own.T,
        gate_grad,
        up_grad,
        down_grad.T,
        gain_grads[0],
        gain_grads[1],
    )


def solution(mesh):
    grid = Mesh(mesh.devices.reshape(SIZES), AXES)
    seq = ("z", "xh", "y", "core")
    rows, both, cols = P(AXES, None), P(seq, "head"), P("head", seq)
    in_specs = (rows, rows, rows, rows, rows, cols, both, both, cols, P(AXES), P(AXES))
    out_specs = (rows, rows, rows, rows, rows, cols, both, both, cols, P(AXES), P(AXES))
    return jax.shard_map(shards, mesh=grid, in_specs=in_specs, out_specs=out_specs, check_vma=False)
```
